32 devices in a mesh: traj: 4 (over y, x), strip: 8 (over z, core).
Axes of the slice: x: 2, y: 2, z: 4, core: 2. Of those that a mesh axis runs over, the one named last changes fastest.
Arguments:
- velocity: float32 [8, 2, 128, 128], P('traj', None, 'strip'), may hold values from -6 to 6
- lengths: int32 [8], P('traj'), may hold values from 1 to 2
- cotangent: float32 [8, 2, 128, 128], P('traj', None, 'strip'), may hold values from -6 to 6
- first_kernel: bfloat16 [9, 64, 2], replicated, may hold values from -1.5 to 1.5
- first_bias: float32 [64], replicated, may hold values from -3 to 3
- middle_kernels: bfloat16 [5, 9, 64, 64], replicated, may hold values from -0.25 to 0.25
- middle_biases: float32 [5, 64], replicated, may hold values from -3 to 3
- last_kernel: bfloat16 [9, 64, 64], replicated, may hold values from -0.0625 to 0.0625
- last_bias: float32 [64], replicated, may hold values from -1.2 to 1.2
Outputs:
- final_velocity: float32 [8, 2, 128, 128], P('traj', None, 'strip')
- velocity_grad: float32 [8, 2, 128, 128], P('traj', None, 'strip')
- grad_first_kernel: float32 [9, 64, 2], replicated
- grad_first_bias: float32 [64], replicated
- grad_middle_kernels: float32 [5, 9, 64, 64], replicated
- grad_middle_biases: float32 [5, 64], replicated
- grad_last_kernel: float32 [9, 64, 64], replicated
- grad_last_bias: float32 [64], replicated
The draws below stay inside these ranges and needn't reach their ends.
All inputs are finite; a program needn't handle non-finite values.
Results may differ from the reference program's by a relative error of at most 0.025.
Values may be sent and summed in bfloat16 or wider, within the bound.
No kernel may reach another device: no remote copies, remote signals or barrier semaphores. Data moves between devices by JAX's collectives and lax.ppermute only.
A program may use at most 192 MiB of HBM per device.

```python
import math
import jax
import jax.numpy as jnp
from jax import lax

CH = 64
MIDDLE = 5
STEN = 64
GRID = 128
STEPS = 2
TRAJ = 8


def with_ends(entries, own_key, least, top_value):
    extent = entries.shape
    index_at = [jax.random.randint(jax.random.fold_in(own_key, axis), (), 0, extent[axis]) for axis in range(len(extent))]
    entries = entries.at[tuple(index_at)].set(least)
    longest = extent.index(max(extent))
    index_at[longest] = (index_at[longest] + 1) % extent[longest]
    return entries.at[tuple(index_at)].set(top_value)


def steps_of(key, shape, shards, low, high):
    loudness = 1.0
    for position, parts in shards:
        draws = jax.random.uniform(jax.random.fold_in(jax.random.fold_in(key, 6), position), (parts,), jnp.float32, low / len(shards), high / len(shards))
        loudness = loudness * jnp.repeat(jnp.exp(draws), shape[position] // parts).reshape((-1,) + (1,) * (len(shape) - 1 - position))
    return loudness


def centred(key, extent, width, limit, pieces=(), held_as=jnp.bfloat16):
    factor_of = steps_of(key, extent, pieces, -0.22, 0.18) if pieces else 1.0
    values = jax.random.normal(key, extent, jnp.float32) * width * factor_of
    return jnp.minimum(jnp.maximum(values, -limit), limit).astype(held_as)


def setup_inputs(seed: int = 0) -> dict:
    seeds = jax.random.split(jax.random.key(seed), 10)
    velocity = centred(seeds[0], (TRAJ, 2, GRID, GRID), 1.0, 6.0, ((0, 4), (2, 8)), jnp.float32)
    lengths = with_ends(jax.random.randint(seeds[1], (TRAJ,), 1, STEPS + 1), jax.random.fold_in(seeds[1], 1), 1, STEPS).astype(jnp.int32)
    cotangent = centred(seeds[2], (TRAJ, 2, GRID, GRID), 1.0, 6.0, ((0, 4), (2, 8)), jnp.float32)
    first_kernel = centred(seeds[3], (9, CH, 2), 18 ** -0.5, 1.5)
    first_bias = centred(seeds[4], (CH,), 0.5, 3.0, (), jnp.float32)
    middle_kernels = centred(seeds[5], (MIDDLE, 9, CH, CH), (9 * CH) ** -0.5, 0.25)
    middle_biases = centred(seeds[6], (MIDDLE, CH), 0.5, 3.0, (), jnp.float32)
    last_kernel = centred(seeds[7], (9, STEN, CH), (144 * CH) ** -0.5, 0.0625)
    last_bias = centred(seeds[8], (STEN,), 0.2, 1.2, (), jnp.float32)
    return {"velocity": velocity, "lengths": lengths, "cotangent": cotangent, "first_kernel": first_kernel, "first_bias": first_bias, "middle_kernels": middle_kernels, "middle_biases": middle_biases, "last_kernel": last_kernel, "last_bias": last_bias}


@jax.custom_vjp
def low(v):
    return lax.optimization_barrier(v.astype(jnp.bfloat16)).astype(jnp.float32)

@jax.custom_vjp
def low_back(v):
    return v

def low_keep(v):
    return (low(v), None)

def low_pass(kept, grad):
    return (grad,)

def back_keep(v):
    return (v, None)

def back_low(kept, grad):
    return (low(grad),)
low.defvjp(low_keep, low_pass)
low_back.defvjp(back_keep, back_low)
dt_step = 0.25
highest = lax.Precision.HIGHEST

def hartley_table(length):
    wave_numbers = jnp.arange(length, dtype=jnp.int32)
    product = wave_numbers[:, None] * wave_numbers[None, :] % length
    angles = product.astype(jnp.float32) * (2.0 * math.pi / length)
    return (jnp.cos(angles) + jnp.sin(angles)) * (1.0 / math.sqrt(length))

def spectral_weights(row_waves, col_waves, length):
    row_eigen = 2.0 - 2.0 * jnp.cos(row_waves.astype(jnp.float32) * (2.0 * math.pi / length))
    col_eigen = 2.0 - 2.0 * jnp.cos(col_waves.astype(jnp.float32) * (2.0 * math.pi / length))
    eigen_sum = row_eigen[:, None] + col_eigen[None, :]
    anchor = (row_waves[:, None] == 0) & (col_waves[None, :] == 0)
    return jnp.where(anchor, 0.0, 1.0 / jnp.where(anchor, 1.0, eigen_sum))

def stencil_tables():
    point_ids = jnp.arange(16, dtype=jnp.int32)
    along_x = (point_ids % 4).astype(jnp.float32) - 1.5
    along_y = (point_ids // 4).astype(jnp.float32) - 1.5
    target_x = jnp.array([0.0, -0.5, 0.0, -0.5], jnp.float32)
    target_y = jnp.array([-0.5, 0.0, -0.5, 0.0], jnp.float32)
    offsets = 1.0 / 16.0 + target_x[:, None] * along_x[None, :] / 20.0 + target_y[:, None] * along_y[None, :] / 20.0
    return (along_x, along_y, offsets)

def project_stencil(raw_weights):
    along_x, along_y, offsets = stencil_tables()
    shape_x = along_x[None, None, :, None, None]
    shape_y = along_y[None, None, :, None, None]
    mean_part = lax.optimization_barrier(jnp.mean(raw_weights, axis=2, keepdims=True))
    moment_x = lax.optimization_barrier(jnp.sum(raw_weights * shape_x, axis=2, keepdims=True)) / 20.0
    moment_y = lax.optimization_barrier(jnp.sum(raw_weights * shape_y, axis=2, keepdims=True)) / 20.0
    return raw_weights - mean_part - moment_x * shape_x - moment_y * shape_y + offsets[None, :, :, None, None]

def convolve(inputs, kernels, bias_vec):
    running = None
    for row_step in range(3):
        for col_step in range(3):
            shifted = jnp.roll(inputs, (1 - row_step, 1 - col_step), (2, 3))
            product_term = jnp.einsum('oi,birc->borc', kernels[row_step * 3 + col_step], shifted, precision=highest)
            running = product_term if running is None else running + product_term
    return running + bias_vec[None, :, None, None]

def network(velocity, first_kernel, first_bias, middle_kernels, middle_biases, last_kernel, last_bias):
    hidden = low(velocity)
    layers = [(first_kernel, first_bias)] + [(middle_kernels[layer_idx], middle_biases[layer_idx]) for layer_idx in range(middle_kernels.shape[0])]
    for kernels, bias_vec in layers:
        hidden = low(jax.nn.gelu(low_back(convolve(hidden, kernels, bias_vec))))
    return low_back(convolve(hidden, last_kernel, last_bias))

def poisson(source):
    length = source.shape[-1]
    hartley = hartley_table(length)
    wave_numbers = jnp.arange(length, dtype=jnp.int32)
    weighting = spectral_weights(wave_numbers, wave_numbers, length)
    spectrum = jnp.einsum('brc,cd->brd', source, hartley, precision=highest)
    spectrum = jnp.einsum('jr,brd->bjd', hartley, spectrum, precision=highest) * weighting
    spectrum = jnp.einsum('jr,brd->bjd', hartley, spectrum, precision=highest)
    return -jnp.einsum('brc,cd->brd', spectrum, hartley, precision=highest)

def advance(velocity, step_mask, params):
    raw = network(velocity, *params)
    count_traj = velocity.shape[0]
    length = velocity.shape[2]
    stencil = project_stencil(raw.reshape(count_traj, 4, 16, length, length))
    field_u = velocity[:, 0]
    field_v = velocity[:, 1]
    sources = (field_u, field_u, field_v, field_v)
    interp = []
    for interp_idx in range(4):
        summed = jnp.zeros_like(field_u)
        for point_idx in range(16):
            shifted = jnp.roll(sources[interp_idx], (1 - point_idx // 4, 1 - point_idx % 4), (1, 2))
            summed = summed + stencil[:, interp_idx, point_idx] * shifted
        interp.append(summed)
    flux_xu = 0.5 * (field_u + jnp.roll(field_u, -1, 2)) * interp[0]
    flux_yu = 0.5 * (field_v + jnp.roll(field_v, -1, 2)) * interp[1]
    flux_xv = 0.5 * (field_u + jnp.roll(field_u, -1, 1)) * interp[2]
    flux_yv = 0.5 * (field_v + jnp.roll(field_v, -1, 1)) * interp[3]
    star_u = field_u - dt_step * (flux_xu - jnp.roll(flux_xu, 1, 2) + (flux_yu - jnp.roll(flux_yu, 1, 1)))
    star_v = field_v - dt_step * (flux_xv - jnp.roll(flux_xv, 1, 2) + (flux_yv - jnp.roll(flux_yv, 1, 1)))
    divergence = star_u - jnp.roll(star_u, 1, 2) + (star_v - jnp.roll(star_v, 1, 1))
    pressure = poisson(divergence)
    new_u = star_u - (jnp.roll(pressure, -1, 2) - pressure)
    new_v = star_v - (jnp.roll(pressure, -1, 1) - pressure)
    corrected = jnp.stack([new_u, new_v], axis=1)
    return velocity + step_mask * (corrected - velocity)

def rollout(velocity, step_masks, params):
    current = velocity
    for step_idx in range(STEPS):
        current = advance(current, step_masks[step_idx], params)
    return current

def reference(velocity, lengths, cotangent, first_kernel, first_bias, middle_kernels, middle_biases, last_kernel, last_bias):
    params = tuple((argument.astype(jnp.float32) for argument in (first_kernel, first_bias, middle_kernels, middle_biases, last_kernel, last_bias)))
    step_ids = jnp.arange(STEPS, dtype=jnp.int32)
    step_masks = (lengths[:, None] > step_ids[None, :]).astype(jnp.float32)

    def per_traj(running, sliced):
        vel_one, mask_one, cot_one = sliced

        def forward(vel_in, params_in):
            return rollout(vel_in[None], mask_one, params_in)[0]
        result, pullback = jax.vjp(forward, vel_one, params)
        grad_vel, grad_params = pullback(cot_one)
        running = tuple((earlier + addition for earlier, addition in zip(running, grad_params)))
        return (running, (result, grad_vel))
    initial = tuple((jnp.zeros_like(argument) for argument in params))
    totals, outputs = lax.scan(per_traj, initial, (velocity, step_masks, cotangent))
    return (outputs[0], outputs[1], totals[0], totals[1], totals[2], totals[3], totals[4], totals[5])
```

```python
import functools
import math

import jax
import jax.numpy as jnp
import numpy as np
from jax import lax
from jax.experimental import pallas as pl
from jax.experimental.pallas import tpu as pltpu
from jax.sharding import PartitionSpec as P

STEPS = 2
DT = 0.25
MARGIN = 16
MID = 8
RAW = 2
CH = 64
N = 128
bf16 = jnp.bfloat16
f32 = jnp.float32
NT = (((1,), (1,)), ((), ()))
VMEM_BYTES = 56 * 2**20


def reach(layer):
    return 12 - layer


def lanes(x, s):
    return x if s == 0 else pltpu.roll(x, (-s) % x.shape[1], 1)


def rows(x, s):
    return x if s == 0 else pltpu.roll(x, (-s) % x.shape[0], 0)


def poisson_tables(length):
    k = np.arange(length)
    angle = 2.0 * math.pi * ((k[:, None] * k[None, :]) % length) / length
    table = (np.cos(angle) + np.sin(angle)) / math.sqrt(length)
    high = table.astype(jnp.bfloat16)
    low = (table - high.astype(np.float64)).astype(jnp.bfloat16)
    eigen = 2.0 - 2.0 * np.cos(2.0 * math.pi * k / length)
    total = eigen[:, None] + eigen[None, :]
    total[0, 0] = 1.0
    weight = 1.0 / total
    weight[0, 0] = 0.0
    right = np.concatenate([high, high, low], axis=0)
    left = np.concatenate([high, low, high], axis=1)
    return right, left, weight.astype(np.float32)


def split(x):
    high = x.astype(bf16)
    return high, (x - high.astype(f32)).astype(bf16)


def times_right(x, right):
    high, low = split(x)
    return jnp.dot(jnp.concatenate([high, low, high], axis=1), right[...], preferred_element_type=f32)


def times_left(x, left):
    high, low = split(x)
    return jnp.dot(left[...], jnp.concatenate([high, high, low], axis=0), preferred_element_type=f32)


def project(fields, right, left, weight):
    count = len(fields)
    source = [u - lanes(u, -1) + (v - rows(v, -1)) for u, v in fields]
    x = times_right(jnp.concatenate(source, axis=0), right)
    x = jnp.concatenate([x[i * N : (i + 1) * N] for i in range(count)], axis=1)
    x = times_left(x, left) * jnp.concatenate([weight[...]] * count, axis=1)
    x = times_left(x, left)
    x = jnp.concatenate([x[:, i * N : (i + 1) * N] for i in range(count)], axis=0)
    x = times_right(x, right)
    out = []
    for i, (u, v) in enumerate(fields):
        p = -x[i * N : (i + 1) * N]
        out.append((u - (lanes(p, 1) - p), v - (rows(p, 1) - p)))
    return out


def local(x, count):
    return jnp.concatenate([x[N - MARGIN :], x[: count + MARGIN]], axis=0)


def fold(o):
    third = o.shape[0] // 3
    return lanes(o[:third], -1) + o[third : 2 * third] + lanes(o[2 * third :], 1)


def conv_rows(window, kernel, low, high, emit):
    starts = list(range(low, high, 2))
    for k in range(0, len(starts), 2):
        group = starts[k : k + 2]
        o = jnp.dot(
            kernel[...],
            jnp.concatenate([window(r) for r in group], axis=1),
            preferred_element_type=f32,
        )
        half = o.shape[0] // 2
        for i, r in enumerate(group):
            part = o[:, i * N : (i + 1) * N]
            emit(r, part[:half])
            emit(r + 1, part[half:])


def first_window(us, vs, r):
    a = r - 1 + MARGIN
    return jnp.concatenate(
        [us[1, a : a + 4, :], vs[1, a : a + 4, :], jnp.zeros((8, N), f32)], axis=0
    ).astype(bf16)


def row_window(ref, low):
    return lambda r: ref[(r - 1 - low) * CH : (r + 3 - low) * CH, :]


def gelu_parts(z):
    c = math.sqrt(2.0 / math.pi)
    zz = z * z
    t = jnp.tanh(z * (c + (c * 0.044715) * zz))
    h = 0.5 + 0.5 * t
    return z * h, h + (0.5 * z) * (1.0 - t * t) * (c + (3.0 * c * 0.044715) * zz)


def spread_columns(u, v, us, vs):
    for j in range(4):
        us[j] = lanes(u, j - 1)
        vs[j] = lanes(v, j - 1)


def network_forward(count, us, vs, w_first, w_hidden, bias, feats, slopes, raw):
    layers = len(feats)
    for m in range(1, layers + 1):
        low = -reach(m)

        def emit(r, o, m=m, low=low):
            value, slope = gelu_parts(fold(o) + bias[m - 1])
            feats[m - 1][(r - low) * CH : (r - low + 1) * CH, :] = value.astype(bf16)
            if -m <= r < count + m:
                slopes[m - 1][(r + m) * CH : (r + m + 1) * CH, :] = slope.astype(bf16)

        if m == 1:
            conv_rows(functools.partial(first_window, us, vs), w_first, low, count - low, emit)
        else:
            conv_rows(
                row_window(feats[m - 2], -reach(m - 1)), w_hidden.at[m - 2], low, count - low, emit
            )

    def emit_raw(r, o):
        raw[(r + MID) * CH : (r + MID + 1) * CH, :] = fold(o) + bias[layers]

    conv_rows(
        row_window(feats[-1], -reach(layers)), w_hidden.at[layers - 1], -RAW, count + RAW, emit_raw
    )


PX = [p % 4 - 1.5 for p in range(16)]
PY = [p // 4 - 1.5 for p in range(16)]
TARGETS = ((0.0, -0.5), (-0.5, 0.0), (0.0, -0.5), (-0.5, 0.0))


def moments(values):
    cols = [values[j] + values[4 + j] + values[8 + j] + values[12 + j] for j in range(4)]
    lines = [values[4 * i] + values[4 * i + 1] + values[4 * i + 2] + values[4 * i + 3] for i in range(4)]
    mean = (cols[0] + cols[1] + (cols[2] + cols[3])) * (1.0 / 16.0)
    mx = (1.5 * (cols[3] - cols[0]) + 0.5 * (cols[2] - cols[1])) * (1.0 / 20.0)
    my = (1.5 * (lines[3] - lines[0]) + 0.5 * (lines[2] - lines[1])) * (1.0 / 20.0)
    return mean, mx, my


def less_moments(values):
    mean, mx, my = moments(values)
    by_col = [mean + mx * (j - 1.5) for j in range(4)]
    by_line = [my * (i - 1.5) for i in range(4)]
    return [values[p] - by_col[p % 4] - by_line[p // 4] for p in range(16)]


def stencil(raw, k, mid):
    tx, ty = TARGETS[k]
    values = less_moments([raw[pl.ds(k * 16 + p, mid, stride=CH), :] for p in range(16)])
    return [values[p] + (1.0 / 16.0 + tx * PX[p] / 20.0 + ty * PY[p] / 20.0) for p in range(16)]


def patches(src, mid):
    a = MARGIN - MID
    return [src[p % 4, a + p // 4 - 1 : a + p // 4 - 1 + mid, :] for p in range(16)]


def carriers(u, v):
    return (
        0.5 * (u + lanes(u, 1)),
        0.5 * (v + lanes(v, 1)),
        0.5 * (u + rows(u, 1)),
        0.5 * (v + rows(v, 1)),
    )


def weighted(values, others):
    total = values[0] * others[0]
    for a, b in zip(values[1:], others[1:]):
        total = total + a * b
    return total


def provisional(count, u, v, us, vs, raw):
    mid = count + 2 * MID
    a = MARGIN - MID
    here = [x[a : a + mid] for x in carriers(u, v)]
    pu, pv = patches(us, mid), patches(vs, mid)
    flux = [here[k] * weighted(stencil(raw, k, mid), pu if k < 2 else pv) for k in range(4)]
    u, v = u[a : a + mid], v[a : a + mid]
    su = u - DT * (flux[0] - lanes(flux[0], -1) + (flux[1] - rows(flux[1], -1)))
    sv = v - DT * (flux[2] - lanes(flux[2], -1) + (flux[3] - rows(flux[3], -1)))
    return su[MID : MID + count], sv[MID : MID + count]


def flux_backward(count, gu, gv, u, v, us, vs, raw, graw32):
    mid = count + 2 * MID
    a = MARGIN - MID
    cut = lambda x: x[a : a + mid]
    here = [cut(x) for x in carriers(u, v)]
    gflux = [
        cut(x)
        for x in (
            (gu - lanes(gu, 1)) * (-DT),
            (gu - rows(gu, 1)) * (-DT),
            (gv - lanes(gv, 1)) * (-DT),
            (gv - rows(gv, 1)) * (-DT),
        )
    ]
    ginterp = [here[k] * gflux[k] for k in range(4)]
    out = []
    for which, (src, g) in enumerate(((us, gu), (vs, gv))):
        patch = patches(src, mid)
        clear = less_moments(patch)
        ks = (2 * which, 2 * which + 1)
        interp = {}
        spread = None
        for k in ks:
            for p in range(16):
                graw32[pl.ds(k * 16 + p, mid, stride=CH), :] = clear[p] * ginterp[k]
            weights = stencil(raw, k, mid)
            interp[k] = weighted(weights, patch)
            terms = [x * ginterp[k] for x in weights]
            spread = terms if spread is None else [x + y for x, y in zip(spread, terms)]
        total = None
        for i in range(4):
            line = None
            for j in range(4):
                term = lanes(spread[4 * i + j], 1 - j)
                line = term if line is None else line + term
            line = rows(line, 1 - i)
            total = line if total is None else total + line
        out.append((interp, total + cut(g)))
    half = [0.5 * gflux[k] * out[k // 2][0][k] for k in range(4)]
    grad_u = out[0][1] + (half[0] + lanes(half[0], -1)) + (half[2] + rows(half[2], -1))
    grad_v = out[1][1] + (half[1] + lanes(half[1], -1)) + (half[3] + rows(half[3], -1))
    return grad_u[MID : MID + count], grad_v[MID : MID + count]


def network_backward(count, us, vs, w_first, w_hidden, feats, feat_low, slopes, graw, grads, gvel, buffer, previous):
    layers = len(feats)
    sums = [None] * (layers + 1)

    def collect(m, g):
        g = g.astype(f32)
        sums[m - 1] = g if sums[m - 1] is None else sums[m - 1] + g

    for r in range(count):
        collect(layers + 1, graw[(r + MID) * CH : (r + MID + 1) * CH, :])
    for m in range(layers, 0, -1):
        source = row_window(graw, -MID) if m == layers else row_window(grads[m], -(m + 1))

        def emit(r, o, m=m):
            at = slice((r + m) * CH, (r + m + 1) * CH)
            g = (fold(o) * slopes[m - 1][at, :].astype(f32)).astype(bf16)
            grads[m - 1][at, :] = g
            if 0 <= r < count:
                collect(m, g)

        conv_rows(source, w_hidden.at[m - 1], -m, count + m, emit)

    window = row_window(grads[0], -1)
    starts = list(range(0, count, 2))
    for k in range(0, len(starts), 2):
        group = starts[k : k + 2]
        o = jnp.dot(
            w_first[...],
            jnp.concatenate([window(r) for r in group], axis=1),
            preferred_element_type=f32,
        )
        for i, r in enumerate(group):
            part = o[:, i * N : (i + 1) * N]
            both = lanes(part, -1)[0:4] + part[4:8] + lanes(part, 1)[8:12]
            gvel[0, r : r + 2, :] = both[0:2]
            gvel[1, r : r + 2, :] = both[2:4]

    starts = list(range(0, count, 2))
    products = []
    for m in range(1, layers + 2):
        ref, low = (graw, -MID) if m == layers + 1 else (grads[m - 1], -m)
        left = []
        for r in starts:
            g = [ref[(r + k - low) * CH : (r + k + 1 - low) * CH, :] for k in range(2)]
            left.append(jnp.concatenate([lanes(x, -e) for x in g for e in (-1, 0, 1)], axis=0))
        if m == 1:
            right = [first_window(us, vs, r) for r in starts]
        else:
            right = [row_window(feats[m - 2], feat_low(m - 1))(r) for r in starts]
        products.append(
            lax.dot_general(
                jnp.concatenate(left, axis=1),
                jnp.concatenate(right, axis=1),
                NT,
                preferred_element_type=f32,
            )
        )

    def put(block, value):
        at = slice(block * 3 * CH, (block + 1) * 3 * CH)
        if previous is not None:
            value = value + previous[at, :]
        buffer[at, :] = value.astype(buffer.dtype)

    def folded(x):
        return x[: 3 * CH, : 3 * CH] + x[3 * CH :, CH:]

    for pair in range(3):
        wide = jnp.concatenate([folded(products[1 + 2 * pair]), folded(products[2 + 2 * pair])], axis=1)
        for q in range(3):
            put(3 * pair + q, wide[:, q * N : (q + 1) * N])
    first = jnp.concatenate(
        [products[0][: 3 * CH], products[0][3 * CH :], jnp.zeros((3 * CH, N - 32), f32)], axis=1
    )
    lane = lax.broadcasted_iota(jnp.int32, (CH, N), 1)
    columns = jnp.zeros((CH, N), f32)
    for m in range(layers + 1):
        columns = jnp.where(lane == 32 + m, jnp.sum(sums[m], axis=1, keepdims=True), columns)
    columns = jnp.concatenate([columns, jnp.zeros((2 * CH, N), f32)], axis=0)
    put(9, first + columns)


def forward_kernel(count, vel, w_first, w_hidden, bias, star, *rest):
    layers = 6
    kept, slope_out, raw_out = rest[:layers], rest[layers : 2 * layers], rest[2 * layers]
    scratch = rest[2 * layers + 1 :]
    us, vs, raw, sems = scratch[:4]
    feats, slopes = scratch[4 : 4 + layers], scratch[4 + layers :]
    u, v = vel[0], vel[1]
    spread_columns(u, v, us, vs)
    network_forward(count, us, vs, w_first, w_hidden, bias, feats, slopes, raw)
    copies = []
    for m in range(1, layers + 1):
        copies.append((feats[m - 1].at[(reach(m) - 1) * CH : (reach(m) + count + 1) * CH, :], kept[m - 1]))
        copies.append((slopes[m - 1], slope_out[m - 1]))
    copies.append((raw, raw_out))
    copies = [pltpu.make_async_copy(a, b, sems.at[i]) for i, (a, b) in enumerate(copies)]
    for copy in copies:
        copy.start()
    su, sv = provisional(count, u, v, us, vs, raw)
    star[0] = su
    star[1] = sv
    for copy in copies:
        copy.wait()


def middle_kernel(count, blocks, masks, *refs):
    layers = 6
    gathered, refs = refs[:blocks], refs[blocks:]
    vel, cot, right, left, weight, w_first, w_hidden, bias, b_first, b_hidden = refs[:10]
    back, now, buffer = refs[10:13]
    us, vs, raw, graw32, graw, gvel = refs[13:19]
    feats, slopes, grads = refs[19:25], refs[25:31], refs[31:37]
    su, sv, cu, cv = [jnp.concatenate([g[i] for g in gathered], axis=0) for i in range(4)]
    m0, m1 = masks[0], masks[1]
    (nu, nv), (gu, gv) = project([(su, sv), (m1 * cu, m1 * cv)], right, left, weight)
    u = vel[0] + m0 * (local(nu, count) - vel[0])
    v = vel[1] + m0 * (local(nv, count) - vel[1])
    now[0] = u[MARGIN : MARGIN + count]
    now[1] = v[MARGIN : MARGIN + count]
    spread_columns(u, v, us, vs)
    network_forward(count, us, vs, w_first, w_hidden, bias, feats, slopes, raw)
    su, sv = provisional(count, u, v, us, vs, raw)
    back[0] = su
    back[1] = sv
    gu, gv = local(gu, count), local(gv, count)
    gu, gv = flux_backward(count, gu, gv, u, v, us, vs, raw, graw32)
    graw[...] = graw32[...].astype(bf16)
    network_backward(
        count, us, vs, b_first, b_hidden, feats, lambda m: -reach(m), slopes, graw, grads, gvel, buffer, None
    )
    back[2] = (1.0 - m1) * cu[:count] + gu + gvel[0]
    back[3] = (1.0 - m1) * cv[:count] + gv + gvel[1]


def backward_kernel(count, blocks, masks, *refs):
    layers = 6
    gathered, refs = refs[:blocks], refs[blocks:]
    vel, now, right, left, weight, b_first, b_hidden, previous = refs[:8]
    kept, slope_in, raw_in = refs[8:14], refs[14:20], refs[20]
    out, buffer = refs[21:23]
    us, vs, raw, graw32, graw, gvel, sems = refs[23:30]
    feats, slopes, grads = refs[30:36], refs[36:42], refs[42:48]
    copies = [(raw_in, raw)]
    for m in range(layers, 0, -1):
        copies += [(slope_in[m - 1], slopes[m - 1]), (kept[m - 1], feats[m - 1])]
    copies = [pltpu.make_async_copy(a, b, sems.at[i]) for i, (a, b) in enumerate(copies)]
    for copy in copies:
        copy.start()
    su, sv, cu, cv = [jnp.concatenate([g[i] for g in gathered], axis=0) for i in range(4)]
    m0, m1 = masks[0], masks[1]
    (nu, nv), (gu, gv) = project([(su, sv), (m0 * cu, m0 * cv)], right, left, weight)
    out[0] = now[0] + m1 * (nu[:count] - now[0])
    out[1] = now[1] + m1 * (nv[:count] - now[1])
    u, v = vel[0], vel[1]
    spread_columns(u, v, us, vs)
    for copy in copies:
        copy.wait()
    gu, gv = flux_backward(count, local(gu, count), local(gv, count), u, v, us, vs, raw, graw32)
    graw[...] = graw32[...].astype(bf16)
    network_backward(
        count, us, vs, b_first, b_hidden, feats, lambda m: -1, slopes, graw, grads, gvel, buffer, previous
    )
    out[2] = (1.0 - m0) * cu[:count] + gu + gvel[0]
    out[3] = (1.0 - m0) * cv[:count] + gv + gvel[1]


VMEM = pl.BlockSpec(memory_space=pltpu.VMEM)
SMEM = pl.BlockSpec(memory_space=pltpu.SMEM)
ANY = pl.BlockSpec(memory_space=pl.ANY)
PARAMS = pltpu.CompilerParams(vmem_limit_bytes=VMEM_BYTES)
LAYERS = 6


def scratch_shapes(count, backward, feature_rows):
    local_rows, mid = count + 2 * MARGIN, count + 2 * MID
    shapes = [
        pltpu.VMEM((4, local_rows, N), f32),
        pltpu.VMEM((4, local_rows, N), f32),
        pltpu.VMEM((mid * CH, N), f32),
    ]
    if backward:
        shapes += [
            pltpu.VMEM((mid * CH, N), f32),
            pltpu.VMEM((mid * CH, N), bf16),
            pltpu.VMEM((2, count, N), f32),
        ]
    features = [pltpu.VMEM((feature_rows(m) * CH, N), bf16) for m in range(1, LAYERS + 1)]
    slopes = [pltpu.VMEM(((count + 2 * m) * CH, N), bf16) for m in range(1, LAYERS + 1)]
    return shapes, features, slopes


def run_forward(count, vel, w_first, w_hidden, bias):
    shapes, features, slopes = scratch_shapes(count, False, lambda m: count + 2 * reach(m))
    mid = count + 2 * MID
    return pl.pallas_call(
        functools.partial(forward_kernel, count),
        in_specs=[VMEM] * 4,
        out_specs=[VMEM] + [ANY] * (2 * LAYERS + 1),
        out_shape=[jax.ShapeDtypeStruct((2, count, N), f32)]
        + [jax.ShapeDtypeStruct(((count + 2) * CH, N), bf16)] * LAYERS
        + [jax.ShapeDtypeStruct(((count + 2 * m) * CH, N), bf16) for m in range(1, LAYERS + 1)]
        + [jax.ShapeDtypeStruct((mid * CH, N), f32)],
        scratch_shapes=shapes + [pltpu.SemaphoreType.DMA((2 * LAYERS + 1,))] + features + slopes,
        compiler_params=PARAMS,
        name="forward_first",
    )(vel, w_first, w_hidden, bias)


def run_middle(count, gathered, masks, vel, cot, tables, w_first, w_hidden, bias, b_first, b_hidden):
    shapes, features, slopes = scratch_shapes(count, True, lambda m: count + 2 * reach(m))
    return pl.pallas_call(
        functools.partial(middle_kernel, count, len(gathered)),
        in_specs=[SMEM] + [VMEM] * (len(gathered) + 10),
        out_specs=[VMEM] * 3,
        out_shape=[
            jax.ShapeDtypeStruct((4, count, N), f32),
            jax.ShapeDtypeStruct((2, count, N), f32),
            jax.ShapeDtypeStruct((30 * CH, N), f32),
        ],
        scratch_shapes=shapes + features + slopes + slopes,
        compiler_params=PARAMS,
        name="both_last",
    )(masks, *gathered, vel, cot, *tables, w_first, w_hidden, bias, b_first, b_hidden)


def run_backward(count, gathered, masks, vel, now, tables, b_first, b_hidden, previous, kept):
    shapes, features, slopes = scratch_shapes(count, True, lambda m: count + 2)
    return pl.pallas_call(
        functools.partial(backward_kernel, count, len(gathered)),
        in_specs=[SMEM] + [VMEM] * (len(gathered) + 8) + [ANY] * len(kept),
        out_specs=[VMEM] * 2,
        out_shape=[
            jax.ShapeDtypeStruct((4, count, N), f32),
            jax.ShapeDtypeStruct((30 * CH, N), bf16),
        ],
        scratch_shapes=shapes
        + [pltpu.SemaphoreType.DMA((2 * LAYERS + 1,))]
        + features
        + slopes
        + slopes,
        compiler_params=PARAMS,
        name="backward_first",
    )(masks, *gathered, vel, now, *tables, b_first, b_hidden, previous, *kept)


def swap(x, axis, offset):
    count = lax.axis_size(axis)
    return lax.ppermute(x, axis, [(i, i ^ offset) for i in range(count)])


def from_group(x, ahead):
    count = lax.axis_size("strip")
    return lax.ppermute(x, "strip", [(i, (i - 2 * ahead) % count) for i in range(count)])


def gather_groups(x):
    return [x] + [from_group(x, k) for k in range(1, lax.axis_size("strip") // 2)]


def margins(velocity, pair, core):
    if velocity.shape[2] < MARGIN:
        return from_group(pair[:, -MARGIN:], -1), from_group(pair[:, :MARGIN], 1)
    count = lax.axis_size("strip")
    upper = core == 0
    cross = jnp.where(upper, velocity[1, :, :MARGIN], velocity[0, :, -MARGIN:])
    same = jnp.where(upper, velocity[0, :, :MARGIN], velocity[1, :, -MARGIN:])
    cross = lax.ppermute(
        cross, "strip", [(i, (i - 1) % count if i % 2 == 0 else (i + 1) % count) for i in range(count)]
    )
    same = lax.ppermute(
        same, "strip", [(i, (i - 2) % count if i % 2 == 0 else (i + 2) % count) for i in range(count)]
    )
    return jnp.where(upper, cross, same), jnp.where(upper, same, cross)


def sum_everywhere(x, core):
    t = lax.axis_index("traj")
    parts = lax.axis_size("traj")
    groups = lax.axis_size("strip") // 2
    pick = lambda y, i: lax.dynamic_index_in_dim(y, i, 0, False)
    x = x.reshape(2, -1, N)
    x = pick(x, core).astype(f32) + swap(pick(x, 1 - core), "strip", 1).astype(f32)
    x = x.astype(bf16).reshape(parts, -1, N)
    total = pick(x, t).astype(f32)
    for k in range(1, parts):
        total = total + swap(pick(x, t ^ k), "traj", k).astype(f32)
    x = total.astype(bf16)
    total = x.astype(f32)
    for k in range(1, groups):
        total = total + swap(x, "strip", 2 * k).astype(f32)
    x = total.astype(bf16)
    whole = jnp.zeros((parts,) + x.shape, bf16)
    for k in range(parts):
        block = x if k == 0 else swap(x, "traj", k)
        whole = lax.dynamic_update_slice(whole, block[None], (t ^ k, 0, 0))
    x = whole.reshape(-1, N)
    other = swap(x, "strip", 1)
    return jnp.where(core == 0, jnp.concatenate([x, other]), jnp.concatenate([other, x]))


def wide_kernel(square):
    pad = jnp.zeros(square.shape[:2] + (CH,), square.dtype)
    return jnp.concatenate(
        [jnp.concatenate([square, pad], axis=2), jnp.concatenate([pad, square], axis=2)], axis=1
    )


def prepare_kernels(first, middle, last):
    hidden = jnp.concatenate([middle, last[None]], axis=0).reshape(-1, 3, 3, CH, CH)
    count = hidden.shape[0]
    forward = wide_kernel(hidden.transpose(0, 2, 3, 1, 4).reshape(count, 3 * CH, 3 * CH))
    flipped = hidden[:, ::-1, ::-1]
    backward = wide_kernel(flipped.transpose(0, 2, 4, 1, 3).reshape(count, 3 * CH, 3 * CH))
    taps = first.reshape(3, 3, CH, 2)
    narrow = taps.transpose(1, 2, 3, 0)
    zero = jnp.zeros((3, CH, 2, 1), first.dtype)
    rows_first = [
        jnp.concatenate([narrow, zero], axis=3).reshape(3 * CH, 8),
        jnp.concatenate([zero, narrow], axis=3).reshape(3 * CH, 8),
    ]
    first_forward = jnp.pad(jnp.concatenate(rows_first, axis=0), ((0, 0), (0, 8)))
    back = taps[::-1, ::-1].transpose(1, 3, 0, 2)
    zero = jnp.zeros((3, 2, 1, CH), first.dtype)
    back = jnp.stack([jnp.concatenate([back, zero], axis=2), jnp.concatenate([zero, back], axis=2)], axis=2)
    first_backward = jnp.pad(back.reshape(12, 4 * CH), ((0, 4), (0, 0)))
    return first_forward, forward, first_backward, backward


def unpack(total, hidden):
    blocks = total.reshape(10, 3 * CH, N)
    squares = []
    for pair in range(3):
        wide = jnp.concatenate([blocks[3 * pair + q] for q in range(3)], axis=1)
        squares += [wide[:, : 3 * CH], wide[:, 3 * CH :]]
    kernels = jnp.stack(squares).reshape(6, 3, CH, 3, CH).transpose(0, 3, 1, 2, 4).reshape(6, 9, CH, CH)
    kernels = kernels.astype(f32)
    rest = blocks[9].astype(f32)
    first = rest[:, 0:8].reshape(3, CH, 2, 4)[..., 0:3] + rest[:, 16:24].reshape(3, CH, 2, 4)[..., 1:4]
    first = first.transpose(3, 0, 1, 2).reshape(9, CH, 2)
    biases = rest[:CH, 32 : 32 + hidden + 2].T
    return first, biases[0], kernels[:hidden], biases[1 : hidden + 1], kernels[hidden], biases[hidden + 1]


def per_device(
    velocity, lengths, cotangent, first_kernel, first_bias, middle_kernels, middle_biases, last_kernel, last_bias
):
    rc = velocity.shape[2]
    count = 2 * rc
    core = lax.axis_index("strip") % 2
    upper = core == 0
    pick = lambda y, i: lax.dynamic_index_in_dim(y, i, 0, False)
    join = lambda mine, other, axis: jnp.where(
        upper, jnp.concatenate([mine, other], axis=axis), jnp.concatenate([other, mine], axis=axis)
    )

    both = jnp.concatenate([velocity, cotangent], axis=1)
    pair = join(pick(both, core), swap(pick(both, 1 - core), "strip", 1), 1)
    above, below = margins(velocity, pair[:2], core)
    vel = jnp.concatenate([above, pair[:2], below], axis=1)
    cot = pair[2:]
    masks = (pick(lengths, core) > jnp.arange(STEPS)).astype(f32)

    w_first, w_hidden, b_first, b_hidden = prepare_kernels(first_kernel, middle_kernels, last_kernel)
    bias = jnp.concatenate([first_bias[None], middle_biases, last_bias[None]], axis=0)
    bias = jnp.broadcast_to(bias[:, :, None], bias.shape + (N,))
    tables = tuple(jnp.asarray(x) for x in poisson_tables(N))

    star, *kept = run_forward(count, vel, w_first, w_hidden, bias)
    gathered = gather_groups(jnp.concatenate([star, cot], axis=0))
    back, now, buffer = run_middle(
        count, gathered, masks, vel, cot, tables, w_first, w_hidden, bias, b_first, b_hidden
    )
    gathered = gather_groups(back)
    out, buffer = run_backward(count, gathered, masks, vel, now, tables, b_first, b_hidden, buffer, kept)

    strips = out.reshape(4, 2, rc, N).transpose(1, 0, 2, 3)
    out = join(pick(strips, core)[None], swap(pick(strips, 1 - core), "strip", 1)[None], 0)
    total = sum_everywhere(buffer, core)
    return (out[:, :2], out[:, 2:]) + unpack(total, middle_kernels.shape[0])


def solution(mesh):
    band = P("traj", None, "strip", None)
    return jax.shard_map(
        per_device,
        mesh=mesh,
        in_specs=(band, P("traj"), band) + (P(),) * 6,
        out_specs=(band, band) + (P(),) * 6,
        check_vma=False,
    )
```

```python
import functools
import math

import jax
import jax.numpy as jnp
import numpy as np
from jax import lax
from jax.experimental import pallas as pl
from jax.experimental.pallas import tpu as pltpu
from jax.sharding import PartitionSpec as P

STEPS = 2
DT = 0.25
MARGIN = 16
MID = 8
RAW = 2
CH = 64
LAYERS = 6
N = 128
bf16 = jnp.bfloat16
f32 = jnp.float32
NT = (((1,), (1,)), ((), ()))
VMEM_BYTES = 36 * 2**20


def reach(layer):
    return 12 - layer


def lanes(x, s):
    return x if s == 0 else pltpu.roll(x, (-s) % x.shape[1], 1)


def rows(x, s):
    return x if s == 0 else pltpu.roll(x, (-s) % x.shape[0], 0)


def poisson_tables(length):
    k = np.arange(length)
    angle = 2.0 * math.pi * ((k[:, None] * k[None, :]) % length) / length
    table = (np.cos(angle) + np.sin(angle)) / math.sqrt(length)
    eigen = 2.0 - 2.0 * np.cos(2.0 * math.pi * k / length)
    total = eigen[:, None] + eigen[None, :]
    total[0, 0] = 1.0
    weight = 1.0 / total
    weight[0, 0] = 0.0
    return np.stack([table, weight]).astype(np.float32)


def split(x):
    high = x.astype(bf16)
    return high, (x - high.astype(f32)).astype(bf16)


def times_right(x, right):
    high, low = split(x)
    return jnp.dot(jnp.concatenate([high, low, high], axis=1), right[...], preferred_element_type=f32)


def times_left(x, left):
    high, low = split(x)
    return jnp.dot(left[...], jnp.concatenate([high, high, low], axis=0), preferred_element_type=f32)


def project(fields, right, left, weight):
    count = len(fields)
    source = [u - lanes(u, -1) + (v - rows(v, -1)) for u, v in fields]
    x = times_right(jnp.concatenate(source, axis=0), right)
    x = jnp.concatenate([x[i * N : (i + 1) * N] for i in range(count)], axis=1)
    x = times_left(x, left) * jnp.concatenate([weight[...]] * count, axis=1)
    x = times_left(x, left)
    x = jnp.concatenate([x[:, i * N : (i + 1) * N] for i in range(count)], axis=0)
    x = times_right(x, right)
    out = []
    for i, (u, v) in enumerate(fields):
        p = -x[i * N : (i + 1) * N]
        out.append((u - (lanes(p, 1) - p), v - (rows(p, 1) - p)))
    return out


def local(x, count):
    return jnp.concatenate([x[N - MARGIN :], x[: count + MARGIN]], axis=0)


def fold(o):
    third = o.shape[0] // 3
    return lanes(o[:third], -1) + o[third : 2 * third] + lanes(o[2 * third :], 1)


def conv_rows(window, kernel, low, high, emit, between=lambda: None):
    starts = list(range(low, high, 2))
    for k in range(0, len(starts), 2):
        group = starts[k : k + 2]
        o = jnp.dot(
            kernel[...],
            jnp.concatenate([window(r) for r in group], axis=1),
            preferred_element_type=f32,
        )
        half = o.shape[0] // 2
        for i, r in enumerate(group):
            part = o[:, i * N : (i + 1) * N]
            emit(r, part[:half])
            emit(r + 1, part[half:])
        between()


def first_window(us, vs, r):
    a = r - 1 + MARGIN
    return jnp.concatenate(
        [us[1, a : a + 4, :], vs[1, a : a + 4, :], jnp.zeros((8, N), f32)], axis=0
    ).astype(bf16)


def row_window(ref, low):
    return lambda r: ref[(r - 1 - low) * CH : (r + 3 - low) * CH, :]


def gelu_value(z):
    c = math.sqrt(2.0 / math.pi)
    zz = z * z
    h = 0.5 + 0.5 * jnp.tanh(z * (c + (c * 0.044715) * zz))
    return z * h, h, zz


def gelu_slope(f, h, zz):
    c = math.sqrt(2.0 / math.pi)
    return h + (f - f * h) * (2.0 * c + (6.0 * c * 0.044715) * zz)


def spread_columns(u, v, us, vs):
    for j in range(4):
        us[j] = lanes(u, j - 1)
        vs[j] = lanes(v, j - 1)


def network_forward(count, us, vs, w_first, w_hidden, bias, feats, slopes, raw, raw_done):
    for m in range(1, LAYERS + 1):
        low = -reach(m)

        def emit(r, o, m=m, low=low):
            value, h, zz = gelu_value(fold(o) + bias[m - 1])
            feats[m - 1][(r - low) * CH : (r - low + 1) * CH, :] = value.astype(bf16)
            if -m <= r < count + m:
                slopes[m - 1][(r + m) * CH : (r + m + 1) * CH, :] = gelu_slope(value, h, zz).astype(bf16)

        if m == 1:
            conv_rows(functools.partial(first_window, us, vs), w_first, low, count - low, emit)
        else:
            conv_rows(
                row_window(feats[m - 2], -reach(m - 1)), w_hidden.at[m - 2], low, count - low, emit
            )

    def emit_raw(r, o):
        raw[(r + MID) * CH : (r + MID + 1) * CH, :] = fold(o) + bias[LAYERS]
        raw_done(r)

    conv_rows(
        row_window(feats[-1], -reach(LAYERS)), w_hidden.at[LAYERS - 1], -RAW, count + RAW, emit_raw
    )


TARGETS = ((0.0, -0.5), (-0.5, 0.0), (0.0, -0.5), (-0.5, 0.0))


def moments(values):
    cols = [values[j] + values[4 + j] + (values[8 + j] + values[12 + j]) for j in range(4)]
    lines = [values[4 * i] + values[4 * i + 1] + (values[4 * i + 2] + values[4 * i + 3]) for i in range(4)]
    mean = (cols[0] + cols[1] + (cols[2] + cols[3])) * (1.0 / 16.0)
    mx = (1.5 * (cols[3] - cols[0]) + 0.5 * (cols[2] - cols[1])) * (1.0 / 20.0)
    my = (1.5 * (lines[3] - lines[0]) + 0.5 * (lines[2] - lines[1])) * (1.0 / 20.0)
    return mean, mx, my


def less(values, mean, mx, my):
    by_col = [mean + mx * (j - 1.5) for j in range(4)]
    by_line = [my * (i - 1.5) for i in range(4)]
    return [values[p] - (by_col[p % 4] + by_line[p // 4]) for p in range(16)]


def total_of(terms):
    while len(terms) > 1:
        terms = [a + b for a, b in zip(terms[::2], terms[1::2])] + terms[len(terms) // 2 * 2 :]
    return terms[0]


def patches(src, q):
    a = MARGIN - MID + 8 * q
    return [src[p % 4, a + p // 4 - 1 : a + p // 4 + 7, :] for p in range(16)]


def raw_rows(raw, k, q):
    return [raw[pl.ds(8 * q * CH + k * 16 + p, 8, stride=CH), :] for p in range(16)]


def interpolate(q, sources, raw, interp):
    for which, src in enumerate(sources):
        patch = patches(src, q)
        mean, mx, my = moments(patch)
        clear = less(patch, mean, mx, my)
        for k in (2 * which, 2 * which + 1):
            tx, ty = TARGETS[k]
            value = total_of([a * b for a, b in zip(raw_rows(raw, k, q), clear)])
            interp[k, 8 * q : 8 * q + 8, :] = value + (mean + (tx * mx if tx else ty * my))


def raw_gradient(q, sources, ginterp, graw32, graw):
    at = slice(8 * q, 8 * q + 8)
    for which, src in enumerate(sources):
        patch = patches(src, q)
        clear = less(patch, *moments(patch))
        for k in (2 * which, 2 * which + 1):
            g = ginterp[k, at, :]
            for p in range(16):
                graw32[pl.ds(8 * q * CH + k * 16 + p, 8, stride=CH), :] = clear[p] * g
    at = slice(8 * q * CH, 8 * (q + 1) * CH)
    graw[at, :] = graw32[at, :].astype(bf16)


def spread_back(q, which, raw, ginterp, lines):
    k = 2 * which
    at = slice(8 * q, 8 * q + 8)
    g, h = ginterp[k, at, :], ginterp[k + 1, at, :]
    values = [a * g + b * h for a, b in zip(raw_rows(raw, k, q), raw_rows(raw, k + 1, q))]
    mean, mx, my = moments(values)
    values = less(values, mean - (g + h) * (1.0 / 16.0), mx + h * (0.5 / 20.0), my + g * (0.5 / 20.0))
    for i in range(4):
        lines[which, i, at, :] = total_of([lanes(values[4 * i + j], 1 - j) for j in range(4)])


def carriers(u, v):
    return (
        0.5 * (u + lanes(u, 1)),
        0.5 * (v + lanes(v, 1)),
        0.5 * (u + rows(u, 1)),
        0.5 * (v + rows(v, 1)),
    )


def middle(x, count):
    return x[MARGIN - MID : MARGIN + MID + count]


def provisional(count, u, v, interp):
    flux = [middle(x, count) * interp[k] for k, x in enumerate(carriers(u, v))]
    u, v = middle(u, count), middle(v, count)
    su = u - DT * (flux[0] - lanes(flux[0], -1) + (flux[1] - rows(flux[1], -1)))
    sv = v - DT * (flux[2] - lanes(flux[2], -1) + (flux[3] - rows(flux[3], -1)))
    return su[MID : MID + count], sv[MID : MID + count]


def flux_gradients(count, gu, gv):
    return [
        middle(x, count) * (-DT)
        for x in (gu - lanes(gu, 1), gu - rows(gu, 1), gv - lanes(gv, 1), gv - rows(gv, 1))
    ]


def interp_gradients(count, gu, gv, u, v, ginterp):
    for k, (g, x) in enumerate(zip(flux_gradients(count, gu, gv), carriers(u, v))):
        ginterp[k] = g * middle(x, count)


def velocity_gradients(count, gu, gv, interp, lines):
    half = [0.5 * g * interp[k] for k, g in enumerate(flux_gradients(count, gu, gv))]
    out = []
    for which, g in enumerate((gu, gv)):
        along, across = half[which], half[2 + which]
        x = middle(g, count) + (along + lanes(along, -1)) + (across + rows(across, -1))
        x = x[MID : MID + count]
        for i in range(4):
            x = x + lines[which, i, MID + 1 - i : MID + 1 - i + count, :]
        out.append(x)
    return out


def network_backward(count, w_hidden, slopes, graw, grads, between=lambda: None):
    for m in range(LAYERS, 0, -1):
        source = row_window(graw, -MID) if m == LAYERS else row_window(grads[m], -(m + 1))

        def emit(r, o, m=m):
            at = slice((r + m) * CH, (r + m + 1) * CH)
            grads[m - 1][at, :] = (fold(o) * slopes[m - 1][at, :].astype(f32)).astype(bf16)

        conv_rows(source, w_hidden.at[m - 1], -m, count + m, emit, between)


def input_gradient(count, w_first, grad, gvel):
    window = row_window(grad, -1)
    starts = list(range(0, count, 2))
    for k in range(0, len(starts), 2):
        group = starts[k : k + 2]
        o = jnp.dot(
            w_first[...],
            jnp.concatenate([window(r) for r in group], axis=1),
            preferred_element_type=f32,
        )
        for i, r in enumerate(group):
            part = o[:, i * N : (i + 1) * N]
            both = lanes(part, -1)[0:4] + part[4:8] + lanes(part, 1)[8:12]
            gvel[0, r : r + 2, :] = both[0:2]
            gvel[1, r : r + 2, :] = both[2:4]


def weight_gradients(count, us, vs, feats, graw, grads, buffer, previous):
    starts = list(range(0, count, 2))

    def product(m):
        ref, low = (graw, -MID) if m == LAYERS + 1 else (grads[m - 1], -m)
        left, total = [], None
        for r in starts:
            g = [ref[(r + k - low) * CH : (r + k + 1 - low) * CH, :] for k in range(2)]
            left.append(jnp.concatenate([lanes(x, -e) for x in g for e in (-1, 0, 1)], axis=0))
            for x in g:
                x = x.astype(f32)
                total = x if total is None else total + x
        if m == 1:
            right = [first_window(us, vs, r) for r in starts]
        else:
            right = [row_window(feats[m - 2], -reach(m - 1))(r) for r in starts]
        out = lax.dot_general(
            jnp.concatenate(left, axis=1), jnp.concatenate(right, axis=1), NT, preferred_element_type=f32
        )
        return out, jnp.sum(total, axis=1, keepdims=True)

    def put(block, value):
        at = slice(block * 3 * CH, (block + 1) * 3 * CH)
        if previous is not None:
            value = value + previous[at, :]
        buffer[at, :] = value.astype(buffer.dtype)

    def folded(x):
        return x[: 3 * CH, : 3 * CH] + x[3 * CH :, CH:]

    lane = lax.broadcasted_iota(jnp.int32, (CH, N), 1)
    columns = jnp.zeros((CH, N), f32)
    for pair in range(2, -1, -1):
        upper, total = product(3 + 2 * pair)
        columns = jnp.where(lane == 34 + 2 * pair, total, columns)
        lower, total = product(2 + 2 * pair)
        columns = jnp.where(lane == 33 + 2 * pair, total, columns)
        wide = jnp.concatenate([folded(lower), folded(upper)], axis=1)
        for q in range(3):
            put(3 * pair + q, wide[:, q * N : (q + 1) * N])
    first, total = product(1)
    columns = jnp.where(lane == 32, total, columns)
    first = jnp.concatenate([first[: 3 * CH], first[3 * CH :], jnp.zeros((3 * CH, N - 32), f32)], axis=1)
    put(9, first + jnp.concatenate([columns, jnp.zeros((2 * CH, N), f32)], axis=0))


def prepare_kernel(core, *refs):
    own, f_first, f_hidden, b_first, b_hidden, bias, right, left, weight = refs[9:18]
    sems = refs[27]
    copies = [pltpu.make_async_copy(refs[i], refs[18 + i], sems.at[i]) for i in range(9)]
    for copy in copies:
        copy.start()
    for copy in copies:
        copy.wait()
    vel, cot, first, first_bias, middle, middle_bias, last, last_bias, tables = refs[18:27]
    upper = core[0] == 0
    own[0] = jnp.where(upper, vel[0], vel[1])
    own[1] = jnp.where(upper, cot[0], cot[1])
    zero = jnp.zeros((CH, CH), bf16)
    for m in range(LAYERS):
        tap = (lambda a, e: last[3 * a + e]) if m == LAYERS - 1 else (lambda a, e: middle[m, 3 * a + e])
        for two in range(2):
            for e in range(3):
                at = slice((two * 3 + e) * CH, (two * 3 + e + 1) * CH)
                taps = [tap(q - two, e) if 0 <= q - two < 3 else zero for q in range(4)]
                f_hidden[m, at, :] = jnp.concatenate(taps, axis=1)
                taps = [tap(2 - q + two, 2 - e) if 0 <= q - two < 3 else zero for q in range(4)]
                b_hidden[m, at, :] = jnp.concatenate(
                    [jnp.concatenate(taps[:2], axis=0).T, jnp.concatenate(taps[2:], axis=0).T], axis=1
                )
    lines = jnp.zeros((1, CH), f32)
    for two in range(2):
        for e in range(3):
            taps = [lines] * 16
            for a in range(3):
                for ch in range(2):
                    taps[4 * ch + a + two] = first[3 * a + e, ch : ch + 1, :].astype(f32)
            at = slice((two * 3 + e) * CH, (two * 3 + e + 1) * CH)
            f_first[at, :] = jnp.concatenate(taps, axis=0).T.astype(bf16)
    taps = []
    for e in range(3):
        for ch in range(2):
            for two in range(2):
                line = [
                    first[3 * (2 - q + two) + 2 - e, ch : ch + 1, :].astype(f32) if 0 <= q - two < 3 else lines
                    for q in range(4)
                ]
                taps.append(jnp.concatenate(line, axis=1))
    taps.append(jnp.zeros((4, 4 * CH), f32))
    b_first[...] = jnp.concatenate(taps, axis=0).astype(bf16)
    for m in range(LAYERS + 1):
        if 0 < m < LAYERS:
            line = middle_bias[m - 1 : m, :]
        else:
            line = (first_bias if m == 0 else last_bias)[...].reshape(1, CH)
        bias[m] = jnp.broadcast_to(line, (N, CH)).T
    high, low = split(tables[0])
    right[...] = jnp.concatenate([high, high, low], axis=0)
    left[...] = jnp.concatenate([high, low, high], axis=1)
    weight[...] = tables[1]


def forward_kernel(count, core, own, partner, cross, same, cot_partner, w_first, w_hidden, bias, *rest):
    block, ext, raw = rest[:3]
    feats, slopes = rest[3 : 3 + LAYERS], rest[3 + LAYERS : 3 + 2 * LAYERS]
    us, vs, interp = rest[3 + 2 * LAYERS :]
    upper = core[0] == 0
    above = jnp.where(upper, cross[0], same[1])[:, -MARGIN:]
    below = jnp.where(upper, same[0], cross[1])[:, :MARGIN]

    def pair(mine, other, i):
        other = jnp.where(upper, other[0, i], other[1, i])
        return [jnp.where(upper, mine[i], other), jnp.where(upper, other, mine[i])]

    for i in range(2):
        ext[i] = jnp.concatenate([above[i], *pair(own[0], partner, i), below[i]], axis=0)
        block[2 + i] = jnp.concatenate(pair(own[1], cot_partner, i), axis=0)
    u, v = ext[0], ext[1]
    spread_columns(u, v, us, vs)

    def raw_done(r):
        at = r + 1 + MID
        last = count + RAW
        if at % 8 == 0:
            interpolate(at // 8 - 1, (us, vs), raw, interp)
        elif r + 1 == last:
            interpolate(at // 8, (us, vs), raw, interp)

    network_forward(count, us, vs, w_first, w_hidden, bias, feats, slopes, raw, raw_done)
    su, sv = provisional(count, u, v, interp)
    block[0] = su
    block[1] = sv


def step_mask(lengths, core, step):
    return jnp.where(lengths[core[0]] > step, 1.0, 0.0).astype(f32)


def joined(gathered, i):
    return jnp.concatenate([g[i] for g in gathered], axis=0)


def middle_kernel(count, blocks, core, lengths, *refs):
    gathered, refs = refs[:blocks], refs[blocks:]
    vel, right, left, weight, w_first, w_hidden, bias, b_first, b_hidden = refs[:9]
    back, ext, graw = refs[9:12]
    feats, grads, refs = refs[12:18], refs[18:24], refs[24:]
    us, vs, raw, graw32, interp, ginterp, lines, gvel = refs[:8]
    slopes = refs[8:14]
    su, sv, cu, cv = [joined(gathered, i) for i in range(4)]
    m0, m1 = step_mask(lengths, core, 0), step_mask(lengths, core, 1)
    (nu, nv), (gu, gv) = project([(su, sv), (m1 * cu, m1 * cv)], right, left, weight)
    u = vel[0] + m0 * (local(nu, count) - vel[0])
    v = vel[1] + m0 * (local(nv, count) - vel[1])
    ext[0] = u
    ext[1] = v
    gu, gv = local(gu, count), local(gv, count)
    spread_columns(u, v, us, vs)
    interp_gradients(count, gu, gv, u, v, ginterp)
    chunks = (count + 2 * MID) // 8
    for q in range(chunks):
        raw_gradient(q, (us, vs), ginterp, graw32, graw)
    network_forward(count, us, vs, w_first, w_hidden, bias, feats, slopes, raw, lambda r: None)
    tasks = []
    for q in range(chunks):
        tasks.append(functools.partial(interpolate, q, (us, vs), raw, interp))
        tasks += [functools.partial(spread_back, q, which, raw, ginterp, lines) for which in range(2)]
    turn = [0]

    def between():
        turn[0] += 1
        if tasks and turn[0] % 2 == 0:
            tasks.pop(0)()

    network_backward(count, b_hidden, slopes, graw, grads, between)
    for task in tasks:
        task()
    su, sv = provisional(count, u, v, interp)
    back[0] = su
    back[1] = sv
    input_gradient(count, b_first, grads[0], gvel)
    du, dv = velocity_gradients(count, gu, gv, interp, lines)
    back[2] = (1.0 - m1) * cu[:count] + du + gvel[0]
    back[3] = (1.0 - m1) * cv[:count] + dv + gvel[1]


def weights_kernel(count, ext, graw, *refs):
    feats, grads, buffer, us, vs = refs[:6], refs[6:12], refs[12], refs[13], refs[14]
    spread_columns(ext[0], ext[1], us, vs)
    weight_gradients(count, us, vs, feats, graw, grads, buffer, None)


def backward_kernel(count, blocks, core, lengths, *refs):
    gathered, refs = refs[:blocks], refs[blocks:]
    vel, right, left, weight, b_hidden, previous = refs[:6]
    feats, slopes = refs[6:12], refs[12:18]
    gstar, buffer, grad_first, us, vs, graw32, graw, ginterp = refs[18:26]
    grads = (grad_first,) + refs[26:31]
    m0 = step_mask(lengths, core, 0)
    ((gu, gv),) = project([(m0 * joined(gathered, 2), m0 * joined(gathered, 3))], right, left, weight)
    u, v = vel[0], vel[1]
    gu, gv = local(gu, count), local(gv, count)
    gstar[0] = gu
    gstar[1] = gv
    spread_columns(u, v, us, vs)
    interp_gradients(count, gu, gv, u, v, ginterp)
    for q in range((count + 2 * MID) // 8):
        raw_gradient(q, (us, vs), ginterp, graw32, graw)
    network_backward(count, b_hidden, slopes, graw, grads)
    weight_gradients(count, us, vs, feats, graw, grads, buffer, previous)


def finish_kernel(count, blocks, core, lengths, *refs):
    gathered, refs = refs[:blocks], refs[blocks:]
    vel, now, gstar, raw, grad_first, right, left, weight, b_first, out = refs[:10]
    us, vs, interp, ginterp, lines, gvel = refs[10:]
    m0, m1 = step_mask(lengths, core, 0), step_mask(lengths, core, 1)
    ((nu, nv),) = project([(joined(gathered, 0), joined(gathered, 1))], right, left, weight)
    own = slice(MARGIN, MARGIN + count)
    out[0] = now[0, own] + m1 * (nu[:count] - now[0, own])
    out[1] = now[1, own] + m1 * (nv[:count] - now[1, own])
    u, v, gu, gv = vel[0], vel[1], gstar[0], gstar[1]
    spread_columns(u, v, us, vs)
    interp_gradients(count, gu, gv, u, v, ginterp)
    for q in range((count + 2 * MID) // 8):
        interpolate(q, (us, vs), raw, interp)
        for which in range(2):
            spread_back(q, which, raw, ginterp, lines)
    input_gradient(count, b_first, grad_first, gvel)
    du, dv = velocity_gradients(count, gu, gv, interp, lines)
    out[2] = (1.0 - m0) * gathered[0][2] + du + gvel[0]
    out[3] = (1.0 - m0) * gathered[0][3] + dv + gvel[1]


def unpack_kernel(core, mine, other, first, first_bias, middle, middle_bias, last, last_bias):
    upper = core[0] == 0
    half = mine.shape[0]

    def block(b):
        lines = []
        for low, high, a, c in ((0, half, mine, other), (half, 2 * half, other, mine)):
            start, stop = max(b * 3 * CH, low), min((b + 1) * 3 * CH, high)
            if start < stop:
                x = jnp.where(upper, a[start - low : stop - low, :], c[start - low : stop - low, :])
                lines.append(x.astype(f32))
        return lines[0] if len(lines) == 1 else jnp.concatenate(lines, axis=0)

    for pair in range(3):
        wide = jnp.concatenate([block(3 * pair + q) for q in range(3)], axis=1)
        for side in range(2):
            m = 2 * pair + side
            for a in range(3):
                at = (3 * side + a) * CH
                part = wide[:, at : at + CH]
                for e in range(3):
                    value = part[e * CH : (e + 1) * CH]
                    if m < LAYERS - 1:
                        middle[m, 3 * a + e] = value
                    else:
                        last[3 * a + e] = value
    rest = block(9)
    turned = [rest[e * CH : (e + 1) * CH].T for e in range(3)]
    for a in range(3):
        for e in range(3):
            for ch in range(2):
                low, high = 4 * ch + a, 16 + 4 * ch + a + 1
                first[3 * a + e, ch : ch + 1, :] = turned[e][low : low + 1] + turned[e][high : high + 1]
    turned = turned[0]
    first_bias[...] = turned[32]
    middle_bias[...] = turned[33 : 33 + LAYERS - 1]
    last_bias[...] = turned[32 + LAYERS]


VMEM = pl.BlockSpec(memory_space=pltpu.VMEM)
SMEM = pl.BlockSpec(memory_space=pltpu.SMEM)
PARAMS = pltpu.CompilerParams(vmem_limit_bytes=VMEM_BYTES)


def array(dtype, *shape):
    return jax.ShapeDtypeStruct(shape, dtype)


def cost(flops, moved):
    return pl.CostEstimate(flops=flops, bytes_accessed=moved, transcendentals=0)


def field(count, *lead):
    return pltpu.VMEM(lead + (count, N), f32)


def feature_arrays(count):
    return [array(bf16, (count + 2 * reach(m)) * CH, N) for m in range(1, LAYERS + 1)]


def slope_arrays(count):
    return [array(bf16, (count + 2 * m) * CH, N) for m in range(1, LAYERS + 1)]


def call(kernel, name, flops, smem, inputs, out, scratch=()):
    return pl.pallas_call(
        kernel,
        in_specs=[SMEM] * len(smem) + [VMEM] * len(inputs),
        out_specs=jax.tree.map(lambda _: VMEM, out),
        out_shape=out,
        scratch_shapes=list(scratch),
        compiler_params=PARAMS,
        cost_estimate=cost(flops, 10**6),
        name=name,
    )(*smem, *inputs)


def run_prepare(core, vel, cot, params):
    rc = vel.shape[2]
    out = [
        array(f32, 2, 2, rc, N),
        array(bf16, 6 * CH, 16),
        array(bf16, LAYERS, 6 * CH, 4 * CH),
        array(bf16, 16, 4 * CH),
        array(bf16, LAYERS, 6 * CH, 4 * CH),
        array(f32, LAYERS + 1, CH, N),
        array(bf16, 3 * N, N),
        array(bf16, N, 3 * N),
        array(f32, N, N),
    ]
    inputs = [vel, cot, *params, jnp.asarray(poisson_tables(N))]
    inputs = [pltpu.with_memory_space_constraint(x, pltpu.HBM) for x in inputs]
    return pl.pallas_call(
        prepare_kernel,
        in_specs=[SMEM] + [pl.BlockSpec(memory_space=pltpu.HBM)] * len(inputs),
        out_specs=[VMEM] * len(out),
        out_shape=out,
        scratch_shapes=[pltpu.VMEM(x.shape, x.dtype) for x in inputs]
        + [pltpu.SemaphoreType.DMA((len(inputs),))],
        compiler_params=PARAMS,
        cost_estimate=cost(10**9, 10**6),
        name="prepare",
    )(core, *inputs)


def run_forward(count, core, fields, w_first, w_hidden, bias):
    local_rows, mid = count + 2 * MARGIN, count + 2 * MID
    out = [array(f32, 4, count, N), array(f32, 2, local_rows, N), array(f32, mid * CH, N)]
    out += feature_arrays(count) + slope_arrays(count)
    return call(
        functools.partial(forward_kernel, count),
        "forward_first",
        4 * 10**9,
        [core],
        [*fields, w_first, w_hidden, bias],
        out,
        [field(local_rows, 4), field(local_rows, 4), field(mid, 4)],
    )


def run_middle(count, core, lengths, gathered, vel, tables, w_first, w_hidden, bias, b_first, b_hidden):
    local_rows, mid = count + 2 * MARGIN, count + 2 * MID
    out = [array(f32, 4, count, N), array(f32, 2, local_rows, N), array(bf16, mid * CH, N)]
    out += feature_arrays(count) + slope_arrays(count)
    scratch = [field(local_rows, 4), field(local_rows, 4), field(mid * CH), field(mid * CH)]
    scratch += [field(mid, 4), field(mid, 4), field(mid, 2, 4), field(count, 2)]
    scratch += [pltpu.VMEM(x.shape, x.dtype) for x in slope_arrays(count)]
    return call(
        functools.partial(middle_kernel, count, len(gathered)),
        "both_last",
        8 * 10**9,
        [core, lengths],
        [*gathered, vel, *tables, w_first, w_hidden, bias, b_first, b_hidden],
        out,
        scratch,
    )


def run_weights(count, ext, graw, feats, grads):
    return call(
        functools.partial(weights_kernel, count),
        "weights_last",
        3 * 10**9,
        [],
        [ext, graw, *feats, *grads],
        array(f32, 30 * CH, N),
        [field(count + 2 * MARGIN, 4)] * 2,
    )


def run_backward(count, core, lengths, gathered, vel, tables, b_hidden, previous, feats, slopes):
    local_rows, mid = count + 2 * MARGIN, count + 2 * MID
    out = [
        array(f32, 2, local_rows, N),
        array(bf16, 30 * CH, N),
        array(bf16, (count + 2) * CH, N),
    ]
    scratch = [field(local_rows, 4), field(local_rows, 4), field(mid * CH)]
    scratch += [pltpu.VMEM((mid * CH, N), bf16), field(mid, 4)]
    scratch += [pltpu.VMEM(x.shape, x.dtype) for x in slope_arrays(count)[1:]]
    return call(
        functools.partial(backward_kernel, count, len(gathered)),
        "backward_first",
        8 * 10**9,
        [core, lengths],
        [*gathered, vel, *tables, b_hidden, previous, *feats, *slopes],
        out,
        scratch,
    )


def run_finish(count, core, lengths, gathered, vel, now, gstar, raw, grad_first, tables, b_first):
    local_rows, mid = count + 2 * MARGIN, count + 2 * MID
    return call(
        functools.partial(finish_kernel, count, len(gathered)),
        "finish",
        10**9,
        [core, lengths],
        [*gathered, vel, now, gstar, raw, grad_first, *tables, b_first],
        array(f32, 4, count, N),
        [field(local_rows, 4), field(local_rows, 4), field(mid, 4), field(mid, 4), field(mid, 2, 4), field(count, 2)],
    )


def run_unpack(core, mine, other):
    return pl.pallas_call(
        unpack_kernel,
        in_specs=[SMEM] + [VMEM] * 2,
        out_specs=[VMEM] * 6,
        out_shape=[
            array(f32, 9, 2, CH),
            array(f32, CH),
            array(f32, LAYERS - 1, 9, CH, CH),
            array(f32, LAYERS - 1, CH),
            array(f32, 9, CH, CH),
            array(f32, CH),
        ],
        compiler_params=PARAMS,
        cost_estimate=cost(10**7, 2 * 10**6),
        name="unpack",
    )(core, mine, other)


def swap(x, axis, offset):
    count = lax.axis_size(axis)
    return lax.ppermute(x, axis, [(i, i ^ offset) for i in range(count)])


def from_group(x, ahead):
    count = lax.axis_size("strip")
    return lax.ppermute(x, "strip", [(i, (i - 2 * ahead) % count) for i in range(count)])


def gather_groups(x):
    return [x] + [from_group(x, k) for k in range(1, lax.axis_size("strip") // 2)]


def margins(velocity, partner, core):
    count = lax.axis_size("strip")
    if velocity.shape[2] < MARGIN:
        upper = core[0] == 0
        pair = jnp.where(
            upper,
            jnp.concatenate([velocity[0], partner[0]], axis=1),
            jnp.concatenate([partner[1], velocity[1]], axis=1),
        )
        above, below = from_group(pair[:, -MARGIN:], -1), from_group(pair[:, :MARGIN], 1)
        return jnp.stack([above, below]), jnp.stack([below, above])
    cross = [(i, (i - 1) % count if i % 2 == 0 else (i + 1) % count) for i in range(count)]
    same = [(i, (i - 2) % count if i % 2 == 0 else (i + 2) % count) for i in range(count)]
    return lax.ppermute(velocity, "strip", cross), lax.ppermute(velocity, "strip", same)


def sum_everywhere(x, core):
    t = lax.axis_index("traj")
    parts = lax.axis_size("traj")
    groups = lax.axis_size("strip") // 2
    pick = lambda y, i: lax.dynamic_index_in_dim(y, i, 0, False)
    other = swap(x, "strip", 1)
    x = pick(x.reshape(2, -1, N), core).astype(f32) + pick(other.reshape(2, -1, N), core).astype(f32)
    x = x.astype(bf16).reshape(parts, -1, N)
    total = pick(x, t).astype(f32)
    for k in range(1, parts):
        total = total + swap(pick(x, t ^ k), "traj", k).astype(f32)
    x = total.astype(bf16)
    total = x.astype(f32)
    for k in range(1, groups):
        total = total + swap(x, "strip", 2 * k).astype(f32)
    x = total.astype(bf16)
    whole = jnp.zeros((parts,) + x.shape, bf16)
    for k in range(parts):
        block = x if k == 0 else swap(x, "traj", k)
        whole = lax.dynamic_update_slice(whole, block[None], (t ^ k, 0, 0))
    x = whole.reshape(-1, N)
    return x, swap(x, "strip", 1)


def per_device(
    velocity, lengths, cotangent, first_kernel, first_bias, middle_kernels, middle_biases, last_kernel, last_bias
):
    rc = velocity.shape[2]
    count = 2 * rc
    index = lax.axis_index("strip") & 1
    core = index[None]
    pick = lambda y, i: lax.dynamic_index_in_dim(y, i, 0, False)

    partner = swap(velocity, "strip", 1)
    cross, same = margins(velocity, partner, core)
    cot_partner = swap(cotangent, "strip", 1)
    first_kernel = first_kernel.transpose(0, 2, 1)
    params = (first_kernel, first_bias, middle_kernels, middle_biases, last_kernel, last_bias)
    own, w_first, w_hidden, b_first, b_hidden, bias, *tables = run_prepare(core, velocity, cotangent, params)

    fields = (own, partner, cross, same, cot_partner)
    block, vel, raw, *kept = run_forward(count, core, fields, w_first, w_hidden, bias)
    feats, slopes = kept[:LAYERS], kept[LAYERS:]
    gathered = gather_groups(block)
    back, now, graw, *kept = run_middle(
        count, core, lengths, gathered, vel, tables, w_first, w_hidden, bias, b_first, b_hidden
    )
    gathered = gather_groups(back)
    buffer = run_weights(count, now, graw, kept[:LAYERS], kept[LAYERS:])
    gstar, buffer, grad_first = run_backward(
        count, core, lengths, gathered, vel, tables, b_hidden, buffer, feats, slopes
    )
    out = run_finish(count, core, lengths, gathered, vel, now, gstar, raw, grad_first, tables, b_first)

    strips = out.reshape(4, 2, rc, N).transpose(1, 0, 2, 3)
    mine, other = pick(strips, index)[None], swap(pick(strips, 1 - index), "strip", 1)[None]
    out = jnp.where(
        index == 0, jnp.concatenate([mine, other], axis=0), jnp.concatenate([other, mine], axis=0)
    )
    mine, other = sum_everywhere(buffer, index)
    first, *rest = run_unpack(core, mine, other)
    return (out[:, :2], out[:, 2:], first.transpose(0, 2, 1), *rest)


def solution(mesh):
    band = P("traj", None, "strip", None)
    return jax.shard_map(
        per_device,
        mesh=mesh,
        in_specs=(band, P("traj"), band) + (P(),) * 6,
        out_specs=(band, band) + (P(),) * 6,
        check_vma=False,
    )
```

```python
import functools
import math

import jax
import jax.numpy as jnp
import numpy as np
from jax import lax
from jax.experimental import pallas as pl
from jax.experimental.pallas import tpu as pltpu
from jax.sharding import PartitionSpec as P

STEPS = 2
DT = 0.25
MARGIN = 16
MID = 8
RAW = 2
CH = 64
LAYERS = 6
N = 128
BUFFER = 30 * CH
bf16 = jnp.bfloat16
f32 = jnp.float32
NT = (((1,), (1,)), ((), ()))
VMEM_BYTES = 14 * 2**20


def reach(layer):
    return 12 - layer


def place(start, size):
    return slice(start, start + size) if isinstance(start, int) else pl.ds(pl.multiple_of(start, CH), size)


def feature_rows(count, layer, r, rows=1):
    return place(((layer - 1) * (count + 24) + r + 12) * CH, rows * CH)


def gradient_rows(count, layer, r, rows=1):
    return place(((layer - 1) * (count + 16) + r + 8) * CH, rows * CH)


def lanes(x, s):
    return x if s == 0 else pltpu.roll(x, (-s) % x.shape[1], 1)


def rows(x, s):
    return x if s == 0 else pltpu.roll(x, (-s) % x.shape[0], 0)


def poisson_tables(length):
    k = np.arange(length)
    angle = 2.0 * math.pi * ((k[:, None] * k[None, :]) % length) / length
    table = (np.cos(angle) + np.sin(angle)) / math.sqrt(length)
    eigen = 2.0 - 2.0 * np.cos(2.0 * math.pi * k / length)
    total = eigen[:, None] + eigen[None, :]
    total[0, 0] = 1.0
    weight = 1.0 / total
    weight[0, 0] = 0.0
    return np.stack([table, weight]).astype(np.float32)


def split(x):
    high = x.astype(bf16)
    return high, (x - high.astype(f32)).astype(bf16)


def times_right(x, right):
    high, low = split(x)
    return jnp.dot(jnp.concatenate([high, low, high], axis=1), right[...], preferred_element_type=f32)


def times_left(x, left):
    high, low = split(x)
    return jnp.dot(left[...], jnp.concatenate([high, high, low], axis=0), preferred_element_type=f32)


def project(fields, right, left, weight):
    count = len(fields)
    source = [u - lanes(u, -1) + (v - rows(v, -1)) for u, v in fields]
    x = times_right(jnp.concatenate(source, axis=0), right)
    x = jnp.concatenate([x[i * N : (i + 1) * N] for i in range(count)], axis=1)
    x = times_left(x, left) * jnp.concatenate([weight[...]] * count, axis=1)
    x = times_left(x, left)
    x = jnp.concatenate([x[:, i * N : (i + 1) * N] for i in range(count)], axis=0)
    x = times_right(x, right)
    out = []
    for i, (u, v) in enumerate(fields):
        p = -x[i * N : (i + 1) * N]
        out.append((u - (lanes(p, 1) - p), v - (rows(p, 1) - p)))
    return out


def local(x, count):
    return jnp.concatenate([x[N - MARGIN :], x[: count + MARGIN]], axis=0)


def fold(o):
    third = o.shape[0] // 3
    return lanes(o[:third], -1) + o[third : 2 * third] + lanes(o[2 * third :], 1)


def fold_rounded(o):
    third = o.shape[0] // 3
    left, right = lanes(o[:third].astype(bf16), -1), lanes(o[2 * third :].astype(bf16), 1)
    return left.astype(f32) + o[third : 2 * third] + right.astype(f32)


def conv_rows(window, kernel, low, high, emit, between=lambda: None):
    starts = list(range(low, high, 2))
    for k in range(0, len(starts), 2):
        group = starts[k : k + 2]
        o = jnp.dot(
            kernel[...],
            jnp.concatenate([window(r) for r in group], axis=1),
            preferred_element_type=f32,
        )
        half = o.shape[0] // 2
        for i, r in enumerate(group):
            part = o[:, i * N : (i + 1) * N]
            emit(r, part[:half])
            emit(r + 1, part[half:])
        between()


def first_window(us, vs, r):
    a = r - 1 + MARGIN
    return jnp.concatenate(
        [us[1, a : a + 4, :], vs[1, a : a + 4, :], jnp.zeros((8, N), f32)], axis=0
    ).astype(bf16)


def feature_window(feats, count, layer):
    return lambda r: feats[feature_rows(count, layer, r - 1, 4), :]


def gradient_window(grads, count, layer):
    return lambda r: grads[gradient_rows(count, layer, r - 1, 4), :]


def gelu_value(z):
    c = math.sqrt(2.0 / math.pi)
    zz = z * z
    h = 0.5 + 0.5 * jnp.tanh(z * (c + (c * 0.044715) * zz))
    return z * h, h, zz


def gelu_slope(f, h, zz):
    c = math.sqrt(2.0 / math.pi)
    return h + (f - f * h) * (2.0 * c + (6.0 * c * 0.044715) * zz)


def spread_columns(u, v, us, vs):
    for j in range(4):
        us[j] = lanes(u, j - 1)
        vs[j] = lanes(v, j - 1)


def network_forward(count, us, vs, w_first, w_hidden, bias, feats, slopes, raw, raw_done):
    for m in range(1, LAYERS + 1):

        def emit(r, o, m=m):
            value, h, zz = gelu_value(fold(o) + bias[m - 1])
            feats[feature_rows(count, m, r), :] = value.astype(bf16)
            if -m <= r < count + m:
                slopes[gradient_rows(count, m, r), :] = gelu_slope(value, h, zz).astype(bf16)

        low, high = -reach(m), count + reach(m)
        if m == 1:
            conv_rows(functools.partial(first_window, us, vs), w_first, low, high, emit)
        else:
            conv_rows(feature_window(feats, count, m - 1), w_hidden.at[m - 2], low, high, emit)

    def emit_raw(r, o):
        raw[(r + MID) * CH : (r + MID + 1) * CH, :] = fold(o) + bias[LAYERS]
        raw_done(r)

    conv_rows(
        feature_window(feats, count, LAYERS), w_hidden.at[LAYERS - 1], -RAW, count + RAW, emit_raw
    )


TARGETS = ((0.0, -0.5), (-0.5, 0.0), (0.0, -0.5), (-0.5, 0.0))


def moments(values):
    cols = [values[j] + values[4 + j] + (values[8 + j] + values[12 + j]) for j in range(4)]
    lines = [values[4 * i] + values[4 * i + 1] + (values[4 * i + 2] + values[4 * i + 3]) for i in range(4)]
    mean = (cols[0] + cols[1] + (cols[2] + cols[3])) * (1.0 / 16.0)
    mx = (1.5 * (cols[3] - cols[0]) + 0.5 * (cols[2] - cols[1])) * (1.0 / 20.0)
    my = (1.5 * (lines[3] - lines[0]) + 0.5 * (lines[2] - lines[1])) * (1.0 / 20.0)
    return mean, mx, my


def less(values, mean, mx, my):
    by_col = [mean + mx * (j - 1.5) for j in range(4)]
    by_line = [my * (i - 1.5) for i in range(4)]
    return [values[p] - (by_col[p % 4] + by_line[p // 4]) for p in range(16)]


def total_of(terms):
    while len(terms) > 1:
        terms = [a + b for a, b in zip(terms[::2], terms[1::2])] + terms[len(terms) // 2 * 2 :]
    return terms[0]


def patches(src, q):
    a = MARGIN - MID + 8 * q
    return [src[p % 4, a + p // 4 - 1 : a + p // 4 + 7, :] for p in range(16)]


def raw_rows(raw, k, q):
    return [raw[pl.ds(8 * q * CH + k * 16 + p, 8, stride=CH), :] for p in range(16)]


def eight(q):
    return slice(8 * q, 8 * q + 8) if isinstance(q, int) else pl.ds(pl.multiple_of(8 * q, 8), 8)


def interpolate(q, sources, raw, interp):
    for which, src in enumerate(sources):
        patch = patches(src, q)
        mean, mx, my = moments(patch)
        clear = less(patch, mean, mx, my)
        for k in (2 * which, 2 * which + 1):
            tx, ty = TARGETS[k]
            value = total_of([a * b for a, b in zip(raw_rows(raw, k, q), clear)])
            interp[k, 8 * q : 8 * q + 8, :] = value + (mean + (tx * mx if tx else ty * my))


def raw_gradient(count, q, sources, ginterp, graw32, grads):
    at = slice(8 * q, 8 * q + 8)
    for which, src in enumerate(sources):
        patch = patches(src, q)
        clear = less(patch, *moments(patch))
        for k in (2 * which, 2 * which + 1):
            g = ginterp[k, at, :]
            for p in range(16):
                graw32[pl.ds(k * 16 + p, 8, stride=CH), :] = clear[p] * g
    grads[gradient_rows(count, LAYERS + 1, 8 * q - MID, 8), :] = graw32[...].astype(bf16)


def spread_back(q, which, raw, ginterp, lines):
    k = 2 * which
    at = eight(q)
    g, h = ginterp[k, at, :], ginterp[k + 1, at, :]
    values = [a * g + b * h for a, b in zip(raw_rows(raw, k, q), raw_rows(raw, k + 1, q))]
    mean, mx, my = moments(values)
    values = less(values, mean - (g + h) * (1.0 / 16.0), mx + h * (0.5 / 20.0), my + g * (0.5 / 20.0))
    for i in range(4):
        lines[which, i, at, :] = total_of([lanes(values[4 * i + j], 1 - j) for j in range(4)])


def carriers(u, v):
    return (
        0.5 * (u + lanes(u, 1)),
        0.5 * (v + lanes(v, 1)),
        0.5 * (u + rows(u, 1)),
        0.5 * (v + rows(v, 1)),
    )


def middle(x, count):
    return x[MARGIN - MID : MARGIN + MID + count]


def provisional(count, u, v, interp):
    flux = [middle(x, count) * interp[k] for k, x in enumerate(carriers(u, v))]
    u, v = middle(u, count), middle(v, count)
    su = u - DT * (flux[0] - lanes(flux[0], -1) + (flux[1] - rows(flux[1], -1)))
    sv = v - DT * (flux[2] - lanes(flux[2], -1) + (flux[3] - rows(flux[3], -1)))
    return su[MID : MID + count], sv[MID : MID + count]


def flux_gradients(count, gu, gv):
    return [
        middle(x, count) * (-DT)
        for x in (gu - lanes(gu, 1), gu - rows(gu, 1), gv - lanes(gv, 1), gv - rows(gv, 1))
    ]


def interp_gradients(count, gu, gv, u, v, ginterp):
    for k, (g, x) in enumerate(zip(flux_gradients(count, gu, gv), carriers(u, v))):
        ginterp[k] = g * middle(x, count)


def velocity_gradients(count, gu, gv, interp, lines):
    half = [0.5 * g * interp[k] for k, g in enumerate(flux_gradients(count, gu, gv))]
    out = []
    for which, g in enumerate((gu, gv)):
        along, across = half[which], half[2 + which]
        x = middle(g, count) + (along + lanes(along, -1)) + (across + rows(across, -1))
        x = x[MID : MID + count]
        for i in range(4):
            x = x + lines[which, i, MID + 1 - i : MID + 1 - i + count, :]
        out.append(x)
    return out


def network_backward(count, w_hidden, slopes, grads, between=lambda: None):
    for m in range(LAYERS, 0, -1):

        def emit(r, o, m=m):
            at = gradient_rows(count, m, r)
            grads[at, :] = (fold_rounded(o) * slopes[at, :].astype(f32)).astype(bf16)

        conv_rows(gradient_window(grads, count, m + 1), w_hidden.at[m - 1], -m, count + m, emit, between)


def input_gradient(count, w_first, grads, gvel):
    window = gradient_window(grads, count, 1)
    starts = list(range(0, count, 2))
    for k in range(0, len(starts), 2):
        group = starts[k : k + 2]
        o = jnp.dot(
            w_first[...],
            jnp.concatenate([window(r) for r in group], axis=1),
            preferred_element_type=f32,
        )
        for i, r in enumerate(group):
            part = o[:, i * N : (i + 1) * N]
            both = lanes(part, -1)[0:4] + part[4:8] + lanes(part, 1)[8:12]
            gvel[0, r : r + 2, :] = both[0:2]
            gvel[1, r : r + 2, :] = both[2:4]


def folded(x):
    return x[: 3 * CH, : 3 * CH] + x[3 * CH :, CH:]


def weight_product(count, m, us, vs, feats, grads):
    starts = list(range(0, count, 2))
    left, total = [], None
    for r in starts:
        g = [grads[gradient_rows(count, m, r + k), :] for k in range(2)]
        left.append(jnp.concatenate([lanes(x, -e) for x in g for e in (-1, 0, 1)], axis=0))
        for x in g:
            x = x.astype(f32)
            total = x if total is None else total + x
    if isinstance(m, int) and m == 1:
        right = [first_window(us, vs, r) for r in starts]
    else:
        right = [feature_window(feats, count, m - 1)(r) for r in starts]
    out = lax.dot_general(
        jnp.concatenate(left, axis=1), jnp.concatenate(right, axis=1), NT, preferred_element_type=f32
    )
    return out, jnp.sum(total, axis=1, keepdims=True)


def weight_gradients(count, us, vs, feats, grads, put, columns, loop):
    lane = lax.broadcasted_iota(jnp.int32, (CH, N), 1)

    def pair_of(pair):
        lower, a = weight_product(count, 2 + 2 * pair, us, vs, feats, grads)
        upper, b = weight_product(count, 3 + 2 * pair, us, vs, feats, grads)
        x = jnp.where(lane == 33 + 2 * pair, a, columns[...])
        columns[...] = jnp.where(lane == 34 + 2 * pair, b, x)
        wide = jnp.concatenate([folded(lower), folded(upper)], axis=1)
        for q in range(3):
            put(3 * pair + q, wide[:, q * N : (q + 1) * N])

    columns[...] = jnp.zeros((CH, N), f32)
    if loop:
        lax.fori_loop(0, 3, lambda pair, _: (pair_of(pair), 0)[1], 0)
    else:
        for pair in range(2, -1, -1):
            pair_of(pair)
    first, total = weight_product(count, 1, us, vs, feats, grads)
    rest = jnp.where(lane == 32, total, columns[...])
    first = jnp.concatenate([first[: 3 * CH], first[3 * CH :], jnp.zeros((3 * CH, N - 32), f32)], axis=1)
    put(9, first + jnp.concatenate([rest, jnp.zeros((2 * CH, N), f32)], axis=0))


def prepare_kernel(core, group, lengths, *refs):
    own, f_first, f_hidden, b_first, b_hidden, bias, right, left, weight, flags = refs[9:19]
    sems = refs[28]
    copies = [pltpu.make_async_copy(refs[i], refs[19 + i], sems.at[i]) for i in range(9)]
    for copy in copies:
        copy.start()
    upper = core[0] == 0
    for i in range(STEPS):
        flags[i] = jnp.full((8, N), jnp.where(lengths[core[0]] > i, 1.0, 0.0), f32)
    flags[STEPS] = jnp.full((8, N), jnp.where(upper, 1.0, 0.0), f32)
    for bit in range(flags.shape[0] - STEPS - 1):
        flags[STEPS + 1 + bit] = jnp.full((8, N), jnp.where((group[0] >> bit) & 1 == 1, 1.0, 0.0), f32)
    for copy in copies:
        copy.wait()
    vel, cot, first, first_bias, middle, middle_bias, last, last_bias, tables = refs[19:28]
    own[0] = jnp.where(upper, vel[0], vel[1])
    own[1] = jnp.where(upper, cot[0], cot[1])
    zero = jnp.zeros((CH, CH), bf16)
    for m in range(LAYERS):
        tap = (lambda a, e: last[3 * a + e]) if m == LAYERS - 1 else (lambda a, e: middle[m, 3 * a + e])
        for two in range(2):
            for e in range(3):
                at = slice((two * 3 + e) * CH, (two * 3 + e + 1) * CH)
                taps = [tap(q - two, e) if 0 <= q - two < 3 else zero for q in range(4)]
                f_hidden[m, at, :] = jnp.concatenate(taps, axis=1)
                taps = [tap(2 - q + two, 2 - e) if 0 <= q - two < 3 else zero for q in range(4)]
                b_hidden[m, at, :] = jnp.concatenate(
                    [jnp.concatenate(taps[:2], axis=0).T, jnp.concatenate(taps[2:], axis=0).T], axis=1
                )
    lines = jnp.zeros((1, CH), f32)
    for two in range(2):
        for e in range(3):
            taps = [lines] * 16
            for a in range(3):
                for ch in range(2):
                    taps[4 * ch + a + two] = first[3 * a + e, ch : ch + 1, :].astype(f32)
            at = slice((two * 3 + e) * CH, (two * 3 + e + 1) * CH)
            f_first[at, :] = jnp.concatenate(taps, axis=0).T.astype(bf16)
    taps = []
    for e in range(3):
        for ch in range(2):
            for two in range(2):
                line = [
                    first[3 * (2 - q + two) + 2 - e, ch : ch + 1, :].astype(f32) if 0 <= q - two < 3 else lines
                    for q in range(4)
                ]
                taps.append(jnp.concatenate(line, axis=1))
    taps.append(jnp.zeros((4, 4 * CH), f32))
    b_first[...] = jnp.concatenate(taps, axis=0).astype(bf16)
    for m in range(LAYERS + 1):
        if 0 < m < LAYERS:
            line = middle_bias[m - 1 : m, :]
        else:
            line = (first_bias if m == 0 else last_bias)[...].reshape(1, CH)
        bias[m] = jnp.broadcast_to(line, (N, CH)).T
    high, low = split(tables[0])
    right[...] = jnp.concatenate([high, high, low], axis=0)
    left[...] = jnp.concatenate([high, low, high], axis=1)
    weight[...] = tables[1]


def chosen(flag, x, y):
    flag = flag[0:1, :] > 0.5
    return jnp.where(jnp.broadcast_to(flag, x.shape), x, y)


def assemble_kernel(flags, own, partner, cross, same, cot_partner, ext, cot):
    upper = flags[STEPS]

    def pair(mine, other, i):
        other = chosen(upper, other[0, i], other[1, i])
        return [chosen(upper, mine[i], other), chosen(upper, other, mine[i])]

    for i in range(2):
        above = chosen(upper, cross[0, i], same[1, i])[-MARGIN:]
        below = chosen(upper, same[0, i], cross[1, i])[:MARGIN]
        ext[i] = jnp.concatenate([above, *pair(own[0], partner, i), below], axis=0)
        cot[i] = jnp.concatenate(pair(own[1], cot_partner, i), axis=0)


def network_kernel(count, vel, extra, w_first, w_hidden, bias, block, interp, raw, feats, slopes, us, vs):
    u, v = vel[0], vel[1]
    spread_columns(u, v, us, vs)

    def raw_done(r):
        at = r + 1 + MID
        if at % 8 == 0:
            interpolate(at // 8 - 1, (us, vs), raw, interp)
        elif r + 1 == count + RAW:
            interpolate(at // 8, (us, vs), raw, interp)

    network_forward(count, us, vs, w_first, w_hidden, bias, feats, slopes, raw, raw_done)
    su, sv = provisional(count, u, v, interp)
    block[0] = su
    block[1] = sv
    block[2] = extra[0]
    block[3] = extra[1]


def joined(gathered, i):
    return jnp.concatenate([g[i] for g in gathered], axis=0)


def project_kernel(count, blocks, steps, flags, *refs):
    gathered, refs = refs[:blocks], refs[blocks:]
    vel, right, left, weight, gstar, own, *ext = refs
    su, sv, cu, cv = [joined(gathered, i) for i in range(4)]
    mv, mg = [flags[step][0:1, :] for step in steps]
    news, grads = project([(su, sv), (mg * cu, mg * cv)], right, left, weight)
    for i in range(2):
        x = vel[i] + mv * (local(news[i], count) - vel[i])
        for ref in ext:
            ref[i] = x
        own[i] = x[MARGIN : MARGIN + count]
        gstar[i] = local(grads[i], count)
        own[2 + i] = (1.0 - mg) * gathered[0][2 + i]


def back_kernel(count, ext, gstar, b_first, b_hidden, slopes, *refs):
    if len(refs) == 8:
        raw, grads, gvel, lines, us, vs, graw32, ginterp = refs
    else:
        raw, lines = None, None
        grads, gvel, us, vs, graw32, ginterp = refs
    u, v = ext[0], ext[1]
    spread_columns(u, v, us, vs)
    interp_gradients(count, gstar[0], gstar[1], u, v, ginterp)
    chunks = (count + 2 * MID) // 8
    for q in range(chunks):
        raw_gradient(count, q, (us, vs), ginterp, graw32, grads)
    tasks = []
    if raw is not None:
        tasks = [functools.partial(spread_back, q, w, raw, ginterp, lines) for q in range(chunks) for w in range(2)]
    turn = [0]

    def between():
        turn[0] += 1
        if tasks and turn[0] % 4 == 0:
            tasks.pop(0)()

    network_backward(count, b_hidden, slopes, grads, between)
    for task in tasks:
        task()
    input_gradient(count, b_first, grads, gvel)


def finish_kernel(count, front, base, ext, gstar, interp, gvel, *refs):
    raw, out, lines, ginterp = refs if len(refs) == 4 else (None, refs[1], refs[0], None)
    gu, gv = gstar[0], gstar[1]
    if raw is not None:
        interp_gradients(count, gu, gv, ext[0], ext[1], ginterp)

        def step(q, _):
            for which in range(2):
                spread_back(q, which, raw, ginterp, lines)
            return 0

        lax.fori_loop(0, (count + 2 * MID) // 8, step, 0)
    change = velocity_gradients(count, gu, gv, interp, lines)
    for i in range(2):
        out[i] = front[i]
        out[2 + i] = base[2 + i] + change[i] + gvel[i]


def weights_kernel(count, ext, feats, grads, buffer, columns, us, vs):
    spread_columns(ext[0], ext[1], us, vs)

    def put(block, value):
        buffer[place(block * 3 * CH, 3 * CH), :] = value

    weight_gradients(count, us, vs, feats, grads, put, columns, True)


def total_weights_kernel(count, flags, previous, ext, feats, grads, keep, send, columns, us, vs, total):
    spread_columns(ext[0], ext[1], us, vs)
    half = keep.shape[0]

    def put(block, value):
        at = slice(block * 3 * CH, (block + 1) * 3 * CH)
        total[at, :] = value + previous[at, :]

    if 2 * half > BUFFER:
        total[BUFFER:, :] = jnp.zeros((2 * half - BUFFER, N), f32)
    weight_gradients(count, us, vs, feats, grads, put, columns, False)
    for low in range(0, half, 3 * CH):
        high = min(low + 3 * CH, half)
        a, b = total[low:high, :], total[half + low : half + high, :]
        keep[low:high, :] = chosen(flags[STEPS], a, b).astype(bf16)
        send[low:high, :] = chosen(flags[STEPS], b, a).astype(bf16)


def exchanged(flags, blocks):
    for bit in range(len(blocks).bit_length() - 1):
        flag = flags[STEPS + 1 + bit]
        blocks = [chosen(flag, blocks[i ^ (1 << bit)], x) for i, x in enumerate(blocks)]
    return blocks


def halves_kernel(flags, keep, received, *out):
    rows_each = out[0].shape[0]
    blocks = []
    for i in range(len(out)):
        at = slice(i * rows_each, (i + 1) * rows_each)
        blocks.append(keep[at, :].astype(f32) + received[at, :].astype(f32))
    for ref, x in zip(out, exchanged(flags, blocks)):
        ref[...] = x.astype(bf16)


def arrange_kernel(flags, *refs):
    *blocks, out = refs
    rows_each = blocks[0].shape[0]
    for i, x in enumerate(exchanged(flags, [x[...].astype(f32) for x in blocks])):
        out[i * rows_each : (i + 1) * rows_each, :] = x.astype(bf16)


def unpack_kernel(flags, mine, other, first, first_bias, middle, middle_bias, last, last_bias):
    half = mine.shape[0]

    def block(b):
        lines = []
        for low, high, a, c in ((0, half, mine, other), (half, 2 * half, other, mine)):
            start, stop = max(b * 3 * CH, low), min((b + 1) * 3 * CH, high)
            if start < stop:
                at = slice(start - low, stop - low)
                lines.append(chosen(flags[STEPS], a[at, :].astype(f32), c[at, :].astype(f32)))
        return lines[0] if len(lines) == 1 else jnp.concatenate(lines, axis=0)

    for pair in range(3):
        wide = jnp.concatenate([block(3 * pair + q) for q in range(3)], axis=1)
        for side in range(2):
            m = 2 * pair + side
            for a in range(3):
                at = (3 * side + a) * CH
                part = wide[:, at : at + CH]
                for e in range(3):
                    value = part[e * CH : (e + 1) * CH]
                    if m < LAYERS - 1:
                        middle[m, 3 * a + e] = value
                    else:
                        last[3 * a + e] = value
    rest = block(9)
    turned = [rest[e * CH : (e + 1) * CH].T for e in range(3)]
    for a in range(3):
        for e in range(3):
            for ch in range(2):
                low, high = 4 * ch + a, 16 + 4 * ch + a + 1
                first[3 * a + e, ch : ch + 1, :] = turned[e][low : low + 1] + turned[e][high : high + 1]
    turned = turned[0]
    first_bias[...] = turned[32]
    middle_bias[...] = turned[33 : 33 + LAYERS - 1]
    last_bias[...] = turned[32 + LAYERS]


VMEM = pl.BlockSpec(memory_space=pltpu.VMEM)
SMEM = pl.BlockSpec(memory_space=pltpu.SMEM)
PARAMS = pltpu.CompilerParams(vmem_limit_bytes=VMEM_BYTES)


def array(dtype, *shape):
    return jax.ShapeDtypeStruct(shape, dtype)


def cost(flops, moved):
    return pl.CostEstimate(flops=flops, bytes_accessed=moved, transcendentals=0)


def field(count, *lead):
    return pltpu.VMEM(lead + (count, N), f32)


def feature_array(count):
    return array(bf16, LAYERS * (count + 24) * CH, N)


def gradient_array(count, slots):
    return array(bf16, slots * (count + 16) * CH, N)


def call(kernel, name, flops, inputs, out, scratch=()):
    return pl.pallas_call(
        kernel,
        in_specs=[VMEM] * len(inputs),
        out_specs=jax.tree.map(lambda _: VMEM, out),
        out_shape=out,
        scratch_shapes=list(scratch),
        compiler_params=PARAMS,
        cost_estimate=cost(flops, 10**6),
        name=name,
    )(*inputs)


def run_prepare(core, group, lengths, vel, cot, params, bits):
    rc = vel.shape[2]
    out = [
        array(f32, 2, 2, rc, N),
        array(bf16, 6 * CH, 16),
        array(bf16, LAYERS, 6 * CH, 4 * CH),
        array(bf16, 16, 4 * CH),
        array(bf16, LAYERS, 6 * CH, 4 * CH),
        array(f32, LAYERS + 1, CH, N),
        array(bf16, 3 * N, N),
        array(bf16, N, 3 * N),
        array(f32, N, N),
        array(f32, STEPS + 1 + bits, 8, N),
    ]
    inputs = [vel, cot, *params, jnp.asarray(poisson_tables(N))]
    inputs = [pltpu.with_memory_space_constraint(x, pltpu.HBM) for x in inputs]
    return pl.pallas_call(
        prepare_kernel,
        in_specs=[SMEM] * 3 + [pl.BlockSpec(memory_space=pltpu.HBM)] * len(inputs),
        out_specs=[VMEM] * len(out),
        out_shape=out,
        scratch_shapes=[pltpu.VMEM(x.shape, x.dtype) for x in inputs]
        + [pltpu.SemaphoreType.DMA((len(inputs),))],
        compiler_params=PARAMS,
        cost_estimate=cost(10**9, 10**6),
        name="prepare",
    )(core, group, lengths, *inputs)


def run_assemble(count, flags, fields):
    out = [array(f32, 2, count + 2 * MARGIN, N), array(f32, 2, count, N)]
    return call(assemble_kernel, "assemble", 10**6, [flags, *fields], out)


def run_network(count, vel, extra, weights):
    local_rows, mid = count + 2 * MARGIN, count + 2 * MID
    out = [array(f32, 4, count, N), array(f32, 4, mid, N), array(f32, mid * CH, N)]
    out += [feature_array(count), gradient_array(count, LAYERS)]
    scratch = [field(local_rows, 4), field(local_rows, 4)]
    return call(functools.partial(network_kernel, count), "network", 4 * 10**9, [vel, extra, *weights], out, scratch)


def run_project(count, steps, flags, gathered, vel, tables, last=False):
    local_rows = count + 2 * MARGIN
    out = [array(f32, 2, local_rows, N), array(f32, 4, count, N)]
    if not last:
        out.append(array(f32, 2, local_rows, N))
    kernel = functools.partial(project_kernel, count, len(gathered), steps)
    return call(kernel, "project", 10**9, [flags, *gathered, vel, *tables], out)


def run_back(count, ext, gstar, b_first, b_hidden, slopes, raw=None):
    local_rows, mid = count + 2 * MARGIN, count + 2 * MID
    inputs = [ext, gstar, b_first, b_hidden, slopes]
    out = [gradient_array(count, LAYERS + 1), array(f32, 2, count, N)]
    if raw is not None:
        inputs.append(raw)
        out.append(array(f32, 2, 4, mid, N))
    scratch = [field(local_rows, 4), field(local_rows, 4), field(8 * CH), field(mid, 4)]
    return call(functools.partial(back_kernel, count), "back", 4 * 10**9, inputs, out, scratch)


def run_finish(count, front, base, ext, gstar, interp, gvel, raw=None, lines=None):
    mid = count + 2 * MID
    inputs = [front, base, ext, gstar, interp, gvel, lines if raw is None else raw]
    scratch = [] if raw is None else [field(mid, 2, 4), field(mid, 4)]
    return call(functools.partial(finish_kernel, count), "finish", 10**9, inputs, array(f32, 4, count, N), scratch)


def run_weights(count, ext, feats, grads):
    scratch = [field(CH)] + [field(count + 2 * MARGIN, 4)] * 2
    kernel = functools.partial(weights_kernel, count)
    return call(kernel, "weights", 3 * 10**9, [ext, feats, grads], array(f32, BUFFER, N), scratch)


def run_total_weights(count, half, flags, previous, ext, feats, grads):
    scratch = [field(CH)] + [field(count + 2 * MARGIN, 4)] * 2 + [field(2 * half)]
    inputs = [flags, previous, ext, feats, grads]
    kernel = functools.partial(total_weights_kernel, count)
    return call(kernel, "total_weights", 3 * 10**9, inputs, [array(bf16, half, N)] * 2, scratch)


def run_halves(flags, keep, received, parts):
    out = [array(bf16, keep.shape[0] // parts, N)] * parts
    return call(halves_kernel, "halves", 10**6, [flags, keep, received], out)


def run_arrange(flags, blocks):
    out = array(bf16, len(blocks) * blocks[0].shape[0], N)
    return call(arrange_kernel, "arrange", 10**6, [flags, *blocks], out)


def run_unpack(flags, mine, other):
    out = [
        array(f32, 9, 2, CH),
        array(f32, CH),
        array(f32, LAYERS - 1, 9, CH, CH),
        array(f32, LAYERS - 1, CH),
        array(f32, 9, CH, CH),
        array(f32, CH),
    ]
    return call(unpack_kernel, "unpack", 10**7, [flags, mine, other], out)


def swap(x, axis, offset):
    count = lax.axis_size(axis)
    return lax.ppermute(x, axis, [(i, i ^ offset) for i in range(count)])


def from_group(x, ahead):
    count = lax.axis_size("strip")
    return lax.ppermute(x, "strip", [(i, (i - 2 * ahead) % count) for i in range(count)])


def gather_groups(x):
    return [x] + [from_group(x, k) for k in range(1, lax.axis_size("strip") // 2)]


def margins(velocity, partner, core):
    count = lax.axis_size("strip")
    if velocity.shape[2] < MARGIN:
        upper = core[0] == 0
        pair = jnp.where(
            upper,
            jnp.concatenate([velocity[0], partner[0]], axis=1),
            jnp.concatenate([partner[1], velocity[1]], axis=1),
        )
        above, below = from_group(pair[:, -MARGIN:], -1), from_group(pair[:, :MARGIN], 1)
        return jnp.stack([above, below]), jnp.stack([below, above])
    cross = [(i, (i - 1) % count if i % 2 == 0 else (i + 1) % count) for i in range(count)]
    same = [(i, (i - 2) % count if i % 2 == 0 else (i + 2) % count) for i in range(count)]
    return lax.ppermute(velocity, "strip", cross), lax.ppermute(velocity, "strip", same)


def sum_everywhere(keep, send, flags):
    parts = lax.axis_size("traj")
    groups = lax.axis_size("strip") // 2
    blocks = run_halves(flags, keep, swap(send, "strip", 1), parts)
    total = blocks[0].astype(f32)
    for k in range(1, parts):
        total = total + swap(blocks[k], "traj", k).astype(f32)
    x = total.astype(bf16)
    total = x.astype(f32)
    for k in range(1, groups):
        total = total + swap(x, "strip", 2 * k).astype(f32)
    x = total.astype(bf16)
    x = run_arrange(flags, [x] + [swap(x, "traj", k) for k in range(1, parts)])
    return x, swap(x, "strip", 1)


def per_device(
    velocity, lengths, cotangent, first_kernel, first_bias, middle_kernels, middle_biases, last_kernel, last_bias
):
    rc = velocity.shape[2]
    count = 2 * rc
    index = lax.axis_index("strip") & 1
    core = index[None]
    pick = lambda y, i: lax.dynamic_index_in_dim(y, i, 0, False)

    partner = swap(velocity, "strip", 1)
    cross, same = margins(velocity, partner, core)
    cot_partner = swap(cotangent, "strip", 1)
    first_kernel = first_kernel.transpose(0, 2, 1)
    params = (first_kernel, first_bias, middle_kernels, middle_biases, last_kernel, last_bias)
    parts = lax.axis_size("traj")
    half = -(-BUFFER // (2 * parts * 16)) * parts * 16
    group = lax.axis_index("traj")[None]
    own, w_first, w_hidden, b_first, b_hidden, bias, *tables, flags = run_prepare(
        core, group, lengths, velocity, cotangent, params, parts.bit_length() - 1
    )
    weights = (w_first, w_hidden, bias)

    v0, cot = run_assemble(count, flags, (own, partner, cross, same, cot_partner))
    block, interp0, raw0, feats0, slopes0 = run_network(count, v0, cot, weights)
    gathered = gather_groups(block)
    gstar1, base, v1 = run_project(count, (0, 1), flags, gathered, v0, tables)
    block, interp1, raw1, feats1, slopes1 = run_network(count, v1, cot, weights)
    grads1, gvel, lines = run_back(count, v1, gstar1, b_first, b_hidden, slopes1, raw1)
    block = run_finish(count, block, base, v1, gstar1, interp1, gvel, lines=lines)
    gathered = gather_groups(block)
    buffer = run_weights(count, v1, feats1, grads1)
    gstar0, base = run_project(count, (1, 0), flags, gathered, v1, tables, last=True)
    grads0, gvel = run_back(count, v0, gstar0, b_first, b_hidden, slopes0)
    keep, send = run_total_weights(count, half, flags, buffer, v0, feats0, grads0)
    out = run_finish(count, base, base, v0, gstar0, interp0, gvel, raw=raw0)

    strips = out.reshape(4, 2, rc, N).transpose(1, 0, 2, 3)
    mine, other = pick(strips, index)[None], swap(pick(strips, 1 - index), "strip", 1)[None]
    out = jnp.where(
        index == 0, jnp.concatenate([mine, other], axis=0), jnp.concatenate([other, mine], axis=0)
    )
    mine, other = sum_everywhere(keep, send, flags)
    first, *rest = run_unpack(flags, mine, other)
    return (out[:, :2], out[:, 2:], first.transpose(0, 2, 1), *rest)


def solution(mesh):
    band = P("traj", None, "strip", None)
    return jax.shard_map(
        per_device,
        mesh=mesh,
        in_specs=(band, P("traj"), band) + (P(),) * 6,
        out_specs=(band, band) + (P(),) * 6,
        check_vma=False,
    )
```

```python
import functools
import math

import jax
import jax.numpy as jnp
import numpy as np
from jax import lax
from jax.experimental import pallas as pl
from jax.experimental.pallas import tpu as pltpu
from jax.sharding import PartitionSpec as P

STEPS = 2
DT = 0.25
MARGIN = 16
MID = 8
LAG = 3
RAW = 2
CH = 64
LAYERS = 6
N = 128
BUFFER = 30 * CH
bf16 = jnp.bfloat16
f32 = jnp.float32
NT = (((1,), (1,)), ((), ()))
VMEM_BYTES = 14 * 2**20


def reach(layer):
    return 12 - layer


def place(start, size):
    return slice(start, start + size) if isinstance(start, int) else pl.ds(pl.multiple_of(start, CH), size)


def feature_rows(count, layer, r, rows=1):
    return place(((layer - 1) * (count + 24) + r + 12) * CH, rows * CH)


def gradient_rows(count, layer, r, rows=1):
    return place(((layer - 1) * (count + 16) + r + 8) * CH, rows * CH)


def lanes(x, s):
    return x if s == 0 else pltpu.roll(x, (-s) % x.shape[1], 1)


def rows(x, s):
    return x if s == 0 else pltpu.roll(x, (-s) % x.shape[0], 0)


TARGETS = ((0.0, -0.5), (-0.5, 0.0), (0.0, -0.5), (-0.5, 0.0))
POINTS = np.arange(16)
PX, PY = POINTS % 4 - 1.5, POINTS // 4 - 1.5
TAKEN = 5.0 + 4.0 * (PX[:, None] * PX[None, :] + PY[:, None] * PY[None, :])
PUT = [5.0 + 4.0 * (tx * PX + ty * PY) for tx, ty in TARGETS]


def constant_tables(length):
    k = np.arange(length)
    angle = 2.0 * math.pi * ((k[:, None] * k[None, :]) % length) / length
    table = (np.cos(angle) + np.sin(angle)) / math.sqrt(length)
    eigen = 2.0 - 2.0 * np.cos(2.0 * math.pi * k / length)
    total = eigen[:, None] + eigen[None, :]
    total[0, 0] = 1.0
    weight = 1.0 / total
    weight[0, 0] = 0.0
    small = np.zeros((length, length))
    for part in range(2):
        for which in range(2):
            cols = slice(32 * which + 16 * part, 32 * which + 16 * part + 16)
            small[16 * which : 16 * which + 16, cols] = TAKEN
            small[32 + 2 * which, cols] = PUT[2 * which]
            small[33 + 2 * which, cols] = PUT[2 * which + 1]
        for i in range(8):
            small[64 + i, 64 * part + 8 * i : 64 * part + 8 * i + 8] = 1.0
    return np.stack([table, weight, small]).astype(np.float32)


def split(x):
    high = x.astype(bf16)
    return high, (x - high.astype(f32)).astype(bf16)


def times_right(x, right):
    high, low = split(x)
    return jnp.dot(jnp.concatenate([high, low, high], axis=1), right[...], preferred_element_type=f32)


def times_left(x, left):
    high, low = split(x)
    return jnp.dot(left[...], jnp.concatenate([high, high, low], axis=0), preferred_element_type=f32)


def project(fields, right, left, weight):
    count = len(fields)
    source = [u - lanes(u, -1) + (v - rows(v, -1)) for u, v in fields]
    x = times_right(jnp.concatenate(source, axis=0), right)
    x = jnp.concatenate([x[i * N : (i + 1) * N] for i in range(count)], axis=1)
    x = times_left(x, left) * jnp.concatenate([weight[...]] * count, axis=1)
    x = times_left(x, left)
    x = jnp.concatenate([x[:, i * N : (i + 1) * N] for i in range(count)], axis=0)
    x = times_right(x, right)
    out = []
    for i, (u, v) in enumerate(fields):
        p = -x[i * N : (i + 1) * N]
        out.append((u - (lanes(p, 1) - p), v - (rows(p, 1) - p)))
    return out


def local(x, count):
    return jnp.concatenate([x[N - MARGIN :], x[: count + MARGIN]], axis=0)


def fold(o):
    third = o.shape[0] // 3
    return lanes(o[:third], -1) + o[third : 2 * third] + lanes(o[2 * third :], 1)


def fold_rounded(o):
    third = o.shape[0] // 3
    left, right = lanes(o[:third].astype(bf16), -1), lanes(o[2 * third :].astype(bf16), 1)
    return left.astype(f32) + o[third : 2 * third] + right.astype(f32)


def conv_rows(window, kernel, low, high, emit, between=lambda: None):
    starts = list(range(low, high, 2))
    for k in range(0, len(starts), 2):
        group = starts[k : k + 2]
        o = jnp.dot(
            kernel[...],
            jnp.concatenate([window(r) for r in group], axis=1),
            preferred_element_type=f32,
        )
        half = o.shape[0] // 2
        for i, r in enumerate(group):
            part = o[:, i * N : (i + 1) * N]
            emit(r, part[:half])
            emit(r + 1, part[half:])
        between()


def first_window(fields, r):
    a = 4 * (r - 1 + MARGIN)
    return jnp.concatenate([fields[0, a : a + 16, :], fields[1, a : a + 16, :]], axis=0).astype(bf16)


def feature_window(feats, count, layer):
    return lambda r: feats[feature_rows(count, layer, r - 1, 4), :]


def gradient_window(grads, count, layer):
    return lambda r: grads[gradient_rows(count, layer, r - 1, 4), :]


def gelu_value(z):
    c = math.sqrt(2.0 / math.pi)
    zz = z * z
    h = 0.5 + 0.5 * jnp.tanh(z * (c + (c * 0.044715) * zz))
    return z * h, h, zz


def gelu_slope(f, h, zz):
    c = math.sqrt(2.0 / math.pi)
    return h + (f - f * h) * (2.0 * c + (6.0 * c * 0.044715) * zz)


def network_forward(count, fields, w_first, w_hidden, bias, feats, slopes, raw, raw_done):
    for m in range(1, LAYERS + 1):

        def emit(r, o, m=m):
            value, h, zz = gelu_value((o if m == 1 else fold(o)) + bias[m - 1])
            feats[feature_rows(count, m, r), :] = value.astype(bf16)
            if -m <= r < count + m:
                slopes[gradient_rows(count, m, r), :] = gelu_slope(value, h, zz).astype(bf16)

        low, high = -reach(m), count + reach(m)
        if m == 1:
            conv_rows(functools.partial(first_window, fields), w_first, low, high, emit)
        else:
            conv_rows(feature_window(feats, count, m - 1), w_hidden.at[m - 2], low, high, emit)

    def emit_raw(r, o):
        value = fold(o) + bias[LAYERS]
        raw[(r + MID) * CH : (r + MID + 1) * CH, :] = value
        raw_done(r, value)

    conv_rows(
        feature_window(feats, count, LAYERS), w_hidden.at[LAYERS - 1], -RAW, count + RAW, emit_raw
    )


def interleave(vel, fields):
    for which in range(2):
        x = vel[which]
        for j in range(4):
            fields[which, pl.ds(j, x.shape[0], stride=4), :] = lanes(x, j - 1)


def mixed(pairs, mix):
    cols = []
    for u, v in pairs:
        cols.append(jnp.concatenate([*split(u), *split(v)], axis=0))
    o = jnp.dot(mix[...], jnp.concatenate(cols, axis=1), preferred_element_type=f32)
    return [o[:, i * N : (i + 1) * N] * (1.0 / 80.0) for i in range(len(pairs))]


def clear_patches(count, fields, mix, clear, put):
    for r in range(-MID, count + MID, 2):
        pairs = []
        for k in range(2):
            a = 4 * (r + k - 1 + MARGIN)
            pairs.append((fields[0, a : a + 16, :], fields[1, a : a + 16, :]))
        parts = mixed(pairs, mix)
        for k, ((u, v), o) in enumerate(zip(pairs, parts)):
            a = 32 * (r + k + MID)
            clear[a : a + 16, :] = u - o[0:16]
            clear[a + 16 : a + 32, :] = v - o[16:32]
        a = 4 * (r + MID)
        put[a : a + 8, :] = jnp.concatenate([parts[0][32:36], parts[1][32:36]], axis=0)


def point_sums(r, value, clear):
    a = 32 * (r + MID)
    out = []
    for k in range(4):
        b = a + 16 * (k // 2)
        x = value[16 * k : 16 * k + 16] * clear[b : b + 16, :]
        out.append(x[:8] + x[8:])
    return out


def interpolate(r, sums, adder, put, interp):
    cols = []
    for i in range(0, len(sums), 2):
        high, low = split(jnp.concatenate(sums[i] + sums[i + 1], axis=0))
        cols.append(jnp.concatenate([high, low], axis=0))
    o = jnp.dot(adder[...], jnp.concatenate(cols, axis=1), preferred_element_type=f32)
    for i in range(len(cols)):
        a = 4 * (r + 2 * i + MID)
        interp[a : a + 8, :] = o[0:8, i * N : (i + 1) * N] + put[a : a + 8, :]


def by_kind(interp, k, mid):
    return interp[pl.ds(k, mid, stride=4), :]


def raw_gradient(count, clear, ginterp, grads):
    for r in range(-MID, count + MID):
        a = 32 * (r + MID)
        parts = []
        for k in range(4):
            b = a + 16 * (k // 2)
            parts.append(clear[b : b + 16, :] * ginterp[k, r + MID : r + MID + 1, :])
        grads[gradient_rows(count, LAYERS + 1, r), :] = jnp.concatenate(parts, axis=0).astype(bf16)


def put_columns():
    point = lax.broadcasted_iota(jnp.int32, (16, N), 0)
    px, py = (point & 3).astype(f32) - 1.5, (point >> 2).astype(f32) - 1.5
    return [(1.0 / 16.0) + (tx / 20.0) * px + (ty / 20.0) * py for tx, ty in TARGETS]


def spread_back(r, at, columns, mix, raw, ginterp, spread):
    pairs, gs = [], []
    for k in range(2):
        z = raw[at((r + k + MID) * CH, CH), :]
        g = [ginterp[i, at(r + k + MID, 1), :] for i in range(4)]
        x = [z[16 * i : 16 * i + 16] * g[i] for i in range(4)]
        pairs.append((x[0] + x[1], x[2] + x[3]))
        gs.append(g)
    parts = mixed(pairs, mix)
    for which in range(2):
        out = []
        for pair, o, g in zip(pairs, parts, gs):
            back = columns[2 * which] * g[2 * which] + columns[2 * which + 1] * g[2 * which + 1]
            out.append(pair[which] - o[16 * which : 16 * which + 16] + back)
        for i in range(4):
            spread[which, i, at(4 * (r + MID), 8), :] = jnp.concatenate(
                [x[4 * i : 4 * i + 4] for x in out], axis=0
            )


def gathered_back(count, spread, lines):
    out = []
    for which in range(2):
        for r in range(0, count, 2):
            total = None
            for i in range(4):
                a = 4 * (r + 1 - i + MID)
                x = spread[which, i, a : a + 8, :]
                total = x if total is None else total + x
            lines[which, 4 * r : 4 * r + 8, :] = total
        total = None
        for j in range(4):
            x = lanes(lines[which, pl.ds(j, count, stride=4), :], 1 - j)
            total = x if total is None else total + x
        out.append(total)
    return out


def carriers(u, v):
    return (
        0.5 * (u + lanes(u, 1)),
        0.5 * (v + lanes(v, 1)),
        0.5 * (u + rows(u, 1)),
        0.5 * (v + rows(v, 1)),
    )


def middle(x, count):
    return x[MARGIN - MID : MARGIN + MID + count]


def provisional(count, u, v, interp):
    mid = count + 2 * MID
    flux = [middle(x, count) * by_kind(interp, k, mid) for k, x in enumerate(carriers(u, v))]
    u, v = middle(u, count), middle(v, count)
    su = u - DT * (flux[0] - lanes(flux[0], -1) + (flux[1] - rows(flux[1], -1)))
    sv = v - DT * (flux[2] - lanes(flux[2], -1) + (flux[3] - rows(flux[3], -1)))
    return su[MID : MID + count], sv[MID : MID + count]


def flux_gradients(count, gu, gv):
    return [
        middle(x, count) * (-DT)
        for x in (gu - lanes(gu, 1), gu - rows(gu, 1), gv - lanes(gv, 1), gv - rows(gv, 1))
    ]


def interp_gradients(count, gu, gv, u, v, ginterp):
    for k, (g, x) in enumerate(zip(flux_gradients(count, gu, gv), carriers(u, v))):
        ginterp[k] = g * middle(x, count)


def velocity_gradients(count, gu, gv, interp, spread, lines):
    mid = count + 2 * MID
    half = [0.5 * g * by_kind(interp, k, mid) for k, g in enumerate(flux_gradients(count, gu, gv))]
    shares = gathered_back(count, spread, lines)
    out = []
    for which, g in enumerate((gu, gv)):
        along, across = half[which], half[2 + which]
        x = middle(g, count) + (along + lanes(along, -1)) + (across + rows(across, -1))
        out.append(x[MID : MID + count] + shares[which])
    return out


def network_backward(count, w_hidden, slopes, grads, between=lambda: None):
    for m in range(LAYERS, 0, -1):

        def emit(r, o, m=m):
            at = gradient_rows(count, m, r)
            grads[at, :] = (fold_rounded(o) * slopes[at, :].astype(f32)).astype(bf16)

        conv_rows(gradient_window(grads, count, m + 1), w_hidden.at[m - 1], -m, count + m, emit, between)


def input_gradient(count, w_first, grads, gvel):
    window = gradient_window(grads, count, 1)
    starts = list(range(0, count, 2))
    for k in range(0, len(starts), 2):
        group = starts[k : k + 2]
        o = jnp.dot(
            w_first[...],
            jnp.concatenate([window(r) for r in group], axis=1),
            preferred_element_type=f32,
        )
        for i, r in enumerate(group):
            part = o[:, i * N : (i + 1) * N]
            both = lanes(part, -1)[0:4] + part[4:8] + lanes(part, 1)[8:12]
            gvel[0, r : r + 2, :] = both[0:2]
            gvel[1, r : r + 2, :] = both[2:4]


def folded(x):
    return x[: 3 * CH, : 3 * CH] + x[3 * CH :, CH:]


def weight_product(count, m, fields, feats, grads):
    starts = list(range(0, count, 2))
    shifts = (0,) if isinstance(m, int) and m == 1 else (-1, 0, 1)
    left, total = [], None
    for r in starts:
        g = [grads[gradient_rows(count, m, r + k), :] for k in range(2)]
        left.append(jnp.concatenate([lanes(x, -e) for x in g for e in shifts], axis=0))
        for x in g:
            x = x.astype(f32)
            total = x if total is None else total + x
    if isinstance(m, int) and m == 1:
        right = [first_window(fields, r) for r in starts]
    else:
        right = [feature_window(feats, count, m - 1)(r) for r in starts]
    out = lax.dot_general(
        jnp.concatenate(left, axis=1), jnp.concatenate(right, axis=1), NT, preferred_element_type=f32
    )
    return out, jnp.sum(total, axis=1, keepdims=True)


def weight_gradients(count, fields, feats, grads, put, columns, loop):
    lane = lax.broadcasted_iota(jnp.int32, (CH, N), 1)

    def pair_of(pair):
        lower, a = weight_product(count, 2 + 2 * pair, fields, feats, grads)
        upper, b = weight_product(count, 3 + 2 * pair, fields, feats, grads)
        x = jnp.where(lane == 33 + 2 * pair, a, columns[...])
        columns[...] = jnp.where(lane == 34 + 2 * pair, b, x)
        wide = jnp.concatenate([folded(lower), folded(upper)], axis=1)
        for q in range(3):
            put(3 * pair + q, wide[:, q * N : (q + 1) * N])

    columns[...] = jnp.zeros((CH, N), f32)
    if loop:
        lax.fori_loop(0, 3, lambda pair, _: (pair_of(pair), 0)[1], 0)
    else:
        for pair in range(2, -1, -1):
            pair_of(pair)
    first, total = weight_product(count, 1, fields, feats, grads)
    rest = jnp.where(lane == 32, total, columns[...])
    first = jnp.concatenate([first, jnp.zeros((2 * CH, N - 32), f32)], axis=1)
    put(9, jnp.concatenate([first[:CH] + rest, first[CH:], jnp.zeros((CH, N), f32)], axis=0))


def fetch(sources, targets, sems):
    copies = [pltpu.make_async_copy(a, b, sems.at[i]) for i, (a, b) in enumerate(zip(sources, targets))]
    for copy in copies:
        copy.start()
    return copies


def tap_of(middle, last, m):
    return (lambda a, e: last[3 * a + e]) if m == LAYERS - 1 else (lambda a, e: middle[m, 3 * a + e])


def prepare_kernel(*refs):
    own, f_first, f_hidden, bias, mix, adder, flags = refs[10:17]
    vel, cot, first, first_bias, middle, middle_bias, last, last_bias, tables, lengths = refs[17:27]
    copies = fetch(refs[:10], refs[17:27], refs[27])
    core = lax.axis_index("strip") & 1
    group = lax.axis_index("traj")
    for copy in copies:
        copy.wait()
    for i in range(STEPS):
        flags[i] = jnp.full((8, N), jnp.where(lengths[core] > i, 1.0, 0.0), f32)
    flags[STEPS] = jnp.full((8, N), jnp.where(core == 0, 1.0, 0.0), f32)
    for bit in range(flags.shape[0] - STEPS - 1):
        flags[STEPS + 1 + bit] = jnp.full((8, N), jnp.where((group >> bit) & 1 == 1, 1.0, 0.0), f32)
    own[0] = jnp.where(core == 0, vel[0], vel[1])
    own[1] = jnp.where(core == 0, cot[0], cot[1])
    zero = jnp.zeros((CH, CH), bf16)
    for m in range(LAYERS):
        tap = tap_of(middle, last, m)
        for two in range(2):
            for e in range(3):
                taps = [tap(q - two, e) if 0 <= q - two < 3 else zero for q in range(4)]
                f_hidden[m, (two * 3 + e) * CH : (two * 3 + e + 1) * CH, :] = jnp.concatenate(taps, axis=1)
    for two in range(2):
        lines = []
        for ch in range(2):
            for i in range(4):
                for j in range(4):
                    if 0 <= i - two < 3 and j < 3:
                        lines.append(first[3 * (i - two) + j, ch : ch + 1, :].astype(f32))
                    else:
                        lines.append(jnp.zeros((1, CH), f32))
        f_first[two * CH : (two + 1) * CH, :] = jnp.concatenate(lines, axis=0).T.astype(bf16)
    for m in range(LAYERS + 1):
        if 0 < m < LAYERS:
            line = middle_bias[m - 1 : m, :]
        else:
            line = (first_bias if m == 0 else last_bias)[...].reshape(1, CH)
        bias[m] = jnp.broadcast_to(line, (N, CH)).T
    mix[...] = tables[2, 0:48, 0:64].astype(bf16)
    adder[...] = tables[2, 64:80, :].astype(bf16)


def prepare_back_kernel(*refs):
    b_first, b_hidden, right, left, weight = refs[5:10]
    first, middle, last, tables = refs[10:14]
    copies = fetch(refs[:4], refs[10:14], refs[14])
    for copy in copies:
        copy.wait()
    zero = jnp.zeros((CH, CH), bf16)
    for m in range(LAYERS):
        tap = tap_of(middle, last, m)
        for two in range(2):
            for e in range(3):
                taps = [tap(2 - q + two, 2 - e) if 0 <= q - two < 3 else zero for q in range(4)]
                b_hidden[m, (two * 3 + e) * CH : (two * 3 + e + 1) * CH, :] = jnp.concatenate(
                    [jnp.concatenate(taps[:2], axis=0).T, jnp.concatenate(taps[2:], axis=0).T], axis=1
                )
    lines = jnp.zeros((1, CH), f32)
    taps = []
    for e in range(3):
        for ch in range(2):
            for two in range(2):
                line = [
                    first[3 * (2 - q + two) + 2 - e, ch : ch + 1, :].astype(f32) if 0 <= q - two < 3 else lines
                    for q in range(4)
                ]
                taps.append(jnp.concatenate(line, axis=1))
    taps.append(jnp.zeros((4, 4 * CH), f32))
    b_first[...] = jnp.concatenate(taps, axis=0).astype(bf16)
    high, low = split(tables[0])
    right[...] = jnp.concatenate([high, high, low], axis=0)
    left[...] = jnp.concatenate([high, low, high], axis=1)
    weight[...] = tables[1]


def chosen(flag, x, y):
    flag = flag[0:1, :] > 0.5
    return jnp.where(jnp.broadcast_to(flag, x.shape), x, y)


def assemble_kernel(flags, own, partner, cross, same, cot_partner, ext, cot):
    upper = flags[STEPS]

    def pair(mine, other, i):
        other = chosen(upper, other[0, i], other[1, i])
        return [chosen(upper, mine[i], other), chosen(upper, other, mine[i])]

    for i in range(2):
        above = chosen(upper, cross[0, i], same[1, i])[-MARGIN:]
        below = chosen(upper, same[0, i], cross[1, i])[:MARGIN]
        ext[i] = jnp.concatenate([above, *pair(own[0], partner, i), below], axis=0)
        cot[i] = jnp.concatenate(pair(own[1], cot_partner, i), axis=0)


def network_kernel(
    count, vel, extra, w_first, w_hidden, bias, mix, adder, block, interp, raw, clear, fields, feats, slopes, put
):
    interleave(vel, fields)
    clear_patches(count, fields, mix, clear, put)
    sums = []

    def raw_done(r, value):
        sums.append(point_sums(r, value, clear))
        if len(sums) == 4 * LAG + 4:
            interpolate(r + 1 - len(sums), sums[:4], adder, put, interp)
            del sums[:4]

    network_forward(count, fields, w_first, w_hidden, bias, feats, slopes, raw, raw_done)
    for i in range(0, len(sums), 4):
        interpolate(count + RAW - len(sums) + i, sums[i : i + 4], adder, put, interp)
    su, sv = provisional(count, vel[0], vel[1], interp)
    block[0] = su
    block[1] = sv
    block[2] = extra[0]
    block[3] = extra[1]


def joined(gathered, i):
    return jnp.concatenate([g[i] for g in gathered], axis=0)


def project_kernel(count, blocks, steps, flags, *refs):
    gathered, refs = refs[:blocks], refs[blocks:]
    vel, right, left, weight, gstar, own, *ext = refs
    su, sv, cu, cv = [joined(gathered, i) for i in range(4)]
    mv, mg = [flags[step][0:1, :] for step in steps]
    news, grads = project([(su, sv), (mg * cu, mg * cv)], right, left, weight)
    for i in range(2):
        x = vel[i] + mv * (local(news[i], count) - vel[i])
        for ref in ext:
            ref[i] = x
        own[i] = x[MARGIN : MARGIN + count]
        gstar[i] = local(grads[i], count)
        own[2 + i] = (1.0 - mg) * gathered[0][2 + i]


def static(start, size):
    return slice(start, start + size)


def back_kernel(count, ext, gstar, clear, b_first, b_hidden, slopes, *refs):
    if len(refs) == 6:
        mix, raw, grads, gvel, spread, ginterp = refs
    else:
        grads, gvel, ginterp = refs
    interp_gradients(count, gstar[0], gstar[1], ext[0], ext[1], ginterp)
    raw_gradient(count, clear, ginterp, grads)
    tasks = []
    if len(refs) == 6:
        columns = put_columns()
        for r in range(-RAW, count + RAW, 2):
            tasks.append(functools.partial(spread_back, r, static, columns, mix, raw, ginterp, spread))
    turn = [0]

    def between():
        turn[0] += 1
        if tasks and turn[0] % 3 == 0:
            tasks.pop(0)()

    network_backward(count, b_hidden, slopes, grads, between)
    for task in tasks:
        task()
    input_gradient(count, b_first, grads, gvel)


def finish_kernel(count, front, base, ext, gstar, interp, gvel, *refs):
    gu, gv = gstar[0], gstar[1]
    if len(refs) == 3:
        spread, out, lines = refs
    else:
        mix, raw, out, lines, spread, ginterp = refs
        interp_gradients(count, gu, gv, ext[0], ext[1], ginterp)
        columns = put_columns()

        def at(start, size):
            return pl.ds(pl.multiple_of(start, size), size) if size > 1 else pl.ds(start, size)

        def step(i, _):
            for k in range(2):
                spread_back(4 * i + 2 * k - RAW, at, columns, mix, raw, ginterp, spread)
            return 0

        lax.fori_loop(0, (count + 2 * RAW) // 4, step, 0)
    change = velocity_gradients(count, gu, gv, interp, spread, lines)
    for i in range(2):
        out[i] = front[i]
        out[2 + i] = base[2 + i] + change[i] + gvel[i]


def weights_kernel(count, fields, feats, grads, buffer, columns):
    def put(block, value):
        buffer[place(block * 3 * CH, 3 * CH), :] = value

    weight_gradients(count, fields, feats, grads, put, columns, True)


def total_weights_kernel(count, flags, previous, fields, feats, grads, keep, send, columns, total):
    half = keep.shape[0]

    def put(block, value):
        at = slice(block * 3 * CH, (block + 1) * 3 * CH)
        total[at, :] = value + previous[at, :]

    if 2 * half > BUFFER:
        total[BUFFER:, :] = jnp.zeros((2 * half - BUFFER, N), f32)
    weight_gradients(count, fields, feats, grads, put, columns, False)
    for low in range(0, half, 3 * CH):
        high = min(low + 3 * CH, half)
        a, b = total[low:high, :], total[half + low : half + high, :]
        keep[low:high, :] = chosen(flags[STEPS], a, b).astype(bf16)
        send[low:high, :] = chosen(flags[STEPS], b, a).astype(bf16)


def exchanged(flags, blocks):
    for bit in range(len(blocks).bit_length() - 1):
        flag = flags[STEPS + 1 + bit]
        blocks = [chosen(flag, blocks[i ^ (1 << bit)], x) for i, x in enumerate(blocks)]
    return blocks


def halves_kernel(flags, keep, received, *out):
    rows_each = out[0].shape[0]
    blocks = []
    for i in range(len(out)):
        at = slice(i * rows_each, (i + 1) * rows_each)
        blocks.append(keep[at, :].astype(f32) + received[at, :].astype(f32))
    for ref, x in zip(out, exchanged(flags, blocks)):
        ref[...] = x.astype(bf16)


def arrange_kernel(flags, *refs):
    *blocks, out = refs
    rows_each = blocks[0].shape[0]
    for i, x in enumerate(exchanged(flags, [x[...].astype(f32) for x in blocks])):
        out[i * rows_each : (i + 1) * rows_each, :] = x.astype(bf16)


def unpack_kernel(flags, mine, other, first, first_bias, middle, middle_bias, last, last_bias):
    half = mine.shape[0]

    def block(b):
        lines = []
        for low, high, a, c in ((0, half, mine, other), (half, 2 * half, other, mine)):
            start, stop = max(b * 3 * CH, low), min((b + 1) * 3 * CH, high)
            if start < stop:
                at = slice(start - low, stop - low)
                lines.append(chosen(flags[STEPS], a[at, :].astype(f32), c[at, :].astype(f32)))
        return lines[0] if len(lines) == 1 else jnp.concatenate(lines, axis=0)

    for pair in range(3):
        wide = jnp.concatenate([block(3 * pair + q) for q in range(3)], axis=1)
        for side in range(2):
            m = 2 * pair + side
            for a in range(3):
                at = (3 * side + a) * CH
                part = wide[:, at : at + CH]
                for e in range(3):
                    value = part[e * CH : (e + 1) * CH]
                    if m < LAYERS - 1:
                        middle[m, 3 * a + e] = value
                    else:
                        last[3 * a + e] = value
    rest = block(9)
    turned = [rest[two * CH : (two + 1) * CH].T for two in range(2)]
    for a in range(3):
        for e in range(3):
            for ch in range(2):
                low, high = 16 * ch + 4 * a + e, 16 * ch + 4 * (a + 1) + e
                first[3 * a + e, ch : ch + 1, :] = turned[0][low : low + 1] + turned[1][high : high + 1]
    turned = turned[0]
    first_bias[...] = turned[32]
    middle_bias[...] = turned[33 : 33 + LAYERS - 1]
    last_bias[...] = turned[32 + LAYERS]


VMEM = pl.BlockSpec(memory_space=pltpu.VMEM)
SMEM = pl.BlockSpec(memory_space=pltpu.SMEM)
PARAMS = pltpu.CompilerParams(vmem_limit_bytes=VMEM_BYTES)


def array(dtype, *shape):
    return jax.ShapeDtypeStruct(shape, dtype)


def cost(flops, moved):
    return pl.CostEstimate(flops=flops, bytes_accessed=moved, transcendentals=0)


def field(count, *lead):
    return pltpu.VMEM(lead + (count, N), f32)


def feature_array(count):
    return array(bf16, LAYERS * (count + 24) * CH, N)


def gradient_array(count, slots):
    return array(bf16, slots * (count + 16) * CH, N)


def call(kernel, name, flops, inputs, out, scratch=()):
    return pl.pallas_call(
        kernel,
        in_specs=[VMEM] * len(inputs),
        out_specs=jax.tree.map(lambda _: VMEM, out),
        out_shape=out,
        scratch_shapes=list(scratch),
        compiler_params=PARAMS,
        cost_estimate=cost(flops, 10**6),
        name=name,
    )(*inputs)


def run_prepare(lengths, vel, cot, params, bits):
    out = [
        array(f32, 2, 2, vel.shape[2], N),
        array(bf16, 2 * CH, 32),
        array(bf16, LAYERS, 6 * CH, 4 * CH),
        array(f32, LAYERS + 1, CH, N),
        array(bf16, 48, 64),
        array(bf16, 16, N),
        array(f32, STEPS + 1 + bits, 8, N),
    ]
    inputs = [vel, cot, *params, jnp.asarray(constant_tables(N)), lengths]
    scratch = [pltpu.VMEM(x.shape, x.dtype) for x in inputs[:-1]] + [pltpu.SMEM(lengths.shape, lengths.dtype)]
    return call_from_hbm(prepare_kernel, "prepare", inputs, out, scratch)


def run_prepare_back(params, after):
    first, _, middle, _, last, _ = params
    out = [
        array(bf16, 16, 4 * CH),
        array(bf16, LAYERS, 6 * CH, 4 * CH),
        array(bf16, 3 * N, N),
        array(bf16, N, 3 * N),
        array(f32, N, N),
    ]
    inputs = [first, middle, last, jnp.asarray(constant_tables(N))]
    scratch = [pltpu.VMEM(x.shape, x.dtype) for x in inputs]
    b_first, b_hidden, *tables = call_from_hbm(prepare_back_kernel, "prepare_back", inputs, out, scratch, after)
    return b_first, b_hidden, tables


def call_from_hbm(kernel, name, inputs, out, scratch, *after):
    hbm = pl.BlockSpec(memory_space=pltpu.HBM)
    inputs = [pltpu.with_memory_space_constraint(x, pltpu.HBM) for x in inputs]
    return pl.pallas_call(
        kernel,
        in_specs=[hbm] * len(inputs) + [VMEM] * len(after),
        out_specs=[VMEM] * len(out),
        out_shape=out,
        scratch_shapes=scratch + [pltpu.SemaphoreType.DMA((len(inputs),))],
        compiler_params=PARAMS,
        cost_estimate=cost(10**9, 10**6),
        name=name,
    )(*inputs, *after)


def run_assemble(count, flags, fields):
    out = [array(f32, 2, count + 2 * MARGIN, N), array(f32, 2, count, N)]
    return call(assemble_kernel, "assemble", 10**6, [flags, *fields], out)


def run_network(count, vel, extra, weights):
    local_rows, mid = count + 2 * MARGIN, count + 2 * MID
    out = [array(f32, 4, count, N), array(f32, 4 * mid, N), array(f32, mid * CH, N), array(f32, mid * 32, N)]
    out += [array(f32, 2, 4 * local_rows, N)]
    out += [feature_array(count), gradient_array(count, LAYERS)]
    scratch = [field(4 * mid)]
    return call(functools.partial(network_kernel, count), "network", 4 * 10**9, [vel, extra, *weights], out, scratch)


def run_project(count, steps, flags, gathered, vel, tables, last=False):
    local_rows = count + 2 * MARGIN
    out = [array(f32, 2, local_rows, N), array(f32, 4, count, N)]
    if not last:
        out.append(array(f32, 2, local_rows, N))
    kernel = functools.partial(project_kernel, count, len(gathered), steps)
    return call(kernel, "project", 10**9, [flags, *gathered, vel, *tables], out)


def run_back(count, ext, gstar, clear, b_first, b_hidden, slopes, *more):
    mid = count + 2 * MID
    inputs = [ext, gstar, clear, b_first, b_hidden, slopes, *more]
    out = [gradient_array(count, LAYERS + 1), array(f32, 2, count, N)]
    if more:
        out.append(array(f32, 2, 4, 4 * mid, N))
    return call(functools.partial(back_kernel, count), "back", 4 * 10**9, inputs, out, [field(mid, 4)])


def run_finish(count, front, base, ext, gstar, interp, gvel, *more):
    mid = count + 2 * MID
    inputs = [front, base, ext, gstar, interp, gvel, *more]
    scratch = [field(4 * count, 2)]
    if len(more) > 1:
        scratch += [field(4 * mid, 2, 4), field(mid, 4)]
    return call(functools.partial(finish_kernel, count), "finish", 10**9, inputs, array(f32, 4, count, N), scratch)


def run_weights(count, fields, feats, grads):
    scratch = [field(CH)]
    kernel = functools.partial(weights_kernel, count)
    return call(kernel, "weights", 3 * 10**9, [fields, feats, grads], array(f32, BUFFER, N), scratch)


def run_total_weights(count, half, flags, previous, fields, feats, grads):
    scratch = [field(CH), field(2 * half)]
    inputs = [flags, previous, fields, feats, grads]
    kernel = functools.partial(total_weights_kernel, count)
    return call(kernel, "total_weights", 3 * 10**9, inputs, [array(bf16, half, N)] * 2, scratch)


def run_halves(flags, keep, received, parts):
    out = [array(bf16, keep.shape[0] // parts, N)] * parts
    return call(halves_kernel, "halves", 10**6, [flags, keep, received], out)


def run_arrange(flags, blocks):
    out = array(bf16, len(blocks) * blocks[0].shape[0], N)
    return call(arrange_kernel, "arrange", 10**6, [flags, *blocks], out)


def run_unpack(flags, mine, other):
    out = [
        array(f32, 9, 2, CH),
        array(f32, CH),
        array(f32, LAYERS - 1, 9, CH, CH),
        array(f32, LAYERS - 1, CH),
        array(f32, 9, CH, CH),
        array(f32, CH),
    ]
    return call(unpack_kernel, "unpack", 10**7, [flags, mine, other], out)


def swap(x, axis, offset):
    count = lax.axis_size(axis)
    return lax.ppermute(x, axis, [(i, i ^ offset) for i in range(count)])


def from_group(x, ahead):
    count = lax.axis_size("strip")
    return lax.ppermute(x, "strip", [(i, (i - 2 * ahead) % count) for i in range(count)])


def gather_groups(x):
    return [x] + [from_group(x, k) for k in range(1, lax.axis_size("strip") // 2)]


def margins(velocity, partner, core):
    count = lax.axis_size("strip")
    if velocity.shape[2] < MARGIN:
        upper = core[0] == 0
        pair = jnp.where(
            upper,
            jnp.concatenate([velocity[0], partner[0]], axis=1),
            jnp.concatenate([partner[1], velocity[1]], axis=1),
        )
        above, below = from_group(pair[:, -MARGIN:], -1), from_group(pair[:, :MARGIN], 1)
        return jnp.stack([above, below]), jnp.stack([below, above])
    cross = [(i, (i - 1) % count if i % 2 == 0 else (i + 1) % count) for i in range(count)]
    same = [(i, (i - 2) % count if i % 2 == 0 else (i + 2) % count) for i in range(count)]
    return lax.ppermute(velocity, "strip", cross), lax.ppermute(velocity, "strip", same)


def sum_everywhere(keep, send, flags):
    parts = lax.axis_size("traj")
    groups = lax.axis_size("strip") // 2
    blocks = run_halves(flags, keep, swap(send, "strip", 1), parts)
    total = blocks[0].astype(f32)
    for k in range(1, parts):
        total = total + swap(blocks[k], "traj", k).astype(f32)
    x = total.astype(bf16)
    total = x.astype(f32)
    for k in range(1, groups):
        total = total + swap(x, "strip", 2 * k).astype(f32)
    x = total.astype(bf16)
    x = run_arrange(flags, [x] + [swap(x, "traj", k) for k in range(1, parts)])
    return x, swap(x, "strip", 1)


def per_device(
    velocity, lengths, cotangent, first_kernel, first_bias, middle_kernels, middle_biases, last_kernel, last_bias
):
    rc = velocity.shape[2]
    count = 2 * rc
    index = lax.axis_index("strip") & 1
    core = index[None]
    pick = lambda y, i: lax.dynamic_index_in_dim(y, i, 0, False)

    partner = swap(velocity, "strip", 1)
    cross, same = margins(velocity, partner, core)
    cot_partner = swap(cotangent, "strip", 1)
    first_kernel = first_kernel.transpose(0, 2, 1)
    params = (first_kernel, first_bias, middle_kernels, middle_biases, last_kernel, last_bias)
    parts = lax.axis_size("traj")
    half = -(-BUFFER // (2 * parts * 16)) * parts * 16
    own, w_first, w_hidden, bias, mix, adder, flags = run_prepare(
        lengths, velocity, cotangent, params, parts.bit_length() - 1
    )
    weights = (w_first, w_hidden, bias, mix, adder)

    v0, cot = run_assemble(count, flags, (own, partner, cross, same, cot_partner))
    block, interp0, raw0, clear0, fields0, feats0, slopes0 = run_network(count, v0, cot, weights)
    gathered = gather_groups(block)
    b_first, b_hidden, tables = run_prepare_back(params, interp0)
    gstar1, base, v1 = run_project(count, (0, 1), flags, gathered, v0, tables)
    block, interp1, raw1, clear1, fields1, feats1, slopes1 = run_network(count, v1, cot, weights)
    grads1, gvel, spread = run_back(count, v1, gstar1, clear1, b_first, b_hidden, slopes1, mix, raw1)
    block = run_finish(count, block, base, v1, gstar1, interp1, gvel, spread)
    gathered = gather_groups(block)
    buffer = run_weights(count, fields1, feats1, grads1)
    gstar0, base = run_project(count, (1, 0), flags, gathered, v1, tables, last=True)
    grads0, gvel = run_back(count, v0, gstar0, clear0, b_first, b_hidden, slopes0)
    keep, send = run_total_weights(count, half, flags, buffer, fields0, feats0, grads0)
    out = run_finish(count, base, base, v0, gstar0, interp0, gvel, mix, raw0)

    strips = out.reshape(4, 2, rc, N).transpose(1, 0, 2, 3)
    mine, other = pick(strips, index)[None], swap(pick(strips, 1 - index), "strip", 1)[None]
    out = jnp.where(
        index == 0, jnp.concatenate([mine, other], axis=0), jnp.concatenate([other, mine], axis=0)
    )
    mine, other = sum_everywhere(keep, send, flags)
    first, *rest = run_unpack(flags, mine, other)
    return (out[:, :2], out[:, 2:], first.transpose(0, 2, 1), *rest)


def solution(mesh):
    band = P("traj", None, "strip", None)
    return jax.shard_map(
        per_device,
        mesh=mesh,
        in_specs=(band, P("traj"), band) + (P(),) * 6,
        out_specs=(band, band) + (P(),) * 6,
        check_vma=False,
    )
```

```python
import functools
import math

import jax
import jax.numpy as jnp
import numpy as np
from jax import lax
from jax.experimental import pallas as pl
from jax.experimental.pallas import tpu as pltpu
from jax.sharding import PartitionSpec as P

STEPS = 2
DT = 0.25
MARGIN = 16
MID = 8
LAG = 3
RAW = 2
CH = 64
LAYERS = 6
N = 128
HALF = 15 * CH
bf16 = jnp.bfloat16
f32 = jnp.float32
NT = (((1,), (1,)), ((), ()))
VMEM_BYTES = 14 * 2**20


def reach(layer):
    return 12 - layer


def place(start, size):
    return slice(start, start + size) if isinstance(start, int) else pl.ds(pl.multiple_of(start, CH), size)


def feature_rows(count, layer, r, rows=1):
    return place(((layer - 1) * (count + 24) + r + 12) * CH, rows * CH)


def gradient_rows(count, layer, r, rows=1):
    return place(((layer - 1) * (count + 16) + r + 8) * CH, rows * CH)


def lanes(x, s):
    return x if s == 0 else pltpu.roll(x, (-s) % x.shape[1], 1)


def rows(x, s):
    return x if s == 0 else pltpu.roll(x, (-s) % x.shape[0], 0)


TARGETS = ((0.0, -0.5), (-0.5, 0.0), (0.0, -0.5), (-0.5, 0.0))
POINTS = np.arange(16)
PX, PY = POINTS % 4 - 1.5, POINTS // 4 - 1.5
TAKEN = 5.0 + 4.0 * (PX[:, None] * PX[None, :] + PY[:, None] * PY[None, :])
PUT = [5.0 + 4.0 * (tx * PX + ty * PY) for tx, ty in TARGETS]


def constant_tables(length):
    k = np.arange(length)
    angle = 2.0 * math.pi * ((k[:, None] * k[None, :]) % length) / length
    table = (np.cos(angle) + np.sin(angle)) / math.sqrt(length)
    eigen = 2.0 - 2.0 * np.cos(2.0 * math.pi * k / length)
    total = eigen[:, None] + eigen[None, :]
    total[0, 0] = 1.0
    weight = 1.0 / total
    weight[0, 0] = 0.0
    small = np.zeros((length, length))
    for part in range(2):
        for which in range(2):
            cols = slice(32 * which + 16 * part, 32 * which + 16 * part + 16)
            small[16 * which : 16 * which + 16, cols] = TAKEN
            small[32 + 2 * which, cols] = PUT[2 * which]
            small[33 + 2 * which, cols] = PUT[2 * which + 1]
        for i in range(8):
            small[64 + i, 64 * part + 8 * i : 64 * part + 8 * i + 8] = 1.0
    return np.stack([table, weight, small]).astype(np.float32)


def split(x):
    high = x.astype(bf16)
    return high, (x - high.astype(f32)).astype(bf16)


def times_right(x, right):
    high, low = split(x)
    return jnp.dot(jnp.concatenate([high, low, high], axis=1), right[...], preferred_element_type=f32)


def times_left(x, left):
    high, low = split(x)
    return jnp.dot(left[...], jnp.concatenate([high, high, low], axis=0), preferred_element_type=f32)


def local(x, count):
    return jnp.concatenate([x[N - MARGIN :], x[: count + MARGIN]], axis=0)


def project(fields, count, right, left, weight):
    number = len(fields)
    source = [u - lanes(u, -1) + (v - rows(v, -1)) for u, v in fields]
    x = times_right(jnp.concatenate(source, axis=0), right)
    x = jnp.concatenate([x[i * N : (i + 1) * N] for i in range(number)], axis=1)
    x = times_left(x, left) * jnp.concatenate([weight[...]] * number, axis=1)
    x = local(times_left(x, left), count)
    size = x.shape[0]
    x = times_right(jnp.concatenate([x[:, i * N : (i + 1) * N] for i in range(number)], axis=0), right)
    out = []
    for i, (u, v) in enumerate(fields):
        p = -x[i * size : (i + 1) * size]
        out.append((local(u, count) - (lanes(p, 1) - p), local(v, count) - (rows(p, 1) - p)))
    return out


def fold(o):
    third = o.shape[0] // 3
    return lanes(o[:third], -1) + o[third : 2 * third] + lanes(o[2 * third :], 1)


def fold_rounded(o):
    third = o.shape[0] // 3
    left, right = lanes(o[:third].astype(bf16), -1), lanes(o[2 * third :].astype(bf16), 1)
    return left.astype(f32) + o[third : 2 * third] + right.astype(f32)


def conv_rows(window, kernel, low, high, emit, between=lambda: None):
    starts = list(range(low, high, 2))
    for k in range(0, len(starts), 2):
        group = starts[k : k + 2]
        o = jnp.dot(
            kernel[...],
            jnp.concatenate([window(r) for r in group], axis=1),
            preferred_element_type=f32,
        )
        half = o.shape[0] // 2
        for i, r in enumerate(group):
            part = o[:, i * N : (i + 1) * N]
            emit(r, part[:half])
            emit(r + 1, part[half:])
        between()


def first_window(fields, r):
    a = 4 * (r - 1 + MARGIN)
    return jnp.concatenate([fields[0, a : a + 16, :], fields[1, a : a + 16, :]], axis=0).astype(bf16)


def feature_window(feats, count, layer):
    return lambda r: feats[feature_rows(count, layer, r - 1, 4), :]


def gradient_window(grads, count, layer):
    return lambda r: grads[gradient_rows(count, layer, r - 1, 4), :]


def gelu_value(z):
    c = math.sqrt(2.0 / math.pi)
    zz = z * z
    h = 0.5 + 0.5 * jnp.tanh(z * (c + (c * 0.044715) * zz))
    return z * h, h, zz


def gelu_slope(f, h, zz):
    c = math.sqrt(2.0 / math.pi)
    return h + (f - f * h) * (2.0 * c + (6.0 * c * 0.044715) * zz)


def network_forward(count, fields, w_first, w_hidden, bias, feats, slopes, raw, raw_done, kept):
    tasks = []

    def slope_later(r, at):
        z, h = kept[0, at, :], kept[1, at, :]
        slopes[gradient_rows(count, LAYERS, r), :] = gelu_slope(z * h, h, z * z).astype(bf16)

    for m in range(1, LAYERS + 1):

        def emit(r, o, m=m):
            z = (o if m == 1 else fold(o)) + bias[m - 1]
            value, h, zz = gelu_value(z)
            feats[feature_rows(count, m, r), :] = value.astype(bf16)
            if m == LAYERS:
                at = slice((r + m) * CH, (r + m + 1) * CH)
                kept[0, at, :] = z
                kept[1, at, :] = h
                tasks.append(functools.partial(slope_later, r, at))
            elif -m <= r < count + m:
                slopes[gradient_rows(count, m, r), :] = gelu_slope(value, h, zz).astype(bf16)

        low, high = -reach(m), count + reach(m)
        if m == 1:
            conv_rows(functools.partial(first_window, fields), w_first, low, high, emit)
        else:
            conv_rows(feature_window(feats, count, m - 1), w_hidden.at[m - 2], low, high, emit)

    def emit_raw(r, o):
        value = fold(o) + bias[LAYERS]
        raw[(r + MID) * CH : (r + MID + 1) * CH, :] = value
        raw_done(r, value)

    groups = (count + 2 * RAW) // 4
    share = -(-len(tasks) // groups)

    def between():
        for task in tasks[:share]:
            task()
        del tasks[:share]

    window = feature_window(feats, count, LAYERS)
    conv_rows(window, w_hidden.at[LAYERS - 1], -RAW, count + RAW, emit_raw, between)
    for task in tasks:
        task()


def interleave(vel, fields):
    for which in range(2):
        x = vel[which]
        for j in range(4):
            fields[which, pl.ds(j, x.shape[0], stride=4), :] = lanes(x, j - 1)


def mixed(pairs, mix):
    cols = []
    for u, v in pairs:
        cols.append(jnp.concatenate([*split(u), *split(v)], axis=0))
    o = jnp.dot(mix[...], jnp.concatenate(cols, axis=1), preferred_element_type=f32)
    return [o[:, i * N : (i + 1) * N] * (1.0 / 80.0) for i in range(len(pairs))]


def clear_patches(count, fields, mix, clear, put):
    for r in range(-MID, count + MID, 2):
        pairs = []
        for k in range(2):
            a = 4 * (r + k - 1 + MARGIN)
            pairs.append((fields[0, a : a + 16, :], fields[1, a : a + 16, :]))
        parts = mixed(pairs, mix)
        for k, ((u, v), o) in enumerate(zip(pairs, parts)):
            a = 32 * (r + k + MID)
            clear[a : a + 16, :] = u - o[0:16]
            clear[a + 16 : a + 32, :] = v - o[16:32]
        a = 4 * (r + MID)
        put[a : a + 8, :] = jnp.concatenate([parts[0][32:36], parts[1][32:36]], axis=0)


def point_sums(r, value, clear):
    a = 32 * (r + MID)
    out = []
    for k in range(4):
        b = a + 16 * (k // 2)
        x = value[16 * k : 16 * k + 16] * clear[b : b + 16, :]
        out.append(x[:8] + x[8:])
    return out


def interpolate(r, sums, adder, put, interp):
    cols = []
    for i in range(0, len(sums), 2):
        high, low = split(jnp.concatenate(sums[i] + sums[i + 1], axis=0))
        cols.append(jnp.concatenate([high, low], axis=0))
    o = jnp.dot(adder[...], jnp.concatenate(cols, axis=1), preferred_element_type=f32)
    for i in range(len(cols)):
        a = 4 * (r + 2 * i + MID)
        interp[a : a + 8, :] = o[0:8, i * N : (i + 1) * N] + put[a : a + 8, :]


def by_kind(interp, k, mid):
    return interp[pl.ds(k, mid, stride=4), :]


def raw_gradient(count, clear, ginterp, grads):
    for r in range(-MID, count + MID):
        a = 32 * (r + MID)
        parts = []
        for k in range(4):
            b = a + 16 * (k // 2)
            parts.append(clear[b : b + 16, :] * ginterp[k, r + MID : r + MID + 1, :])
        grads[gradient_rows(count, LAYERS + 1, r), :] = jnp.concatenate(parts, axis=0).astype(bf16)


def put_columns():
    point = lax.broadcasted_iota(jnp.int32, (16, N), 0)
    px, py = (point & 3).astype(f32) - 1.5, (point >> 2).astype(f32) - 1.5
    return [(1.0 / 16.0) + (tx / 20.0) * px + (ty / 20.0) * py for tx, ty in TARGETS]


def spread_back(r, at, columns, mix, raw, ginterp, spread):
    pairs, gs = [], []
    for k in range(2):
        z = raw[at((r + k + MID) * CH, CH), :]
        g = [ginterp[i, at(r + k + MID, 1), :] for i in range(4)]
        x = [z[16 * i : 16 * i + 16] * g[i] for i in range(4)]
        pairs.append((x[0] + x[1], x[2] + x[3]))
        gs.append(g)
    parts = mixed(pairs, mix)
    for which in range(2):
        out = []
        for pair, o, g in zip(pairs, parts, gs):
            back = columns[2 * which] * g[2 * which] + columns[2 * which + 1] * g[2 * which + 1]
            out.append(pair[which] - o[16 * which : 16 * which + 16] + back)
        for i in range(4):
            spread[which, i, at(4 * (r + MID), 8), :] = jnp.concatenate(
                [x[4 * i : 4 * i + 4] for x in out], axis=0
            )


def gathered_back(count, spread, lines):
    out = []
    for which in range(2):
        for r in range(0, count, 2):
            total = None
            for i in range(4):
                a = 4 * (r + 1 - i + MID)
                x = spread[which, i, a : a + 8, :]
                total = x if total is None else total + x
            lines[which, 4 * r : 4 * r + 8, :] = total
        total = None
        for j in range(4):
            x = lanes(lines[which, pl.ds(j, count, stride=4), :], 1 - j)
            total = x if total is None else total + x
        out.append(total)
    return out


def carriers(u, v):
    return (
        0.5 * (u + lanes(u, 1)),
        0.5 * (v + lanes(v, 1)),
        0.5 * (u + rows(u, 1)),
        0.5 * (v + rows(v, 1)),
    )


def middle(x, count):
    return x[MARGIN - MID : MARGIN + MID + count]


def provisional(count, u, v, interp):
    mid = count + 2 * MID
    flux = [middle(x, count) * by_kind(interp, k, mid) for k, x in enumerate(carriers(u, v))]
    u, v = middle(u, count), middle(v, count)
    su = u - DT * (flux[0] - lanes(flux[0], -1) + (flux[1] - rows(flux[1], -1)))
    sv = v - DT * (flux[2] - lanes(flux[2], -1) + (flux[3] - rows(flux[3], -1)))
    return su[MID : MID + count], sv[MID : MID + count]


def flux_gradients(count, gu, gv):
    return [
        middle(x, count) * (-DT)
        for x in (gu - lanes(gu, 1), gu - rows(gu, 1), gv - lanes(gv, 1), gv - rows(gv, 1))
    ]


def interp_gradients(count, gu, gv, u, v, ginterp):
    for k, (g, x) in enumerate(zip(flux_gradients(count, gu, gv), carriers(u, v))):
        ginterp[k] = g * middle(x, count)


def velocity_gradients(count, gu, gv, interp, spread, lines):
    mid = count + 2 * MID
    half = [0.5 * g * by_kind(interp, k, mid) for k, g in enumerate(flux_gradients(count, gu, gv))]
    shares = gathered_back(count, spread, lines)
    out = []
    for which, g in enumerate((gu, gv)):
        along, across = half[which], half[2 + which]
        x = middle(g, count) + (along + lanes(along, -1)) + (across + rows(across, -1))
        out.append(x[MID : MID + count] + shares[which])
    return out


def network_backward(count, w_hidden, slopes, grads, between=lambda: None, copy=None):
    for m in range(LAYERS, 0, -1):

        def emit(r, o, m=m):
            at = gradient_rows(count, m, r)
            value = (fold_rounded(o) * slopes[at, :].astype(f32)).astype(bf16)
            grads[at, :] = value
            if m == 1 and copy is not None:
                copy[(r + 1) * CH : (r + 2) * CH, :] = value

        conv_rows(gradient_window(grads, count, m + 1), w_hidden.at[m - 1], -m, count + m, emit, between)


def input_gradient(count, w_first, window, gvel):
    starts = list(range(0, count, 2))
    for k in range(0, len(starts), 2):
        group = starts[k : k + 2]
        o = jnp.dot(
            w_first[...],
            jnp.concatenate([window(r) for r in group], axis=1),
            preferred_element_type=f32,
        )
        for i, r in enumerate(group):
            part = o[:, i * N : (i + 1) * N]
            both = lanes(part, -1)[0:4] + part[4:8] + lanes(part, 1)[8:12]
            gvel[0, r : r + 2, :] = both[0:2]
            gvel[1, r : r + 2, :] = both[2:4]


def folded(x):
    return x[: 3 * CH, : 3 * CH] + x[3 * CH :, CH:]


def weight_product(count, m, fields, feats, grads):
    starts = list(range(0, count, 2))
    shifts = (0,) if isinstance(m, int) and m == 1 else (-1, 0, 1)
    left, total = [], None
    for r in starts:
        g = [grads[gradient_rows(count, m, r + k), :] for k in range(2)]
        left.append(jnp.concatenate([lanes(x, -e) for x in g for e in shifts], axis=0))
        for x in g:
            x = x.astype(f32)
            total = x if total is None else total + x
    if isinstance(m, int) and m == 1:
        right = [first_window(fields, r) for r in starts]
    else:
        right = [feature_window(feats, count, m - 1)(r) for r in starts]
    out = lax.dot_general(
        jnp.concatenate(left, axis=1), jnp.concatenate(right, axis=1), NT, preferred_element_type=f32
    )
    return out, jnp.sum(total, axis=1, keepdims=True)


def weight_half(count, half, fields, feats, grads, put, extra):
    lane = lax.broadcasted_iota(jnp.int32, (CH, N), 1)
    extra[...] = jnp.zeros((3 * CH, N), f32)

    @pl.when(half == 1)
    def _():
        first, total = weight_product(count, 1, fields, feats, grads)
        first = jnp.concatenate([first, jnp.zeros((2 * CH, N - 32), f32)], axis=1)
        extra[:CH, :] = jnp.where(lane == 35, total, first[:CH])
        extra[CH : 2 * CH, :] = first[CH:]

    parts, columns = [], extra[:CH, :]
    for i in range(3):
        product, total = weight_product(count, 2 + 3 * half + i, fields, feats, grads)
        parts.append(folded(product))
        columns = jnp.where(lane == 32 + i, total, columns)
    parts.append(jnp.concatenate([columns[:, :CH], extra[CH:, :CH]], axis=0))
    wide = jnp.concatenate(parts, axis=1)
    for q in range(5):
        put(q, wide[:, q * N : (q + 1) * N])


def fetch(sources, targets, sems):
    copies = [pltpu.make_async_copy(a, b, sems.at[i]) for i, (a, b) in enumerate(zip(sources, targets))]
    for copy in copies:
        copy.start()
    return copies


def tap_of(middle, last, m):
    return (lambda a, e: last[3 * a + e]) if m == LAYERS - 1 else (lambda a, e: middle[m, 3 * a + e])


def prepare_kernel(*refs):
    own, f_first, f_hidden, bias, mix, adder, flags = refs[10:17]
    vel, cot, first, first_bias, middle, middle_bias, last, last_bias, tables, lengths = refs[17:27]
    copies = fetch(refs[:10], refs[17:27], refs[27])
    core = lax.axis_index("strip") & 1
    group = lax.axis_index("traj")
    for copy in copies:
        copy.wait()
    for i in range(STEPS):
        flags[i] = jnp.full((8, N), jnp.where(lengths[core] > i, 1.0, 0.0), f32)
    flags[STEPS] = jnp.full((8, N), jnp.where(core == 0, 1.0, 0.0), f32)
    for bit in range(flags.shape[0] - STEPS - 1):
        flags[STEPS + 1 + bit] = jnp.full((8, N), jnp.where((group >> bit) & 1 == 1, 1.0, 0.0), f32)
    own[0] = jnp.where(core == 0, vel[0], vel[1])
    own[1] = jnp.where(core == 0, cot[0], cot[1])
    zero = jnp.zeros((CH, CH), bf16)
    for m in range(LAYERS):
        tap = tap_of(middle, last, m)
        for two in range(2):
            for e in range(3):
                taps = [tap(q - two, e) if 0 <= q - two < 3 else zero for q in range(4)]
                f_hidden[m, (two * 3 + e) * CH : (two * 3 + e + 1) * CH, :] = jnp.concatenate(taps, axis=1)
    for two in range(2):
        lines = []
        for ch in range(2):
            for i in range(4):
                for j in range(4):
                    if 0 <= i - two < 3 and j < 3:
                        lines.append(first[3 * (i - two) + j, ch : ch + 1, :].astype(f32))
                    else:
                        lines.append(jnp.zeros((1, CH), f32))
        f_first[two * CH : (two + 1) * CH, :] = jnp.concatenate(lines, axis=0).T.astype(bf16)
    for m in range(LAYERS + 1):
        if 0 < m < LAYERS:
            line = middle_bias[m - 1 : m, :]
        else:
            line = (first_bias if m == 0 else last_bias)[...].reshape(1, CH)
        bias[m] = jnp.broadcast_to(line, (N, CH)).T
    mix[...] = tables[2, 0:48, 0:64].astype(bf16)
    adder[...] = tables[2, 64:80, :].astype(bf16)


def prepare_back_kernel(*refs):
    b_first, b_hidden, right, left, weight = refs[5:10]
    first, middle, last, tables = refs[10:14]
    copies = fetch(refs[:4], refs[10:14], refs[14])
    for copy in copies:
        copy.wait()
    zero = jnp.zeros((CH, CH), bf16)
    for m in range(LAYERS):
        tap = tap_of(middle, last, m)
        for two in range(2):
            for e in range(3):
                taps = [tap(2 - q + two, 2 - e) if 0 <= q - two < 3 else zero for q in range(4)]
                b_hidden[m, (two * 3 + e) * CH : (two * 3 + e + 1) * CH, :] = jnp.concatenate(
                    [jnp.concatenate(taps[:2], axis=0).T, jnp.concatenate(taps[2:], axis=0).T], axis=1
                )
    lines = jnp.zeros((1, CH), f32)
    taps = []
    for e in range(3):
        for ch in range(2):
            for two in range(2):
                line = [
                    first[3 * (2 - q + two) + 2 - e, ch : ch + 1, :].astype(f32) if 0 <= q - two < 3 else lines
                    for q in range(4)
                ]
                taps.append(jnp.concatenate(line, axis=1))
    taps.append(jnp.zeros((4, 4 * CH), f32))
    b_first[...] = jnp.concatenate(taps, axis=0).astype(bf16)
    high, low = split(tables[0])
    right[...] = jnp.concatenate([high, high, low], axis=0)
    left[...] = jnp.concatenate([high, low, high], axis=1)
    weight[...] = tables[1]


def chosen(flag, x, y):
    flag = flag[0:1, :] > 0.5
    return jnp.where(jnp.broadcast_to(flag, x.shape), x, y)


def assemble_kernel(flags, own, partner, cross, same, cot_partner, ext, cot):
    upper = flags[STEPS]

    def pair(mine, other, i):
        other = chosen(upper, other[0, i], other[1, i])
        return [chosen(upper, mine[i], other), chosen(upper, other, mine[i])]

    for i in range(2):
        above = chosen(upper, cross[0, i], same[1, i])[-MARGIN:]
        below = chosen(upper, same[0, i], cross[1, i])[:MARGIN]
        ext[i] = jnp.concatenate([above, *pair(own[0], partner, i), below], axis=0)
        cot[i] = jnp.concatenate(pair(own[1], cot_partner, i), axis=0)


def network_kernel(
    count, vel, extra, w_first, w_hidden, bias, mix, adder, block, interp, raw, clear, fields, feats, slopes, put, kept
):
    interleave(vel, fields)
    clear_patches(count, fields, mix, clear, put)
    sums = []

    def raw_done(r, value):
        sums.append(point_sums(r, value, clear))
        if len(sums) == 4 * LAG + 4:
            interpolate(r + 1 - len(sums), sums[:4], adder, put, interp)
            del sums[:4]

    network_forward(count, fields, w_first, w_hidden, bias, feats, slopes, raw, raw_done, kept)
    for i in range(0, len(sums), 4):
        interpolate(count + RAW - len(sums) + i, sums[i : i + 4], adder, put, interp)
    su, sv = provisional(count, vel[0], vel[1], interp)
    block[0] = su
    block[1] = sv
    block[2] = extra[0]
    block[3] = extra[1]


def joined(gathered, i):
    return jnp.concatenate([g[i] for g in gathered], axis=0)


def project_kernel(count, blocks, steps, flags, *refs):
    gathered, refs = refs[:blocks], refs[blocks:]
    forward, backward = steps
    mg = flags[backward][0:1, :]
    fields = [(mg * joined(gathered, 2), mg * joined(gathered, 3))]
    if forward is None:
        right, left, weight, gstar, own = refs
    else:
        vel, right, left, weight, gstar, own, ext = refs
        fields.append((joined(gathered, 0), joined(gathered, 1)))
        mv = flags[forward][0:1, :]
    out = project(fields, count, right, left, weight)
    for i in range(2):
        gstar[i] = out[0][i]
        own[i] = (1.0 - mg) * gathered[0][2 + i]
        if forward is not None:
            ext[i] = vel[i] + mv * (out[1][i] - vel[i])


def static(start, size):
    return slice(start, start + size)


def back_kernel(count, ext, gstar, clear, b_first, b_hidden, slopes, *refs):
    if len(refs) == 6:
        mix, raw, grads, gvel, spread, ginterp = refs
    else:
        grads, first, ginterp = refs
    interp_gradients(count, gstar[0], gstar[1], ext[0], ext[1], ginterp)
    raw_gradient(count, clear, ginterp, grads)
    tasks = []
    if len(refs) == 6:
        columns = put_columns()
        for r in range(-RAW, count + RAW, 2):
            tasks.append(functools.partial(spread_back, r, static, columns, mix, raw, ginterp, spread))
    turn = [0]

    def between():
        turn[0] += 1
        if tasks and turn[0] % 3 == 0:
            tasks.pop(0)()

    network_backward(count, b_hidden, slopes, grads, between, None if len(refs) == 6 else first)
    for task in tasks:
        task()
    if len(refs) == 6:
        input_gradient(count, b_first, gradient_window(grads, count, 1), gvel)


def finish_kernel(count, front, base, gstar, interp, gvel, spread, out, lines):
    change = velocity_gradients(count, gstar[0], gstar[1], interp, spread, lines)
    for i in range(2):
        out[i] = front[i]
        out[2 + i] = base[i] + change[i] + gvel[i]


def last_kernel(count, blocks, flags, *refs):
    gathered, refs = refs[:blocks], refs[blocks:]
    now, right, left, weight, base, ext, gstar, interp, first, b_first, mix, raw, out = refs[:13]
    lines, spread, ginterp, gvel = refs[13:]
    (news,) = project([(joined(gathered, 0), joined(gathered, 1))], count, right, left, weight)
    own = slice(MARGIN, MARGIN + count)
    mask = flags[STEPS - 1][0:1, :]
    for i in range(2):
        out[i] = now[i, own] + mask * (news[i][own] - now[i, own])
    gu, gv = gstar[0], gstar[1]
    input_gradient(count, b_first, lambda r: first[r * CH : (r + 4) * CH, :], gvel)
    interp_gradients(count, gu, gv, ext[0], ext[1], ginterp)
    columns = put_columns()

    def at(start, size):
        return pl.ds(pl.multiple_of(start, size), size) if size > 1 else pl.ds(start, size)

    def step(i, _):
        for k in range(2):
            spread_back(4 * i + 2 * k - RAW, at, columns, mix, raw, ginterp, spread)
        return 0

    lax.fori_loop(0, (count + 2 * RAW) // 4, step, 0)
    change = velocity_gradients(count, gu, gv, interp, spread, lines)
    for i in range(2):
        out[2 + i] = base[i] + change[i] + gvel[i]


def weights_kernel(count, fields, feats, grads, buffer, extra):
    def both(half, _):
        def put(q, value):
            buffer[place(half * HALF + q * 3 * CH, 3 * CH), :] = value

        weight_half(count, half, fields, feats, grads, put, extra)
        return 0

    lax.fori_loop(0, 2, both, 0)


def half_kernel(count, side, previous, fields, feats, grads, out, extra):
    half = (lax.axis_index("strip") & 1) ^ side

    def put(q, value):
        value = value + previous[place(half * HALF + q * 3 * CH, 3 * CH), :]
        out[q * 3 * CH : (q + 1) * 3 * CH, :] = value.astype(bf16)

    weight_half(count, half, fields, feats, grads, put, extra)
    if out.shape[0] > HALF:
        out[HALF:, :] = jnp.zeros((out.shape[0] - HALF, N), bf16)


def exchanged(flags, blocks):
    for bit in range(len(blocks).bit_length() - 1):
        flag = flags[STEPS + 1 + bit]
        blocks = [chosen(flag, blocks[i ^ (1 << bit)], x) for i, x in enumerate(blocks)]
    return blocks


def halves_kernel(flags, keep, received, *out):
    rows_each = out[0].shape[0]
    blocks = []
    for i in range(len(out)):
        at = slice(i * rows_each, (i + 1) * rows_each)
        blocks.append(keep[at, :].astype(f32) + received[at, :].astype(f32))
    for ref, x in zip(out, exchanged(flags, blocks)):
        ref[...] = x.astype(bf16)


def arrange_kernel(flags, *refs):
    *blocks, out = refs
    rows_each = blocks[0].shape[0]
    for i, x in enumerate(exchanged(flags, [x[...].astype(f32) for x in blocks])):
        out[i * rows_each : (i + 1) * rows_each, :] = x.astype(bf16)


def unpack_kernel(flags, mine, other, first, first_bias, middle, middle_bias, last, last_bias):
    for half in range(2):
        a, b = (mine, other) if half == 0 else (other, mine)
        blocks = []
        for q in range(5):
            at = slice(q * 3 * CH, (q + 1) * 3 * CH)
            blocks.append(chosen(flags[STEPS], a[at, :].astype(f32), b[at, :].astype(f32)))
        wide = jnp.concatenate(blocks, axis=1)
        turned = [blocks[4][two * CH : (two + 1) * CH].T[CH:] for two in range(2)]
        for i in range(3):
            m = 3 * half + i
            for a in range(3):
                part = wide[:, (3 * i + a) * CH : (3 * i + a + 1) * CH]
                for e in range(3):
                    value = part[e * CH : (e + 1) * CH]
                    if m < LAYERS - 1:
                        middle[m, 3 * a + e] = value
                    else:
                        last[3 * a + e] = value
            if m < LAYERS - 1:
                middle_bias[m : m + 1, :] = turned[0][32 + i : 33 + i]
            else:
                last_bias[...] = turned[0][32 + i]
    first_bias[...] = turned[0][35]
    for a in range(3):
        for e in range(3):
            for ch in range(2):
                low, high = 16 * ch + 4 * a + e, 16 * ch + 4 * (a + 1) + e
                first[3 * a + e, ch : ch + 1, :] = turned[0][low : low + 1] + turned[1][high : high + 1]


VMEM = pl.BlockSpec(memory_space=pltpu.VMEM)
SMEM = pl.BlockSpec(memory_space=pltpu.SMEM)
PARAMS = pltpu.CompilerParams(vmem_limit_bytes=VMEM_BYTES)


def array(dtype, *shape):
    return jax.ShapeDtypeStruct(shape, dtype)


def cost(flops, moved):
    return pl.CostEstimate(flops=flops, bytes_accessed=moved, transcendentals=0)


def field(count, *lead):
    return pltpu.VMEM(lead + (count, N), f32)


def feature_array(count):
    return array(bf16, LAYERS * (count + 24) * CH, N)


def gradient_array(count, slots):
    return array(bf16, slots * (count + 16) * CH, N)


def call(kernel, name, flops, inputs, out, scratch=()):
    return pl.pallas_call(
        kernel,
        in_specs=[VMEM] * len(inputs),
        out_specs=jax.tree.map(lambda _: VMEM, out),
        out_shape=out,
        scratch_shapes=list(scratch),
        compiler_params=PARAMS,
        cost_estimate=cost(flops, 10**6),
        name=name,
    )(*inputs)


def run_prepare(lengths, vel, cot, params, bits):
    out = [
        array(f32, 2, 2, vel.shape[2], N),
        array(bf16, 2 * CH, 32),
        array(bf16, LAYERS, 6 * CH, 4 * CH),
        array(f32, LAYERS + 1, CH, N),
        array(bf16, 48, 64),
        array(bf16, 16, N),
        array(f32, STEPS + 1 + bits, 8, N),
    ]
    inputs = [vel, cot, *params, jnp.asarray(constant_tables(N)), lengths]
    scratch = [pltpu.VMEM(x.shape, x.dtype) for x in inputs[:-1]] + [pltpu.SMEM(lengths.shape, lengths.dtype)]
    return call_from_hbm(prepare_kernel, "prepare", inputs, out, scratch)


def run_prepare_back(params, after):
    first, _, middle, _, last, _ = params
    out = [
        array(bf16, 16, 4 * CH),
        array(bf16, LAYERS, 6 * CH, 4 * CH),
        array(bf16, 3 * N, N),
        array(bf16, N, 3 * N),
        array(f32, N, N),
    ]
    inputs = [first, middle, last, jnp.asarray(constant_tables(N))]
    scratch = [pltpu.VMEM(x.shape, x.dtype) for x in inputs]
    b_first, b_hidden, *tables = call_from_hbm(prepare_back_kernel, "prepare_back", inputs, out, scratch, after)
    return b_first, b_hidden, tables


def call_from_hbm(kernel, name, inputs, out, scratch, *after):
    hbm = pl.BlockSpec(memory_space=pltpu.HBM)
    inputs = [pltpu.with_memory_space_constraint(x, pltpu.HBM) for x in inputs]
    return pl.pallas_call(
        kernel,
        in_specs=[hbm] * len(inputs) + [VMEM] * len(after),
        out_specs=[VMEM] * len(out),
        out_shape=out,
        scratch_shapes=scratch + [pltpu.SemaphoreType.DMA((len(inputs),))],
        compiler_params=PARAMS,
        cost_estimate=cost(10**9, 10**6),
        name=name,
    )(*inputs, *after)


def run_assemble(count, flags, fields):
    out = [array(f32, 2, count + 2 * MARGIN, N), array(f32, 2, count, N)]
    return call(assemble_kernel, "assemble", 10**6, [flags, *fields], out)


def run_network(count, vel, extra, weights):
    local_rows, mid = count + 2 * MARGIN, count + 2 * MID
    out = [array(f32, 4, count, N), array(f32, 4 * mid, N), array(f32, mid * CH, N), array(f32, mid * 32, N)]
    out += [array(f32, 2, 4 * local_rows, N)]
    out += [feature_array(count), gradient_array(count, LAYERS)]
    scratch = [field(4 * mid), field((count + 2 * LAYERS) * CH, 2)]
    return call(functools.partial(network_kernel, count), "network", 4 * 10**9, [vel, extra, *weights], out, scratch)


def run_project(count, steps, flags, gathered, tables, *vel):
    local_rows = count + 2 * MARGIN
    out = [array(f32, 2, local_rows, N), array(f32, 2, count, N)]
    if vel:
        out.append(array(f32, 2, local_rows, N))
    kernel = functools.partial(project_kernel, count, len(gathered), steps)
    return call(kernel, "project", 10**9, [flags, *gathered, *vel, *tables], out)


def run_back(count, ext, gstar, clear, b_first, b_hidden, slopes, *more):
    mid = count + 2 * MID
    inputs = [ext, gstar, clear, b_first, b_hidden, slopes, *more]
    out = [gradient_array(count, LAYERS + 1)]
    if more:
        out += [array(f32, 2, count, N), array(f32, 2, 4, 4 * mid, N)]
    else:
        out.append(array(bf16, (count + 2) * CH, N))
    return call(functools.partial(back_kernel, count), "back", 4 * 10**9, inputs, out, [field(mid, 4)])


def run_finish(count, *inputs):
    kernel = functools.partial(finish_kernel, count)
    return call(kernel, "finish", 10**9, inputs, array(f32, 4, count, N), [field(4 * count, 2)])


def run_last(count, flags, gathered, *inputs):
    mid = count + 2 * MID
    scratch = [field(4 * count, 2), field(4 * mid, 2, 4), field(mid, 4), field(count, 2)]
    kernel = functools.partial(last_kernel, count, len(gathered))
    return call(kernel, "last", 10**9, [flags, *gathered, *inputs], array(f32, 4, count, N), scratch)


def run_weights(count, fields, feats, grads):
    kernel = functools.partial(weights_kernel, count)
    return call(kernel, "weights", 3 * 10**9, [fields, feats, grads], array(f32, 2 * HALF, N), [field(3 * CH)])


def run_half(count, side, rows, previous, fields, feats, grads, *after):
    inputs = [previous, fields, feats, grads, *after]
    kernel = functools.partial(half_kernel, count, side)
    if after:
        kernel = lambda *refs: half_kernel(count, side, *refs[:4], *refs[5:])
    return call(kernel, "half", 10**9, inputs, array(bf16, rows, N), [field(3 * CH)])


def run_halves(flags, keep, received, parts):
    out = [array(bf16, keep.shape[0] // parts, N)] * parts
    return call(halves_kernel, "halves", 10**6, [flags, keep, received], out)


def run_arrange(flags, blocks):
    out = array(bf16, len(blocks) * blocks[0].shape[0], N)
    return call(arrange_kernel, "arrange", 10**6, [flags, *blocks], out)


def run_unpack(flags, mine, other):
    out = [
        array(f32, 9, 2, CH),
        array(f32, CH),
        array(f32, LAYERS - 1, 9, CH, CH),
        array(f32, LAYERS - 1, CH),
        array(f32, 9, CH, CH),
        array(f32, CH),
    ]
    return call(unpack_kernel, "unpack", 10**7, [flags, mine, other], out)


def swap(x, axis, offset):
    count = lax.axis_size(axis)
    return lax.ppermute(x, axis, [(i, i ^ offset) for i in range(count)])


def from_group(x, ahead):
    count = lax.axis_size("strip")
    return lax.ppermute(x, "strip", [(i, (i - 2 * ahead) % count) for i in range(count)])


def gather_groups(x):
    return [x] + [from_group(x, k) for k in range(1, lax.axis_size("strip") // 2)]


def margins(velocity, partner, core):
    count = lax.axis_size("strip")
    if velocity.shape[2] < MARGIN:
        upper = core[0] == 0
        pair = jnp.where(
            upper,
            jnp.concatenate([velocity[0], partner[0]], axis=1),
            jnp.concatenate([partner[1], velocity[1]], axis=1),
        )
        above, below = from_group(pair[:, -MARGIN:], -1), from_group(pair[:, :MARGIN], 1)
        return jnp.stack([above, below]), jnp.stack([below, above])
    cross = [(i, (i - 1) % count if i % 2 == 0 else (i + 1) % count) for i in range(count)]
    same = [(i, (i - 2) % count if i % 2 == 0 else (i + 2) % count) for i in range(count)]
    return lax.ppermute(velocity, "strip", cross), lax.ppermute(velocity, "strip", same)


def sum_everywhere(keep, received, flags):
    parts = lax.axis_size("traj")
    groups = lax.axis_size("strip") // 2
    blocks = run_halves(flags, keep, received, parts)
    total = blocks[0].astype(f32)
    for k in range(1, parts):
        total = total + swap(blocks[k], "traj", k).astype(f32)
    x = total.astype(bf16)
    total = x.astype(f32)
    for k in range(1, groups):
        total = total + swap(x, "strip", 2 * k).astype(f32)
    x = total.astype(bf16)
    x = run_arrange(flags, [x] + [swap(x, "traj", k) for k in range(1, parts)])
    return x, swap(x, "strip", 1)


def per_device(
    velocity, lengths, cotangent, first_kernel, first_bias, middle_kernels, middle_biases, last_kernel, last_bias
):
    rc = velocity.shape[2]
    count = 2 * rc
    index = lax.axis_index("strip") & 1
    core = index[None]
    pick = lambda y, i: lax.dynamic_index_in_dim(y, i, 0, False)

    partner = swap(velocity, "strip", 1)
    cross, same = margins(velocity, partner, core)
    cot_partner = swap(cotangent, "strip", 1)
    first_kernel = first_kernel.transpose(0, 2, 1)
    params = (first_kernel, first_bias, middle_kernels, middle_biases, last_kernel, last_bias)
    parts = lax.axis_size("traj")
    half_rows = -(-HALF // (parts * 16)) * parts * 16
    own, w_first, w_hidden, bias, mix, adder, flags = run_prepare(
        lengths, velocity, cotangent, params, parts.bit_length() - 1
    )
    weights = (w_first, w_hidden, bias, mix, adder)

    v0, cot = run_assemble(count, flags, (own, partner, cross, same, cot_partner))
    block, interp0, raw0, clear0, fields0, feats0, slopes0 = run_network(count, v0, cot, weights)
    gathered = gather_groups(block)
    b_first, b_hidden, tables = run_prepare_back(params, interp0)
    gstar1, base, v1 = run_project(count, (0, 1), flags, gathered, tables, v0)
    block, interp1, raw1, clear1, fields1, feats1, slopes1 = run_network(count, v1, cot, weights)
    grads1, gvel, spread = run_back(count, v1, gstar1, clear1, b_first, b_hidden, slopes1, mix, raw1)
    block = run_finish(count, block, base, gstar1, interp1, gvel, spread)
    gathered = gather_groups(block)
    buffer = run_weights(count, fields1, feats1, grads1)
    gstar0, base = run_project(count, (None, 0), flags, gathered, tables)
    grads0, first = run_back(count, v0, gstar0, clear0, b_first, b_hidden, slopes0)
    send = run_half(count, 1, half_rows, buffer, fields0, feats0, grads0)
    received = swap(send, "strip", 1)
    keep = run_half(count, 0, half_rows, buffer, fields0, feats0, grads0, send)
    out = run_last(
        count, flags, gathered, v1, *tables, base, v0, gstar0, interp0, first, b_first, mix, raw0
    )

    strips = out.reshape(4, 2, rc, N).transpose(1, 0, 2, 3)
    mine, other = pick(strips, index)[None], swap(pick(strips, 1 - index), "strip", 1)[None]
    out = jnp.where(
        index == 0, jnp.concatenate([mine, other], axis=0), jnp.concatenate([other, mine], axis=0)
    )
    mine, other = sum_everywhere(keep, received, flags)
    grad_first, *rest = run_unpack(flags, mine, other)
    return (out[:, :2], out[:, 2:], grad_first.transpose(0, 2, 1), *rest)


def solution(mesh):
    band = P("traj", None, "strip", None)
    return jax.shard_map(
        per_device,
        mesh=mesh,
        in_specs=(band, P("traj"), band) + (P(),) * 6,
        out_specs=(band, band) + (P(),) * 6,
        check_vma=False,
    )
```

```python
import functools
import math

import jax
import jax.numpy as jnp
import numpy as np
from jax import lax
from jax.experimental import pallas as pl
from jax.experimental.pallas import tpu as pltpu
from jax.sharding import PartitionSpec as P

STEPS = 2
DT = 0.25
MARGIN = 16
MID = 8
LAG = 3
RAW = 2
CH = 64
LAYERS = 6
N = 128
HALF = 15 * CH
bf16 = jnp.bfloat16
f32 = jnp.float32
NT = (((1,), (1,)), ((), ()))
VMEM_BYTES = 14 * 2**20


def reach(layer):
    return 12 - layer


def place(start, size):
    return slice(start, start + size) if isinstance(start, int) else pl.ds(pl.multiple_of(start, CH), size)


def feature_rows(count, layer, r, rows=1):
    return place(((layer - 1) * (count + 24) + r + 12) * CH, rows * CH)


def gradient_rows(count, layer, r, rows=1):
    return place(((layer - 1) * (count + 16) + r + 8) * CH, rows * CH)


def lanes(x, s):
    return x if s == 0 else pltpu.roll(x, (-s) % x.shape[1], 1)


def rows(x, s):
    return x if s == 0 else pltpu.roll(x, (-s) % x.shape[0], 0)


TARGETS = ((0.0, -0.5), (-0.5, 0.0), (0.0, -0.5), (-0.5, 0.0))
POINTS = np.arange(16)
PX, PY = POINTS % 4 - 1.5, POINTS // 4 - 1.5
TAKEN = 5.0 + 4.0 * (PX[:, None] * PX[None, :] + PY[:, None] * PY[None, :])
PUT = [5.0 + 4.0 * (tx * PX + ty * PY) for tx, ty in TARGETS]


def constant_tables(length):
    k = np.arange(length)
    angle = 2.0 * math.pi * ((k[:, None] * k[None, :]) % length) / length
    table = (np.cos(angle) + np.sin(angle)) / math.sqrt(length)
    eigen = 2.0 - 2.0 * np.cos(2.0 * math.pi * k / length)
    total = eigen[:, None] + eigen[None, :]
    total[0, 0] = 1.0
    weight = 1.0 / total
    weight[0, 0] = 0.0
    small = np.zeros((length, length))
    for part in range(2):
        for which in range(2):
            cols = slice(32 * which + 16 * part, 32 * which + 16 * part + 16)
            small[16 * which : 16 * which + 16, cols] = TAKEN
            small[32 + 2 * which, cols] = PUT[2 * which]
            small[33 + 2 * which, cols] = PUT[2 * which + 1]
        for i in range(8):
            small[64 + i, 64 * part + 8 * i : 64 * part + 8 * i + 8] = 1.0
    return np.stack([table, weight, small]).astype(np.float32)


def split(x):
    high = x.astype(bf16)
    return high, (x - high.astype(f32)).astype(bf16)


def times_right(x, right):
    high, low = split(x)
    return jnp.dot(jnp.concatenate([high, low, high], axis=1), right[...], preferred_element_type=f32)


def times_left(x, left):
    high, low = split(x)
    return jnp.dot(left[...], jnp.concatenate([high, high, low], axis=0), preferred_element_type=f32)


def local(x, count):
    return jnp.concatenate([x[N - MARGIN :], x[: count + MARGIN]], axis=0)


def with_row_above(v, above):
    first = lax.broadcasted_iota(jnp.int32, v.shape, 0) == 0
    return jnp.where(first, jnp.broadcast_to(above, v.shape), rows(v, -1))


def divergence(u, v, above):
    return u - lanes(u, -1) + (v - with_row_above(v, above))


def write_messages(fields, top, bottom, far):
    count = fields[0].shape[0]
    rest = count - MARGIN
    zero = jnp.zeros((1, N), f32)
    sources = [divergence(fields[2 * i], fields[2 * i + 1], zero) for i in range(2)]

    def ends(row):
        return [jnp.concatenate([fields[1][row : row + 1], fields[3][row : row + 1], jnp.zeros((6, N), f32)], axis=0)]

    parts = [x[:MARGIN] for x in fields] + [x[MARGIN:] for x in sources if rest] + ends(count - 1)
    top[...] = jnp.concatenate(parts, axis=0)
    parts = [x[rest:] for x in fields] + [x[:rest] for x in sources if rest] + ends(max(rest - 1, 0))
    bottom[...] = jnp.concatenate(parts, axis=0)
    far[...] = jnp.concatenate(sources + ends(count - 1), axis=0)


def read_messages(kind, block, messages):
    count = block.shape[1]
    rest = count - MARGIN
    top, far, bottom = messages[0], messages[1:-1], messages[-1]
    cut = lambda ref, start, size: ref[start : start + size, :]
    u, v = block[2 * kind], block[2 * kind + 1]
    top_u, top_v = [cut(top, (2 * kind + i) * MARGIN, MARGIN) for i in range(2)]
    low_u, low_v = [cut(bottom, (2 * kind + i) * MARGIN, MARGIN) for i in range(2)]
    source = [divergence(u, v, low_v[MARGIN - 1 :]), divergence(top_u, top_v, v[count - 1 :])]
    fields = 4 * MARGIN
    last = top_v[MARGIN - 1 :]
    if rest:
        source.append(cut(top, fields + kind * rest, rest))
        last = cut(top, fields + 2 * rest + kind, 1)
    first = lax.broadcasted_iota(jnp.int32, (count, N), 0) == 0
    for ref in far:
        x = cut(ref, kind * count, count)
        source.append(x - jnp.where(first, jnp.broadcast_to(last, x.shape), 0.0))
        last = cut(ref, 2 * count + kind, 1)
    if rest:
        x = cut(bottom, fields + kind * rest, rest)
        source.append(x - jnp.where(first[:rest], jnp.broadcast_to(last, x.shape), 0.0))
        last = cut(bottom, fields + 2 * rest + kind, 1)
    source.append(divergence(low_u, low_v, last))
    return [
        jnp.concatenate([low_u, u, top_u], axis=0),
        jnp.concatenate([low_v, v, top_v], axis=0),
        jnp.concatenate(source, axis=0),
    ]


def project(fields, count, right, left, weight):
    number = len(fields)
    x = times_right(jnp.concatenate([source for _, _, source in fields], axis=0), right)
    x = jnp.concatenate([x[i * N : (i + 1) * N] for i in range(number)], axis=1)
    x = times_left(x, left) * jnp.concatenate([weight[...]] * number, axis=1)
    x = local(times_left(x, left), count)
    size = x.shape[0]
    x = times_right(jnp.concatenate([x[:, i * N : (i + 1) * N] for i in range(number)], axis=0), right)
    out = []
    for i, (u, v, _) in enumerate(fields):
        p = -x[i * size : (i + 1) * size]
        out.append((u - (lanes(p, 1) - p), v - (rows(p, 1) - p)))
    return out


def fold(o):
    third = o.shape[0] // 3
    return lanes(o[:third], -1) + o[third : 2 * third] + lanes(o[2 * third :], 1)


def fold_rounded(o):
    third = o.shape[0] // 3
    left, right = lanes(o[:third].astype(bf16), -1), lanes(o[2 * third :].astype(bf16), 1)
    return left.astype(f32) + o[third : 2 * third] + right.astype(f32)


def conv_rows(window, kernel, low, high, emit, between=lambda: None):
    starts = list(range(low, high, 2))
    for k in range(0, len(starts), 2):
        group = starts[k : k + 2]
        o = jnp.dot(
            kernel[...],
            jnp.concatenate([window(r) for r in group], axis=1),
            preferred_element_type=f32,
        )
        half = o.shape[0] // 2
        for i, r in enumerate(group):
            part = o[:, i * N : (i + 1) * N]
            emit(r, part[:half])
            emit(r + 1, part[half:])
        between()


def first_window(fields, r):
    a = 4 * (r - 1 + MARGIN)
    return jnp.concatenate([fields[0, a : a + 16, :], fields[1, a : a + 16, :]], axis=0).astype(bf16)


def feature_window(feats, count, layer):
    return lambda r: feats[feature_rows(count, layer, r - 1, 4), :]


def gradient_window(grads, count, layer):
    return lambda r: grads[gradient_rows(count, layer, r - 1, 4), :]


def gelu_value(z):
    c = math.sqrt(2.0 / math.pi)
    zz = z * z
    h = 0.5 + 0.5 * jnp.tanh(z * (c + (c * 0.044715) * zz))
    return z * h, h, zz


def gelu_slope(f, h, zz):
    c = math.sqrt(2.0 / math.pi)
    return h + (f - f * h) * (2.0 * c + (6.0 * c * 0.044715) * zz)


def network_forward(count, fields, w_first, w_hidden, bias, feats, slopes, raw, raw_done, kept):
    tasks = []

    def slope_later(r, at):
        z, h = kept[0, at, :], kept[1, at, :]
        slopes[gradient_rows(count, LAYERS, r), :] = gelu_slope(z * h, h, z * z).astype(bf16)

    for m in range(1, LAYERS + 1):

        def emit(r, o, m=m):
            z = (o if m == 1 else fold(o)) + bias[m - 1]
            value, h, zz = gelu_value(z)
            feats[feature_rows(count, m, r), :] = value.astype(bf16)
            if m == LAYERS:
                at = slice((r + m) * CH, (r + m + 1) * CH)
                kept[0, at, :] = z
                kept[1, at, :] = h
                tasks.append(functools.partial(slope_later, r, at))
            elif -m <= r < count + m:
                slopes[gradient_rows(count, m, r), :] = gelu_slope(value, h, zz).astype(bf16)

        low, high = -reach(m), count + reach(m)
        if m == 1:
            conv_rows(functools.partial(first_window, fields), w_first, low, high, emit)
        else:
            conv_rows(feature_window(feats, count, m - 1), w_hidden.at[m - 2], low, high, emit)

    def emit_raw(r, o):
        value = fold(o) + bias[LAYERS]
        raw[(r + MID) * CH : (r + MID + 1) * CH, :] = value
        raw_done(r, value)

    groups = (count + 2 * RAW) // 4
    share = -(-len(tasks) // groups)

    def between():
        for task in tasks[:share]:
            task()
        del tasks[:share]

    window = feature_window(feats, count, LAYERS)
    conv_rows(window, w_hidden.at[LAYERS - 1], -RAW, count + RAW, emit_raw, between)
    for task in tasks:
        task()


def interleave(vel, fields):
    for which in range(2):
        x = vel[which]
        for j in range(4):
            fields[which, pl.ds(j, x.shape[0], stride=4), :] = lanes(x, j - 1)


def mixed(pairs, mix):
    cols = []
    for u, v in pairs:
        cols.append(jnp.concatenate([*split(u), *split(v)], axis=0))
    o = jnp.dot(mix[...], jnp.concatenate(cols, axis=1), preferred_element_type=f32)
    return [o[:, i * N : (i + 1) * N] * (1.0 / 80.0) for i in range(len(pairs))]


def clear_patches(count, fields, mix, clear, put):
    for r in range(-MID, count + MID, 2):
        pairs = []
        for k in range(2):
            a = 4 * (r + k - 1 + MARGIN)
            pairs.append((fields[0, a : a + 16, :], fields[1, a : a + 16, :]))
        parts = mixed(pairs, mix)
        for k, ((u, v), o) in enumerate(zip(pairs, parts)):
            a = 32 * (r + k + MID)
            clear[a : a + 16, :] = u - o[0:16]
            clear[a + 16 : a + 32, :] = v - o[16:32]
        a = 4 * (r + MID)
        put[a : a + 8, :] = jnp.concatenate([parts[0][32:36], parts[1][32:36]], axis=0)


def point_sums(r, value, clear):
    a = 32 * (r + MID)
    out = []
    for k in range(4):
        b = a + 16 * (k // 2)
        x = value[16 * k : 16 * k + 16] * clear[b : b + 16, :]
        out.append(x[:8] + x[8:])
    return out


def interpolate(r, sums, adder, put, interp):
    cols = []
    for i in range(0, len(sums), 2):
        high, low = split(jnp.concatenate(sums[i] + sums[i + 1], axis=0))
        cols.append(jnp.concatenate([high, low], axis=0))
    o = jnp.dot(adder[...], jnp.concatenate(cols, axis=1), preferred_element_type=f32)
    for i in range(len(cols)):
        a = 4 * (r + 2 * i + MID)
        interp[a : a + 8, :] = o[0:8, i * N : (i + 1) * N] + put[a : a + 8, :]


def by_kind(interp, k, mid):
    return interp[pl.ds(k, mid, stride=4), :]


def raw_gradient(count, clear, ginterp, grads):
    for r in range(-MID, count + MID):
        a = 32 * (r + MID)
        parts = []
        for k in range(4):
            b = a + 16 * (k // 2)
            parts.append(clear[b : b + 16, :] * ginterp[k, r + MID : r + MID + 1, :])
        grads[gradient_rows(count, LAYERS + 1, r), :] = jnp.concatenate(parts, axis=0).astype(bf16)


def put_columns():
    point = lax.broadcasted_iota(jnp.int32, (16, N), 0)
    px, py = (point & 3).astype(f32) - 1.5, (point >> 2).astype(f32) - 1.5
    return [(1.0 / 16.0) + (tx / 20.0) * px + (ty / 20.0) * py for tx, ty in TARGETS]


def spread_back(r, at, columns, mix, raw, ginterp, spread):
    pairs, gs = [], []
    for k in range(2):
        z = raw[at((r + k + MID) * CH, CH), :]
        g = [ginterp[i, at(r + k + MID, 1), :] for i in range(4)]
        x = [z[16 * i : 16 * i + 16] * g[i] for i in range(4)]
        pairs.append((x[0] + x[1], x[2] + x[3]))
        gs.append(g)
    parts = mixed(pairs, mix)
    for which in range(2):
        out = []
        for pair, o, g in zip(pairs, parts, gs):
            back = columns[2 * which] * g[2 * which] + columns[2 * which + 1] * g[2 * which + 1]
            out.append(pair[which] - o[16 * which : 16 * which + 16] + back)
        for i in range(4):
            spread[which, i, at(4 * (r + MID), 8), :] = jnp.concatenate(
                [x[4 * i : 4 * i + 4] for x in out], axis=0
            )


def gathered_back(count, spread, lines):
    out = []
    for which in range(2):
        for r in range(0, count, 2):
            total = None
            for i in range(4):
                a = 4 * (r + 1 - i + MID)
                x = spread[which, i, a : a + 8, :]
                total = x if total is None else total + x
            lines[which, 4 * r : 4 * r + 8, :] = total
        total = None
        for j in range(4):
            x = lanes(lines[which, pl.ds(j, count, stride=4), :], 1 - j)
            total = x if total is None else total + x
        out.append(total)
    return out


def carriers(u, v):
    return (
        0.5 * (u + lanes(u, 1)),
        0.5 * (v + lanes(v, 1)),
        0.5 * (u + rows(u, 1)),
        0.5 * (v + rows(v, 1)),
    )


def middle(x, count):
    return x[MARGIN - MID : MARGIN + MID + count]


def provisional(count, u, v, interp):
    mid = count + 2 * MID
    flux = [middle(x, count) * by_kind(interp, k, mid) for k, x in enumerate(carriers(u, v))]
    u, v = middle(u, count), middle(v, count)
    su = u - DT * (flux[0] - lanes(flux[0], -1) + (flux[1] - rows(flux[1], -1)))
    sv = v - DT * (flux[2] - lanes(flux[2], -1) + (flux[3] - rows(flux[3], -1)))
    return su[MID : MID + count], sv[MID : MID + count]


def flux_gradients(count, gu, gv):
    return [
        middle(x, count) * (-DT)
        for x in (gu - lanes(gu, 1), gu - rows(gu, 1), gv - lanes(gv, 1), gv - rows(gv, 1))
    ]


def interp_gradients(count, gu, gv, u, v, ginterp):
    for k, (g, x) in enumerate(zip(flux_gradients(count, gu, gv), carriers(u, v))):
        ginterp[k] = g * middle(x, count)


def velocity_gradients(count, gu, gv, interp, spread, lines):
    mid = count + 2 * MID
    half = [0.5 * g * by_kind(interp, k, mid) for k, g in enumerate(flux_gradients(count, gu, gv))]
    shares = gathered_back(count, spread, lines)
    out = []
    for which, g in enumerate((gu, gv)):
        along, across = half[which], half[2 + which]
        x = middle(g, count) + (along + lanes(along, -1)) + (across + rows(across, -1))
        out.append(x[MID : MID + count] + shares[which])
    return out


def network_backward(count, w_hidden, slopes, grads, between=lambda: None, copy=None):
    for m in range(LAYERS, 0, -1):

        def emit(r, o, m=m):
            at = gradient_rows(count, m, r)
            value = (fold_rounded(o) * slopes[at, :].astype(f32)).astype(bf16)
            grads[at, :] = value
            if m == 1 and copy is not None:
                copy[(r + 1) * CH : (r + 2) * CH, :] = value

        conv_rows(gradient_window(grads, count, m + 1), w_hidden.at[m - 1], -m, count + m, emit, between)


def input_gradient(count, w_first, window, gvel):
    starts = list(range(0, count, 2))
    for k in range(0, len(starts), 2):
        group = starts[k : k + 2]
        o = jnp.dot(
            w_first[...],
            jnp.concatenate([window(r) for r in group], axis=1),
            preferred_element_type=f32,
        )
        for i, r in enumerate(group):
            part = o[:, i * N : (i + 1) * N]
            both = lanes(part, -1)[0:4] + part[4:8] + lanes(part, 1)[8:12]
            gvel[0, r : r + 2, :] = both[0:2]
            gvel[1, r : r + 2, :] = both[2:4]


def folded(x):
    return x[: 3 * CH, : 3 * CH] + x[3 * CH :, CH:]


def weight_product(count, m, fields, feats, grads):
    starts = list(range(0, count, 2))
    shifts = (0,) if isinstance(m, int) and m == 1 else (-1, 0, 1)
    left, total = [], None
    for r in starts:
        g = [grads[gradient_rows(count, m, r + k), :] for k in range(2)]
        left.append(jnp.concatenate([lanes(x, -e) for x in g for e in shifts], axis=0))
        for x in g:
            x = x.astype(f32)
            total = x if total is None else total + x
    if isinstance(m, int) and m == 1:
        right = [first_window(fields, r) for r in starts]
    else:
        right = [feature_window(feats, count, m - 1)(r) for r in starts]
    out = lax.dot_general(
        jnp.concatenate(left, axis=1), jnp.concatenate(right, axis=1), NT, preferred_element_type=f32
    )
    return out, jnp.sum(total, axis=1, keepdims=True)


def weight_half(count, half, fields, feats, grads, put, extra):
    lane = lax.broadcasted_iota(jnp.int32, (CH, N), 1)
    extra[...] = jnp.zeros((3 * CH, N), f32)

    def first_layer():
        first, total = weight_product(count, 1, fields, feats, grads)
        first = jnp.concatenate([first, jnp.zeros((2 * CH, N - 32), f32)], axis=1)
        extra[:CH, :] = jnp.where(lane == 35, total, first[:CH])
        extra[CH : 2 * CH, :] = first[CH:]

    if not isinstance(half, int):
        pl.when(half == 1)(first_layer)
    elif half == 1:
        first_layer()
    parts, columns = [], extra[:CH, :]
    for i in range(3):
        product, total = weight_product(count, 2 + 3 * half + i, fields, feats, grads)
        parts.append(folded(product))
        columns = jnp.where(lane == 32 + i, total, columns)
    parts.append(jnp.concatenate([columns[:, :CH], extra[CH:, :CH]], axis=0))
    wide = jnp.concatenate(parts, axis=1)
    for q in range(5):
        put(q, wide[:, q * N : (q + 1) * N])


def fetch(sources, targets, sems):
    copies = [pltpu.make_async_copy(a, b, sems.at[i]) for i, (a, b) in enumerate(zip(sources, targets))]
    for copy in copies:
        copy.start()
    return copies


def tap_of(middle, last, m):
    return (lambda a, e: last[3 * a + e]) if m == LAYERS - 1 else (lambda a, e: middle[m, 3 * a + e])


def prepare_kernel(*refs):
    own, f_first, f_hidden, bias, mix, adder, flags = refs[10:17]
    vel, cot, first, first_bias, middle, middle_bias, last, last_bias, tables, lengths = refs[17:27]
    copies = fetch(refs[:10], refs[17:27], refs[27])
    core = lax.axis_index("strip") & 1
    group = lax.axis_index("traj")
    for copy in copies:
        copy.wait()
    for i in range(STEPS):
        flags[i] = jnp.full((8, N), jnp.where(lengths[core] > i, 1.0, 0.0), f32)
    flags[STEPS] = jnp.full((8, N), jnp.where(core == 0, 1.0, 0.0), f32)
    for bit in range(flags.shape[0] - STEPS - 1):
        flags[STEPS + 1 + bit] = jnp.full((8, N), jnp.where((group >> bit) & 1 == 1, 1.0, 0.0), f32)
    own[0] = jnp.where(core == 0, vel[0], vel[1])
    own[1] = jnp.where(core == 0, cot[0], cot[1])
    zero = jnp.zeros((CH, CH), bf16)
    for m in range(LAYERS):
        tap = tap_of(middle, last, m)
        for two in range(2):
            for e in range(3):
                taps = [tap(q - two, e) if 0 <= q - two < 3 else zero for q in range(4)]
                f_hidden[m, (two * 3 + e) * CH : (two * 3 + e + 1) * CH, :] = jnp.concatenate(taps, axis=1)
    for two in range(2):
        lines = []
        for ch in range(2):
            for i in range(4):
                for j in range(4):
                    if 0 <= i - two < 3 and j < 3:
                        lines.append(first[3 * (i - two) + j, ch : ch + 1, :].astype(f32))
                    else:
                        lines.append(jnp.zeros((1, CH), f32))
        f_first[two * CH : (two + 1) * CH, :] = jnp.concatenate(lines, axis=0).T.astype(bf16)
    for m in range(LAYERS + 1):
        if 0 < m < LAYERS:
            line = middle_bias[m - 1 : m, :]
        else:
            line = (first_bias if m == 0 else last_bias)[...].reshape(1, CH)
        bias[m] = jnp.broadcast_to(line, (N, CH)).T
    mix[...] = tables[2, 0:48, 0:64].astype(bf16)
    adder[...] = tables[2, 64:80, :].astype(bf16)


def prepare_back_kernel(*refs):
    b_first, b_hidden, right, left, weight = refs[5:10]
    first, middle, last, tables = refs[10:14]
    copies = fetch(refs[:4], refs[10:14], refs[14])
    for copy in copies:
        copy.wait()
    zero = jnp.zeros((CH, CH), bf16)
    for m in range(LAYERS):
        tap = tap_of(middle, last, m)
        for two in range(2):
            for e in range(3):
                taps = [tap(2 - q + two, 2 - e) if 0 <= q - two < 3 else zero for q in range(4)]
                b_hidden[m, (two * 3 + e) * CH : (two * 3 + e + 1) * CH, :] = jnp.concatenate(
                    [jnp.concatenate(taps[:2], axis=0).T, jnp.concatenate(taps[2:], axis=0).T], axis=1
                )
    lines = jnp.zeros((1, CH), f32)
    taps = []
    for e in range(3):
        for ch in range(2):
            for two in range(2):
                line = [
                    first[3 * (2 - q + two) + 2 - e, ch : ch + 1, :].astype(f32) if 0 <= q - two < 3 else lines
                    for q in range(4)
                ]
                taps.append(jnp.concatenate(line, axis=1))
    taps.append(jnp.zeros((4, 4 * CH), f32))
    b_first[...] = jnp.concatenate(taps, axis=0).astype(bf16)
    high, low = split(tables[0])
    right[...] = jnp.concatenate([high, high, low], axis=0)
    left[...] = jnp.concatenate([high, low, high], axis=1)
    weight[...] = tables[1]


def chosen(flag, x, y):
    flag = flag[0:1, :] > 0.5
    return jnp.where(jnp.broadcast_to(flag, x.shape), x, y)


def assemble_kernel(flags, own, partner, cross, same, cot_partner, ext, cot):
    upper = flags[STEPS]

    def pair(mine, other, i):
        other = chosen(upper, other[0, i], other[1, i])
        return [chosen(upper, mine[i], other), chosen(upper, other, mine[i])]

    for i in range(2):
        above = chosen(upper, cross[0, i], same[1, i])[-MARGIN:]
        below = chosen(upper, same[0, i], cross[1, i])[:MARGIN]
        ext[i] = jnp.concatenate([above, *pair(own[0], partner, i), below], axis=0)
        cot[i] = jnp.concatenate(pair(own[1], cot_partner, i), axis=0)


def network_kernel(count, vel, extra, w_first, w_hidden, bias, mix, adder, *refs):
    block, refs = refs[0], refs[1:]
    messages = refs[:-8]
    interp, raw, clear, fields, feats, slopes, put, kept = refs[-8:]
    interleave(vel, fields)
    clear_patches(count, fields, mix, clear, put)
    sums = []

    def raw_done(r, value):
        sums.append(point_sums(r, value, clear))
        if len(sums) == 4 * LAG + 4:
            interpolate(r + 1 - len(sums), sums[:4], adder, put, interp)
            del sums[:4]

    network_forward(count, fields, w_first, w_hidden, bias, feats, slopes, raw, raw_done, kept)
    for i in range(0, len(sums), 4):
        interpolate(count + RAW - len(sums) + i, sums[i : i + 4], adder, put, interp)
    su, sv = provisional(count, vel[0], vel[1], interp)
    out = [su, sv, extra[0], extra[1]]
    for i in range(4):
        block[i] = out[i]
    if messages:
        write_messages(out, *messages)


def project_kernel(count, blocks, steps, flags, *refs):
    block, messages, refs = refs[0], refs[1:blocks], refs[blocks:]
    forward, backward = steps
    mg = flags[backward][0:1, :]
    fields = [[mg * x for x in read_messages(1, block, messages)]]
    if forward is None:
        right, left, weight, gstar, own = refs
    else:
        vel, right, left, weight, gstar, own, ext = refs
        fields.append(read_messages(0, block, messages))
        mv = flags[forward][0:1, :]
    out = project(fields, count, right, left, weight)
    for i in range(2):
        gstar[i] = out[0][i]
        own[i] = (1.0 - mg) * block[2 + i]
        if forward is not None:
            ext[i] = vel[i] + mv * (out[1][i] - vel[i])


def static(start, size):
    return slice(start, start + size)


def back_kernel(count, ext, gstar, clear, b_first, b_hidden, slopes, *refs):
    if len(refs) == 6:
        mix, raw, grads, gvel, spread, ginterp = refs
    else:
        grads, first, ginterp = refs
    interp_gradients(count, gstar[0], gstar[1], ext[0], ext[1], ginterp)
    raw_gradient(count, clear, ginterp, grads)
    tasks = []
    if len(refs) == 6:
        columns = put_columns()
        for r in range(-RAW, count + RAW, 2):
            tasks.append(functools.partial(spread_back, r, static, columns, mix, raw, ginterp, spread))
    turn = [0]

    def between():
        turn[0] += 1
        if tasks and turn[0] % 3 == 0:
            tasks.pop(0)()

    network_backward(count, b_hidden, slopes, grads, between, None if len(refs) == 6 else first)
    for task in tasks:
        task()
    if len(refs) == 6:
        input_gradient(count, b_first, gradient_window(grads, count, 1), gvel)


def finish_kernel(count, front, base, gstar, interp, gvel, spread, block, top, bottom, far, lines):
    change = velocity_gradients(count, gstar[0], gstar[1], interp, spread, lines)
    out = [front[0], front[1]] + [base[i] + change[i] + gvel[i] for i in range(2)]
    for i in range(4):
        block[i] = out[i]
    write_messages(out, top, bottom, far)


def last_kernel(count, blocks, flags, *refs):
    block, messages, refs = refs[0], refs[1:blocks], refs[blocks:]
    now, right, left, weight, base, ext, gstar, interp, first, b_first, mix, raw, out = refs[:13]
    lines, spread, ginterp, gvel = refs[13:]
    (news,) = project([read_messages(0, block, messages)], count, right, left, weight)
    own = slice(MARGIN, MARGIN + count)
    mask = flags[STEPS - 1][0:1, :]
    for i in range(2):
        out[i] = now[i, own] + mask * (news[i][own] - now[i, own])
    gu, gv = gstar[0], gstar[1]
    input_gradient(count, b_first, lambda r: first[r * CH : (r + 4) * CH, :], gvel)
    interp_gradients(count, gu, gv, ext[0], ext[1], ginterp)
    columns = put_columns()

    def at(start, size):
        return pl.ds(pl.multiple_of(start, size), size) if size > 1 else pl.ds(start, size)

    def step(i, _):
        for k in range(2):
            spread_back(4 * i + 2 * k - RAW, at, columns, mix, raw, ginterp, spread)
        return 0

    lax.fori_loop(0, (count + 2 * RAW) // 4, step, 0)
    change = velocity_gradients(count, gu, gv, interp, spread, lines)
    for i in range(2):
        out[2 + i] = base[i] + change[i] + gvel[i]


def weights_kernel(count, fields, feats, grads, buffer, extra):
    for half in range(2):

        def put(q, value, half=half):
            buffer[place(half * HALF + q * 3 * CH, 3 * CH), :] = value

        weight_half(count, half, fields, feats, grads, put, extra)


def half_kernel(count, side, previous, fields, feats, grads, out, extra):
    half = (lax.axis_index("strip") & 1) ^ side

    def put(q, value):
        value = value + previous[place(half * HALF + q * 3 * CH, 3 * CH), :]
        out[q * 3 * CH : (q + 1) * 3 * CH, :] = value.astype(bf16)

    weight_half(count, half, fields, feats, grads, put, extra)
    if out.shape[0] > HALF:
        out[HALF:, :] = jnp.zeros((out.shape[0] - HALF, N), bf16)


def exchanged(flags, blocks):
    for bit in range(len(blocks).bit_length() - 1):
        flag = flags[STEPS + 1 + bit]
        blocks = [chosen(flag, blocks[i ^ (1 << bit)], x) for i, x in enumerate(blocks)]
    return blocks


def halves_kernel(flags, keep, received, *out):
    rows_each = out[0].shape[0]
    blocks = []
    for i in range(len(out)):
        at = slice(i * rows_each, (i + 1) * rows_each)
        blocks.append(keep[at, :].astype(f32) + received[at, :].astype(f32))
    for ref, x in zip(out, exchanged(flags, blocks)):
        ref[...] = x.astype(bf16)


def arrange_kernel(flags, *refs):
    *blocks, out = refs
    rows_each = blocks[0].shape[0]
    for i, x in enumerate(exchanged(flags, [x[...].astype(f32) for x in blocks])):
        out[i * rows_each : (i + 1) * rows_each, :] = x.astype(bf16)


def unpack_kernel(flags, mine, other, first, first_bias, middle, middle_bias, last, last_bias):
    for half in range(2):
        a, b = (mine, other) if half == 0 else (other, mine)
        blocks = []
        for q in range(5):
            at = slice(q * 3 * CH, (q + 1) * 3 * CH)
            blocks.append(chosen(flags[STEPS], a[at, :].astype(f32), b[at, :].astype(f32)))
        wide = jnp.concatenate(blocks, axis=1)
        turned = [blocks[4][two * CH : (two + 1) * CH].T[CH:] for two in range(2)]
        for i in range(3):
            m = 3 * half + i
            for a in range(3):
                part = wide[:, (3 * i + a) * CH : (3 * i + a + 1) * CH]
                for e in range(3):
                    value = part[e * CH : (e + 1) * CH]
                    if m < LAYERS - 1:
                        middle[m, 3 * a + e] = value
                    else:
                        last[3 * a + e] = value
            if m < LAYERS - 1:
                middle_bias[m : m + 1, :] = turned[0][32 + i : 33 + i]
            else:
                last_bias[...] = turned[0][32 + i]
    first_bias[...] = turned[0][35]
    for a in range(3):
        for e in range(3):
            for ch in range(2):
                low, high = 16 * ch + 4 * a + e, 16 * ch + 4 * (a + 1) + e
                first[3 * a + e, ch : ch + 1, :] = turned[0][low : low + 1] + turned[1][high : high + 1]


VMEM = pl.BlockSpec(memory_space=pltpu.VMEM)
SMEM = pl.BlockSpec(memory_space=pltpu.SMEM)
PARAMS = pltpu.CompilerParams(vmem_limit_bytes=VMEM_BYTES)


def array(dtype, *shape):
    return jax.ShapeDtypeStruct(shape, dtype)


def cost(flops, moved):
    return pl.CostEstimate(flops=flops, bytes_accessed=moved, transcendentals=0)


def field(count, *lead):
    return pltpu.VMEM(lead + (count, N), f32)


def feature_array(count):
    return array(bf16, LAYERS * (count + 24) * CH, N)


def gradient_array(count, slots):
    return array(bf16, slots * (count + 16) * CH, N)


def call(kernel, name, flops, inputs, out, scratch=()):
    return pl.pallas_call(
        kernel,
        in_specs=[VMEM] * len(inputs),
        out_specs=jax.tree.map(lambda _: VMEM, out),
        out_shape=out,
        scratch_shapes=list(scratch),
        compiler_params=PARAMS,
        cost_estimate=cost(flops, 10**6),
        name=name,
    )(*inputs)


def run_prepare(lengths, vel, cot, params, bits):
    out = [
        array(f32, 2, 2, vel.shape[2], N),
        array(bf16, 2 * CH, 32),
        array(bf16, LAYERS, 6 * CH, 4 * CH),
        array(f32, LAYERS + 1, CH, N),
        array(bf16, 48, 64),
        array(bf16, 16, N),
        array(f32, STEPS + 1 + bits, 8, N),
    ]
    inputs = [vel, cot, *params, jnp.asarray(constant_tables(N)), lengths]
    scratch = [pltpu.VMEM(x.shape, x.dtype) for x in inputs[:-1]] + [pltpu.SMEM(lengths.shape, lengths.dtype)]
    return call_from_hbm(prepare_kernel, "prepare", inputs, out, scratch)


def run_prepare_back(params, after):
    first, _, middle, _, last, _ = params
    out = [
        array(bf16, 16, 4 * CH),
        array(bf16, LAYERS, 6 * CH, 4 * CH),
        array(bf16, 3 * N, N),
        array(bf16, N, 3 * N),
        array(f32, N, N),
    ]
    inputs = [first, middle, last, jnp.asarray(constant_tables(N))]
    scratch = [pltpu.VMEM(x.shape, x.dtype) for x in inputs]
    b_first, b_hidden, *tables = call_from_hbm(prepare_back_kernel, "prepare_back", inputs, out, scratch, after)
    return b_first, b_hidden, tables


def call_from_hbm(kernel, name, inputs, out, scratch, *after):
    hbm = pl.BlockSpec(memory_space=pltpu.HBM)
    inputs = [pltpu.with_memory_space_constraint(x, pltpu.HBM) for x in inputs]
    return pl.pallas_call(
        kernel,
        in_specs=[hbm] * len(inputs) + [VMEM] * len(after),
        out_specs=[VMEM] * len(out),
        out_shape=out,
        scratch_shapes=scratch + [pltpu.SemaphoreType.DMA((len(inputs),))],
        compiler_params=PARAMS,
        cost_estimate=cost(10**9, 10**6),
        name=name,
    )(*inputs, *after)


def message_arrays(count):
    near = 4 * MARGIN + 2 * (count - MARGIN) + 8
    return [array(f32, near, N), array(f32, near, N), array(f32, 2 * count + 8, N)]


def run_assemble(count, flags, fields):
    out = [array(f32, 2, count + 2 * MARGIN, N), array(f32, 2, count, N)]
    return call(assemble_kernel, "assemble", 10**6, [flags, *fields], out)


def run_network(count, vel, extra, weights, last=False):
    local_rows, mid = count + 2 * MARGIN, count + 2 * MID
    out = [array(f32, 4, count, N), *([] if last else message_arrays(count)), array(f32, 4 * mid, N), array(f32, mid * CH, N), array(f32, mid * 32, N)]
    out += [array(f32, 2, 4 * local_rows, N)]
    out += [feature_array(count), gradient_array(count, LAYERS)]
    scratch = [field(4 * mid), field((count + 2 * LAYERS) * CH, 2)]
    return call(functools.partial(network_kernel, count), "network", 4 * 10**9, [vel, extra, *weights], out, scratch)


def run_project(count, steps, flags, gathered, tables, *vel):
    local_rows = count + 2 * MARGIN
    out = [array(f32, 2, local_rows, N), array(f32, 2, count, N)]
    if vel:
        out.append(array(f32, 2, local_rows, N))
    kernel = functools.partial(project_kernel, count, len(gathered), steps)
    return call(kernel, "project", 10**9, [flags, *gathered, *vel, *tables], out)


def run_back(count, ext, gstar, clear, b_first, b_hidden, slopes, *more):
    mid = count + 2 * MID
    inputs = [ext, gstar, clear, b_first, b_hidden, slopes, *more]
    out = [gradient_array(count, LAYERS + 1)]
    if more:
        out += [array(f32, 2, count, N), array(f32, 2, 4, 4 * mid, N)]
    else:
        out.append(array(bf16, (count + 2) * CH, N))
    return call(functools.partial(back_kernel, count), "back", 4 * 10**9, inputs, out, [field(mid, 4)])


def run_finish(count, *inputs):
    kernel = functools.partial(finish_kernel, count)
    out = [array(f32, 4, count, N), *message_arrays(count)]
    return call(kernel, "finish", 10**9, inputs, out, [field(4 * count, 2)])


def run_last(count, flags, gathered, *inputs):
    mid = count + 2 * MID
    scratch = [field(4 * count, 2), field(4 * mid, 2, 4), field(mid, 4), field(count, 2)]
    kernel = functools.partial(last_kernel, count, len(gathered))
    return call(kernel, "last", 10**9, [flags, *gathered, *inputs], array(f32, 4, count, N), scratch)


def run_weights(count, fields, feats, grads):
    kernel = functools.partial(weights_kernel, count)
    return call(kernel, "weights", 3 * 10**9, [fields, feats, grads], array(f32, 2 * HALF, N), [field(3 * CH)])


def run_half(count, side, rows, previous, fields, feats, grads, *after):
    inputs = [previous, fields, feats, grads, *after]
    kernel = functools.partial(half_kernel, count, side)
    if after:
        kernel = lambda *refs: half_kernel(count, side, *refs[:4], *refs[5:])
    return call(kernel, "half", 10**9, inputs, array(bf16, rows, N), [field(3 * CH)])


def run_halves(flags, keep, received, parts):
    out = [array(bf16, keep.shape[0] // parts, N)] * parts
    return call(halves_kernel, "halves", 10**6, [flags, keep, received], out)


def run_arrange(flags, blocks):
    out = array(bf16, len(blocks) * blocks[0].shape[0], N)
    return call(arrange_kernel, "arrange", 10**6, [flags, *blocks], out)


def run_unpack(flags, mine, other):
    out = [
        array(f32, 9, 2, CH),
        array(f32, CH),
        array(f32, LAYERS - 1, 9, CH, CH),
        array(f32, LAYERS - 1, CH),
        array(f32, 9, CH, CH),
        array(f32, CH),
    ]
    return call(unpack_kernel, "unpack", 10**7, [flags, mine, other], out)


def swap(x, axis, offset):
    count = lax.axis_size(axis)
    return lax.ppermute(x, axis, [(i, i ^ offset) for i in range(count)])


def from_group(x, ahead):
    count = lax.axis_size("strip")
    return lax.ppermute(x, "strip", [(i, (i - 2 * ahead) % count) for i in range(count)])


def gather_groups(block, top, bottom, far):
    groups = lax.axis_size("strip") // 2
    others = [from_group(far, k) for k in range(2, groups - 1)]
    return [block, from_group(top, 1), *others, from_group(bottom, -1)]


def margins(velocity, partner, core):
    count = lax.axis_size("strip")
    if velocity.shape[2] < MARGIN:
        upper = core[0] == 0
        pair = jnp.where(
            upper,
            jnp.concatenate([velocity[0], partner[0]], axis=1),
            jnp.concatenate([partner[1], velocity[1]], axis=1),
        )
        above, below = from_group(pair[:, -MARGIN:], -1), from_group(pair[:, :MARGIN], 1)
        return jnp.stack([above, below]), jnp.stack([below, above])
    cross = [(i, (i - 1) % count if i % 2 == 0 else (i + 1) % count) for i in range(count)]
    same = [(i, (i - 2) % count if i % 2 == 0 else (i + 2) % count) for i in range(count)]
    return lax.ppermute(velocity, "strip", cross), lax.ppermute(velocity, "strip", same)


def sum_everywhere(keep, received, flags):
    parts = lax.axis_size("traj")
    groups = lax.axis_size("strip") // 2
    blocks = run_halves(flags, keep, received, parts)
    total = blocks[0].astype(f32)
    for k in range(1, parts):
        total = total + swap(blocks[k], "traj", k).astype(f32)
    x = total.astype(bf16)
    total = x.astype(f32)
    for k in range(1, groups):
        total = total + swap(x, "strip", 2 * k).astype(f32)
    x = total.astype(bf16)
    x = run_arrange(flags, [x] + [swap(x, "traj", k) for k in range(1, parts)])
    return x, swap(x, "strip", 1)


def per_device(
    velocity, lengths, cotangent, first_kernel, first_bias, middle_kernels, middle_biases, last_kernel, last_bias
):
    rc = velocity.shape[2]
    count = 2 * rc
    index = lax.axis_index("strip") & 1
    core = index[None]
    pick = lambda y, i: lax.dynamic_index_in_dim(y, i, 0, False)

    partner = swap(velocity, "strip", 1)
    cross, same = margins(velocity, partner, core)
    cot_partner = swap(cotangent, "strip", 1)
    first_kernel = first_kernel.transpose(0, 2, 1)
    params = (first_kernel, first_bias, middle_kernels, middle_biases, last_kernel, last_bias)
    parts = lax.axis_size("traj")
    half_rows = -(-HALF // (parts * 16)) * parts * 16
    own, w_first, w_hidden, bias, mix, adder, flags = run_prepare(
        lengths, velocity, cotangent, params, parts.bit_length() - 1
    )
    weights = (w_first, w_hidden, bias, mix, adder)

    v0, cot = run_assemble(count, flags, (own, partner, cross, same, cot_partner))
    block, *sent, interp0, raw0, clear0, fields0, feats0, slopes0 = run_network(count, v0, cot, weights)
    gathered = gather_groups(block, *sent)
    b_first, b_hidden, tables = run_prepare_back(params, interp0)
    gstar1, base, v1 = run_project(count, (0, 1), flags, gathered, tables, v0)
    block, interp1, raw1, clear1, fields1, feats1, slopes1 = run_network(count, v1, cot, weights, last=True)
    grads1, gvel, spread = run_back(count, v1, gstar1, clear1, b_first, b_hidden, slopes1, mix, raw1)
    gathered = gather_groups(*run_finish(count, block, base, gstar1, interp1, gvel, spread))
    buffer = run_weights(count, fields1, feats1, grads1)
    gstar0, base = run_project(count, (None, 0), flags, gathered, tables)
    grads0, first = run_back(count, v0, gstar0, clear0, b_first, b_hidden, slopes0)
    send = run_half(count, 1, half_rows, buffer, fields0, feats0, grads0)
    received = swap(send, "strip", 1)
    keep = run_half(count, 0, half_rows, buffer, fields0, feats0, grads0, send)
    out = run_last(
        count, flags, gathered, v1, *tables, base, v0, gstar0, interp0, first, b_first, mix, raw0
    )

    strips = out.reshape(4, 2, rc, N).transpose(1, 0, 2, 3)
    mine, other = pick(strips, index)[None], swap(pick(strips, 1 - index), "strip", 1)[None]
    out = jnp.where(
        index == 0, jnp.concatenate([mine, other], axis=0), jnp.concatenate([other, mine], axis=0)
    )
    mine, other = sum_everywhere(keep, received, flags)
    grad_first, *rest = run_unpack(flags, mine, other)
    return (out[:, :2], out[:, 2:], grad_first.transpose(0, 2, 1), *rest)


def solution(mesh):
    band = P("traj", None, "strip", None)
    return jax.shard_map(
        per_device,
        mesh=mesh,
        in_specs=(band, P("traj"), band) + (P(),) * 6,
        out_specs=(band, band) + (P(),) * 6,
        check_vma=False,
    )
```

```python
import functools
import math

import jax
import jax.numpy as jnp
import numpy as np
from jax import lax
from jax.experimental import pallas as pl
from jax.experimental.pallas import tpu as pltpu
from jax.sharding import PartitionSpec as P

STEPS = 2
DT = 0.25
MARGIN = 16
MID = 8
LAG = 3
RAW = 2
CH = 64
LAYERS = 6
N = 128
HALF = 15 * CH
bf16 = jnp.bfloat16
f32 = jnp.float32
NT = (((1,), (1,)), ((), ()))
VMEM_BYTES = 14 * 2**20


def reach(layer):
    return 12 - layer


def place(start, size):
    return slice(start, start + size) if isinstance(start, int) else pl.ds(pl.multiple_of(start, CH), size)


def feature_rows(count, layer, r, rows=1):
    return place(((layer - 1) * (count + 24) + r + 12) * CH, rows * CH)


def gradient_rows(count, layer, r, rows=1):
    return place(((layer - 1) * (count + 16) + r + 8) * CH, rows * CH)


def lanes(x, s):
    return x if s == 0 else pltpu.roll(x, (-s) % x.shape[1], 1)


def rows(x, s):
    return x if s == 0 else pltpu.roll(x, (-s) % x.shape[0], 0)


TARGETS = ((0.0, -0.5), (-0.5, 0.0), (0.0, -0.5), (-0.5, 0.0))
POINTS = np.arange(16)
PX, PY = POINTS % 4 - 1.5, POINTS // 4 - 1.5
TAKEN = 5.0 + 4.0 * (PX[:, None] * PX[None, :] + PY[:, None] * PY[None, :])
PUT = [5.0 + 4.0 * (tx * PX + ty * PY) for tx, ty in TARGETS]


def constant_tables(length):
    k = np.arange(length)
    angle = 2.0 * math.pi * ((k[:, None] * k[None, :]) % length) / length
    table = (np.cos(angle) + np.sin(angle)) / math.sqrt(length)
    eigen = 2.0 - 2.0 * np.cos(2.0 * math.pi * k / length)
    total = eigen[:, None] + eigen[None, :]
    total[0, 0] = 1.0
    weight = 1.0 / total
    weight[0, 0] = 0.0
    small = np.zeros((length, length))
    for part in range(2):
        for which in range(2):
            cols = slice(32 * which + 16 * part, 32 * which + 16 * part + 16)
            small[16 * which : 16 * which + 16, cols] = TAKEN
            small[32 + 2 * which, cols] = PUT[2 * which]
            small[33 + 2 * which, cols] = PUT[2 * which + 1]
        for i in range(8):
            small[64 + i, 64 * part + 8 * i : 64 * part + 8 * i + 8] = 1.0
    return np.stack([table, weight, small]).astype(np.float32)


def split(x):
    high = x.astype(bf16)
    return high, (x - high.astype(f32)).astype(bf16)


def times_right(x, right):
    high, low = split(x)
    return jnp.dot(jnp.concatenate([high, low, high], axis=1), right[...], preferred_element_type=f32)


def times_left(x, left):
    high, low = split(x)
    return jnp.dot(left[...], jnp.concatenate([high, high, low], axis=0), preferred_element_type=f32)


def local(x, count):
    return jnp.concatenate([x[N - MARGIN :], x[: count + MARGIN]], axis=0)


def with_row_above(v, above):
    first = lax.broadcasted_iota(jnp.int32, v.shape, 0) == 0
    return jnp.where(first, jnp.broadcast_to(above, v.shape), rows(v, -1))


def divergence(u, v, above):
    return u - lanes(u, -1) + (v - with_row_above(v, above))


def write_messages(kind, u, v, top, bottom, far):
    count = u.shape[0]
    rest = count - MARGIN
    fields = 4 * MARGIN
    source = divergence(u, v, jnp.zeros((1, N), f32))
    for i, x in enumerate((u, v)):
        at = slice((2 * kind + i) * MARGIN, (2 * kind + i + 1) * MARGIN)
        top[at, :] = x[:MARGIN]
        bottom[at, :] = x[rest:]
    if rest:
        at = slice(fields + kind * rest, fields + (kind + 1) * rest)
        top[at, :] = source[MARGIN:]
        bottom[at, :] = source[:rest]
        bottom[fields + 2 * rest + kind : fields + 2 * rest + kind + 1, :] = v[rest - 1 : rest]
    top[fields + 2 * rest + kind : fields + 2 * rest + kind + 1, :] = v[count - 1 :]
    far[kind * count : (kind + 1) * count, :] = source
    far[2 * count + kind : 2 * count + kind + 1, :] = v[count - 1 :]


def read_messages(kind, block, messages):
    count = block.shape[1]
    rest = count - MARGIN
    top, far, bottom = messages[0], messages[1:-1], messages[-1]
    cut = lambda ref, start, size: ref[start : start + size, :]
    u, v = block[2 * kind], block[2 * kind + 1]
    top_u, top_v = [cut(top, (2 * kind + i) * MARGIN, MARGIN) for i in range(2)]
    low_u, low_v = [cut(bottom, (2 * kind + i) * MARGIN, MARGIN) for i in range(2)]
    source = [divergence(u, v, low_v[MARGIN - 1 :]), divergence(top_u, top_v, v[count - 1 :])]
    fields = 4 * MARGIN
    last = top_v[MARGIN - 1 :]
    if rest:
        source.append(cut(top, fields + kind * rest, rest))
        last = cut(top, fields + 2 * rest + kind, 1)
    first = lax.broadcasted_iota(jnp.int32, (count, N), 0) == 0
    for ref in far:
        x = cut(ref, kind * count, count)
        source.append(x - jnp.where(first, jnp.broadcast_to(last, x.shape), 0.0))
        last = cut(ref, 2 * count + kind, 1)
    if rest:
        x = cut(bottom, fields + kind * rest, rest)
        source.append(x - jnp.where(first[:rest], jnp.broadcast_to(last, x.shape), 0.0))
        last = cut(bottom, fields + 2 * rest + kind, 1)
    source.append(divergence(low_u, low_v, last))
    return [
        jnp.concatenate([low_u, u, top_u], axis=0),
        jnp.concatenate([low_v, v, top_v], axis=0),
        jnp.concatenate(source, axis=0),
    ]


def project(fields, count, right, left, weight):
    number = len(fields)
    x = times_right(jnp.concatenate([source for _, _, source in fields], axis=0), right)
    x = jnp.concatenate([x[i * N : (i + 1) * N] for i in range(number)], axis=1)
    x = times_left(x, left) * jnp.concatenate([weight[...]] * number, axis=1)
    x = local(times_left(x, left), count)
    size = x.shape[0]
    x = times_right(jnp.concatenate([x[:, i * N : (i + 1) * N] for i in range(number)], axis=0), right)
    out = []
    for i, (u, v, _) in enumerate(fields):
        p = -x[i * size : (i + 1) * size]
        out.append((u - (lanes(p, 1) - p), v - (rows(p, 1) - p)))
    return out


def fold(o):
    third = o.shape[0] // 3
    return lanes(o[:third], -1) + o[third : 2 * third] + lanes(o[2 * third :], 1)


def fold_rounded(o):
    third = o.shape[0] // 3
    left, right = lanes(o[:third].astype(bf16), -1), lanes(o[2 * third :].astype(bf16), 1)
    return left.astype(f32) + o[third : 2 * third] + right.astype(f32)


def conv_rows(window, kernel, low, high, emit, between=lambda: None):
    starts = list(range(low, high, 2))
    for k in range(0, len(starts), 2):
        group = starts[k : k + 2]
        o = jnp.dot(
            kernel[...],
            jnp.concatenate([window(r) for r in group], axis=1),
            preferred_element_type=f32,
        )
        half = o.shape[0] // 2
        for i, r in enumerate(group):
            part = o[:, i * N : (i + 1) * N]
            emit(r, part[:half])
            emit(r + 1, part[half:])
        between()


def first_window(fields, r):
    a = 4 * (r - 1 + MARGIN)
    return jnp.concatenate([fields[0, a : a + 16, :], fields[1, a : a + 16, :]], axis=0).astype(bf16)


def feature_window(feats, count, layer):
    return lambda r: feats[feature_rows(count, layer, r - 1, 4), :]


def gradient_window(grads, count, layer):
    return lambda r: grads[gradient_rows(count, layer, r - 1, 4), :]


def gelu_value(z):
    c = math.sqrt(2.0 / math.pi)
    zz = z * z
    h = 0.5 + 0.5 * jnp.tanh(z * (c + (c * 0.044715) * zz))
    return z * h, h, zz


def gelu_slope(f, h, zz):
    c = math.sqrt(2.0 / math.pi)
    return h + (f - f * h) * (2.0 * c + (6.0 * c * 0.044715) * zz)


def network_forward(count, fields, w_first, w_hidden, bias, feats, slopes, raw, raw_done, kept):
    tasks = []

    def slope_later(r, at):
        z, h = kept[0, at, :], kept[1, at, :]
        slopes[gradient_rows(count, LAYERS, r), :] = gelu_slope(z * h, h, z * z).astype(bf16)

    for m in range(1, LAYERS + 1):

        def emit(r, o, m=m):
            z = (o if m == 1 else fold(o)) + bias[m - 1]
            value, h, zz = gelu_value(z)
            feats[feature_rows(count, m, r), :] = value.astype(bf16)
            if m == LAYERS:
                at = slice((r + m) * CH, (r + m + 1) * CH)
                kept[0, at, :] = z
                kept[1, at, :] = h
                tasks.append(functools.partial(slope_later, r, at))
            elif -m <= r < count + m:
                slopes[gradient_rows(count, m, r), :] = gelu_slope(value, h, zz).astype(bf16)

        low, high = -reach(m), count + reach(m)
        if m == 1:
            conv_rows(functools.partial(first_window, fields), w_first, low, high, emit)
        else:
            conv_rows(feature_window(feats, count, m - 1), w_hidden.at[m - 2], low, high, emit)

    def emit_raw(r, o):
        value = fold(o) + bias[LAYERS]
        raw[(r + MID) * CH : (r + MID + 1) * CH, :] = value
        raw_done(r, value)

    groups = (count + 2 * RAW) // 4
    share = -(-len(tasks) // groups)

    def between():
        for task in tasks[:share]:
            task()
        del tasks[:share]

    window = feature_window(feats, count, LAYERS)
    conv_rows(window, w_hidden.at[LAYERS - 1], -RAW, count + RAW, emit_raw, between)
    for task in tasks:
        task()


def interleave(vel, fields):
    for which in range(2):
        x = vel[which]
        for j in range(4):
            fields[which, pl.ds(j, x.shape[0], stride=4), :] = lanes(x, j - 1)


def mixed(pairs, mix):
    cols = []
    for u, v in pairs:
        cols.append(jnp.concatenate([*split(u), *split(v)], axis=0))
    o = jnp.dot(mix[...], jnp.concatenate(cols, axis=1), preferred_element_type=f32)
    return [o[:, i * N : (i + 1) * N] * (1.0 / 80.0) for i in range(len(pairs))]


def clear_patches(count, fields, mix, clear, put):
    for r in range(-MID, count + MID, 2):
        pairs = []
        for k in range(2):
            a = 4 * (r + k - 1 + MARGIN)
            pairs.append((fields[0, a : a + 16, :], fields[1, a : a + 16, :]))
        parts = mixed(pairs, mix)
        for k, ((u, v), o) in enumerate(zip(pairs, parts)):
            a = 32 * (r + k + MID)
            clear[a : a + 16, :] = u - o[0:16]
            clear[a + 16 : a + 32, :] = v - o[16:32]
        a = 4 * (r + MID)
        put[a : a + 8, :] = jnp.concatenate([parts[0][32:36], parts[1][32:36]], axis=0)


def point_sums(r, value, clear):
    a = 32 * (r + MID)
    out = []
    for k in range(4):
        b = a + 16 * (k // 2)
        x = value[16 * k : 16 * k + 16] * clear[b : b + 16, :]
        out.append(x[:8] + x[8:])
    return out


def interpolate(r, sums, adder, put, interp):
    cols = []
    for i in range(0, len(sums), 2):
        high, low = split(jnp.concatenate(sums[i] + sums[i + 1], axis=0))
        cols.append(jnp.concatenate([high, low], axis=0))
    o = jnp.dot(adder[...], jnp.concatenate(cols, axis=1), preferred_element_type=f32)
    for i in range(len(cols)):
        a = 4 * (r + 2 * i + MID)
        interp[a : a + 8, :] = o[0:8, i * N : (i + 1) * N] + put[a : a + 8, :]


def by_kind(interp, k, mid):
    return interp[pl.ds(k, mid, stride=4), :]


def raw_gradient(count, clear, ginterp, grads):
    for r in range(-MID, count + MID):
        a = 32 * (r + MID)
        parts = []
        for k in range(4):
            b = a + 16 * (k // 2)
            parts.append(clear[b : b + 16, :] * ginterp[k, r + MID : r + MID + 1, :])
        grads[gradient_rows(count, LAYERS + 1, r), :] = jnp.concatenate(parts, axis=0).astype(bf16)


def put_columns():
    point = lax.broadcasted_iota(jnp.int32, (16, N), 0)
    px, py = (point & 3).astype(f32) - 1.5, (point >> 2).astype(f32) - 1.5
    return [(1.0 / 16.0) + (tx / 20.0) * px + (ty / 20.0) * py for tx, ty in TARGETS]


def spread_back(r, at, columns, mix, raw, ginterp, spread):
    pairs, gs = [], []
    for k in range(2):
        z = raw[at((r + k + MID) * CH, CH), :]
        g = [ginterp[i, at(r + k + MID, 1), :] for i in range(4)]
        x = [z[16 * i : 16 * i + 16] * g[i] for i in range(4)]
        pairs.append((x[0] + x[1], x[2] + x[3]))
        gs.append(g)
    parts = mixed(pairs, mix)
    for which in range(2):
        out = []
        for pair, o, g in zip(pairs, parts, gs):
            back = columns[2 * which] * g[2 * which] + columns[2 * which + 1] * g[2 * which + 1]
            out.append(pair[which] - o[16 * which : 16 * which + 16] + back)
        for i in range(4):
            spread[which, i, at(4 * (r + MID), 8), :] = jnp.concatenate(
                [x[4 * i : 4 * i + 4] for x in out], axis=0
            )


def gathered_back(count, spread, lines):
    out = []
    for which in range(2):
        for r in range(0, count, 2):
            total = None
            for i in range(4):
                a = 4 * (r + 1 - i + MID)
                x = spread[which, i, a : a + 8, :]
                total = x if total is None else total + x
            lines[which, 4 * r : 4 * r + 8, :] = total
        total = None
        for j in range(4):
            x = lanes(lines[which, pl.ds(j, count, stride=4), :], 1 - j)
            total = x if total is None else total + x
        out.append(total)
    return out


def carriers(u, v):
    return (
        0.5 * (u + lanes(u, 1)),
        0.5 * (v + lanes(v, 1)),
        0.5 * (u + rows(u, 1)),
        0.5 * (v + rows(v, 1)),
    )


def middle(x, count):
    return x[MARGIN - MID : MARGIN + MID + count]


def provisional(count, u, v, interp):
    mid = count + 2 * MID
    flux = [middle(x, count) * by_kind(interp, k, mid) for k, x in enumerate(carriers(u, v))]
    u, v = middle(u, count), middle(v, count)
    su = u - DT * (flux[0] - lanes(flux[0], -1) + (flux[1] - rows(flux[1], -1)))
    sv = v - DT * (flux[2] - lanes(flux[2], -1) + (flux[3] - rows(flux[3], -1)))
    return su[MID : MID + count], sv[MID : MID + count]


def flux_gradients(count, gu, gv):
    return [
        middle(x, count) * (-DT)
        for x in (gu - lanes(gu, 1), gu - rows(gu, 1), gv - lanes(gv, 1), gv - rows(gv, 1))
    ]


def interp_gradients(count, gu, gv, u, v, ginterp):
    for k, (g, x) in enumerate(zip(flux_gradients(count, gu, gv), carriers(u, v))):
        ginterp[k] = g * middle(x, count)


def velocity_gradients(count, gu, gv, interp, spread, lines):
    mid = count + 2 * MID
    half = [0.5 * g * by_kind(interp, k, mid) for k, g in enumerate(flux_gradients(count, gu, gv))]
    shares = gathered_back(count, spread, lines)
    out = []
    for which, g in enumerate((gu, gv)):
        along, across = half[which], half[2 + which]
        x = middle(g, count) + (along + lanes(along, -1)) + (across + rows(across, -1))
        out.append(x[MID : MID + count] + shares[which])
    return out


def network_backward(count, w_hidden, slopes, grads, between=lambda: None, copy=None):
    for m in range(LAYERS, 0, -1):

        def emit(r, o, m=m):
            at = gradient_rows(count, m, r)
            value = (fold_rounded(o) * slopes[at, :].astype(f32)).astype(bf16)
            grads[at, :] = value
            if m == 1 and copy is not None:
                copy[(r + 1) * CH : (r + 2) * CH, :] = value

        conv_rows(gradient_window(grads, count, m + 1), w_hidden.at[m - 1], -m, count + m, emit, between)


def input_gradient(count, w_first, window, gvel):
    starts = list(range(0, count, 2))
    for k in range(0, len(starts), 2):
        group = starts[k : k + 2]
        o = jnp.dot(
            w_first[...],
            jnp.concatenate([window(r) for r in group], axis=1),
            preferred_element_type=f32,
        )
        for i, r in enumerate(group):
            part = o[:, i * N : (i + 1) * N]
            both = lanes(part, -1)[0:4] + part[4:8] + lanes(part, 1)[8:12]
            gvel[0, r : r + 2, :] = both[0:2]
            gvel[1, r : r + 2, :] = both[2:4]


def folded(x):
    return x[: 3 * CH, : 3 * CH] + x[3 * CH :, CH:]


def weight_product(count, m, fields, feats, grads):
    starts = list(range(0, count, 2))
    shifts = (0,) if isinstance(m, int) and m == 1 else (-1, 0, 1)
    left, total = [], None
    for r in starts:
        g = [grads[gradient_rows(count, m, r + k), :] for k in range(2)]
        left.append(jnp.concatenate([lanes(x, -e) for x in g for e in shifts], axis=0))
        for x in g:
            x = x.astype(f32)
            total = x if total is None else total + x
    if isinstance(m, int) and m == 1:
        right = [first_window(fields, r) for r in starts]
    else:
        right = [feature_window(feats, count, m - 1)(r) for r in starts]
    out = lax.dot_general(
        jnp.concatenate(left, axis=1), jnp.concatenate(right, axis=1), NT, preferred_element_type=f32
    )
    return out, jnp.sum(total, axis=1, keepdims=True)


def weight_half(count, half, fields, feats, grads, put, extra):
    lane = lax.broadcasted_iota(jnp.int32, (CH, N), 1)
    extra[...] = jnp.zeros((3 * CH, N), f32)

    def first_layer():
        first, total = weight_product(count, 1, fields, feats, grads)
        first = jnp.concatenate([first, jnp.zeros((2 * CH, N - 32), f32)], axis=1)
        extra[:CH, :] = jnp.where(lane == 35, total, first[:CH])
        extra[CH : 2 * CH, :] = first[CH:]

    if not isinstance(half, int):
        pl.when(half == 1)(first_layer)
    elif half == 1:
        first_layer()
    parts, columns = [], extra[:CH, :]
    for i in range(3):
        product, total = weight_product(count, 2 + 3 * half + i, fields, feats, grads)
        parts.append(folded(product))
        columns = jnp.where(lane == 32 + i, total, columns)
    parts.append(jnp.concatenate([columns[:, :CH], extra[CH:, :CH]], axis=0))
    wide = jnp.concatenate(parts, axis=1)
    for q in range(5):
        put(q, wide[:, q * N : (q + 1) * N])


def fetch(sources, targets, sems):
    copies = [pltpu.make_async_copy(a, b, sems.at[i]) for i, (a, b) in enumerate(zip(sources, targets))]
    for copy in copies:
        copy.start()
    return copies


def tap_of(middle, last, m):
    return (lambda a, e: last[3 * a + e]) if m == LAYERS - 1 else (lambda a, e: middle[m, 3 * a + e])


def prepare_kernel(*refs):
    own, f_first, f_hidden, bias, mix, adder, flags = refs[10:17]
    vel, cot, first, first_bias, middle, middle_bias, last, last_bias, tables, lengths = refs[17:27]
    copies = fetch(refs[:10], refs[17:27], refs[27])
    core = lax.axis_index("strip") & 1
    group = lax.axis_index("traj")
    for copy in copies:
        copy.wait()
    for i in range(STEPS):
        flags[i] = jnp.full((8, N), jnp.where(lengths[core] > i, 1.0, 0.0), f32)
    flags[STEPS] = jnp.full((8, N), jnp.where(core == 0, 1.0, 0.0), f32)
    for bit in range(flags.shape[0] - STEPS - 1):
        flags[STEPS + 1 + bit] = jnp.full((8, N), jnp.where((group >> bit) & 1 == 1, 1.0, 0.0), f32)
    own[0] = jnp.where(core == 0, vel[0], vel[1])
    own[1] = jnp.where(core == 0, cot[0], cot[1])
    zero = jnp.zeros((CH, CH), bf16)
    for m in range(LAYERS):
        tap = tap_of(middle, last, m)
        for two in range(2):
            for e in range(3):
                taps = [tap(q - two, e) if 0 <= q - two < 3 else zero for q in range(4)]
                f_hidden[m, (two * 3 + e) * CH : (two * 3 + e + 1) * CH, :] = jnp.concatenate(taps, axis=1)
    for two in range(2):
        lines = []
        for ch in range(2):
            for i in range(4):
                for j in range(4):
                    if 0 <= i - two < 3 and j < 3:
                        lines.append(first[3 * (i - two) + j, ch : ch + 1, :].astype(f32))
                    else:
                        lines.append(jnp.zeros((1, CH), f32))
        f_first[two * CH : (two + 1) * CH, :] = jnp.concatenate(lines, axis=0).T.astype(bf16)
    for m in range(LAYERS + 1):
        if 0 < m < LAYERS:
            line = middle_bias[m - 1 : m, :]
        else:
            line = (first_bias if m == 0 else last_bias)[...].reshape(1, CH)
        bias[m] = jnp.broadcast_to(line, (N, CH)).T
    mix[...] = tables[2, 0:48, 0:64].astype(bf16)
    adder[...] = tables[2, 64:80, :].astype(bf16)


def prepare_back_kernel(*refs):
    b_first, b_hidden, right, left, weight = refs[5:10]
    first, middle, last, tables = refs[10:14]
    copies = fetch(refs[:4], refs[10:14], refs[14])
    for copy in copies:
        copy.wait()
    zero = jnp.zeros((CH, CH), bf16)
    for m in range(LAYERS):
        tap = tap_of(middle, last, m)
        for two in range(2):
            for e in range(3):
                taps = [tap(2 - q + two, 2 - e) if 0 <= q - two < 3 else zero for q in range(4)]
                b_hidden[m, (two * 3 + e) * CH : (two * 3 + e + 1) * CH, :] = jnp.concatenate(
                    [jnp.concatenate(taps[:2], axis=0).T, jnp.concatenate(taps[2:], axis=0).T], axis=1
                )
    lines = jnp.zeros((1, CH), f32)
    taps = []
    for e in range(3):
        for ch in range(2):
            for two in range(2):
                line = [
                    first[3 * (2 - q + two) + 2 - e, ch : ch + 1, :].astype(f32) if 0 <= q - two < 3 else lines
                    for q in range(4)
                ]
                taps.append(jnp.concatenate(line, axis=1))
    taps.append(jnp.zeros((4, 4 * CH), f32))
    b_first[...] = jnp.concatenate(taps, axis=0).astype(bf16)
    high, low = split(tables[0])
    right[...] = jnp.concatenate([high, high, low], axis=0)
    left[...] = jnp.concatenate([high, low, high], axis=1)
    weight[...] = tables[1]


def chosen(flag, x, y):
    flag = flag[0:1, :] > 0.5
    return jnp.where(jnp.broadcast_to(flag, x.shape), x, y)


def assemble_kernel(flags, own, partner, cross, same, cot_partner, ext, cot):
    upper = flags[STEPS]

    def pair(mine, other, i):
        other = chosen(upper, other[0, i], other[1, i])
        return [chosen(upper, mine[i], other), chosen(upper, other, mine[i])]

    for i in range(2):
        above = chosen(upper, cross[0, i], same[1, i])[-MARGIN:]
        below = chosen(upper, same[0, i], cross[1, i])[:MARGIN]
        ext[i] = jnp.concatenate([above, *pair(own[0], partner, i), below], axis=0)
        cot[i] = jnp.concatenate(pair(own[1], cot_partner, i), axis=0)


def network_kernel(count, vel, extra, w_first, w_hidden, bias, mix, adder, *refs):
    block, refs = refs[0], refs[1:]
    messages = refs[:-8]
    interp, raw, clear, fields, feats, slopes, put, kept = refs[-8:]
    if messages:
        write_messages(1, extra[0], extra[1], *messages)
    interleave(vel, fields)
    clear_patches(count, fields, mix, clear, put)
    sums = []

    def raw_done(r, value):
        sums.append(point_sums(r, value, clear))
        if len(sums) == 4 * LAG + 4:
            interpolate(r + 1 - len(sums), sums[:4], adder, put, interp)
            del sums[:4]

    network_forward(count, fields, w_first, w_hidden, bias, feats, slopes, raw, raw_done, kept)
    for i in range(0, len(sums), 4):
        interpolate(count + RAW - len(sums) + i, sums[i : i + 4], adder, put, interp)
    su, sv = provisional(count, vel[0], vel[1], interp)
    out = [su, sv, extra[0], extra[1]]
    for i in range(4):
        block[i] = out[i]
    if messages:
        write_messages(0, su, sv, *messages)


def project_kernel(count, blocks, steps, flags, *refs):
    block, messages, refs = refs[0], refs[1:blocks], refs[blocks:]
    forward, backward = steps
    mg = flags[backward][0:1, :]
    fields = [[mg * x for x in read_messages(1, block, messages)]]
    if forward is None:
        right, left, weight, gstar, own = refs
    else:
        vel, right, left, weight, gstar, own, ext = refs
        fields.append(read_messages(0, block, messages))
        mv = flags[forward][0:1, :]
    out = project(fields, count, right, left, weight)
    for i in range(2):
        gstar[i] = out[0][i]
        own[i] = (1.0 - mg) * block[2 + i]
        if forward is not None:
            ext[i] = vel[i] + mv * (out[1][i] - vel[i])


def static(start, size):
    return slice(start, start + size)


def back_kernel(count, ext, gstar, clear, b_first, b_hidden, slopes, *refs):
    if len(refs) == 6:
        mix, raw, grads, gvel, spread, ginterp = refs
    else:
        grads, first, ginterp = refs
    interp_gradients(count, gstar[0], gstar[1], ext[0], ext[1], ginterp)
    raw_gradient(count, clear, ginterp, grads)
    tasks = []
    if len(refs) == 6:
        columns = put_columns()
        for r in range(-RAW, count + RAW, 2):
            tasks.append(functools.partial(spread_back, r, static, columns, mix, raw, ginterp, spread))
    turn = [0]

    def between():
        turn[0] += 1
        if tasks and turn[0] % 3 == 0:
            tasks.pop(0)()

    network_backward(count, b_hidden, slopes, grads, between, None if len(refs) == 6 else first)
    for task in tasks:
        task()
    if len(refs) == 6:
        input_gradient(count, b_first, gradient_window(grads, count, 1), gvel)


def finish_kernel(count, front, base, gstar, interp, gvel, spread, block, top, bottom, far, lines):
    change = velocity_gradients(count, gstar[0], gstar[1], interp, spread, lines)
    out = [front[0], front[1]] + [base[i] + change[i] + gvel[i] for i in range(2)]
    for i in range(4):
        block[i] = out[i]
    for kind in range(2):
        write_messages(kind, out[2 * kind], out[2 * kind + 1], top, bottom, far)


def last_kernel(count, blocks, flags, *refs):
    block, messages, refs = refs[0], refs[1:blocks], refs[blocks:]
    now, right, left, weight, base, ext, gstar, interp, first, b_first, mix, raw, out = refs[:13]
    lines, spread, ginterp, gvel = refs[13:]
    (news,) = project([read_messages(0, block, messages)], count, right, left, weight)
    own = slice(MARGIN, MARGIN + count)
    mask = flags[STEPS - 1][0:1, :]
    for i in range(2):
        out[i] = now[i, own] + mask * (news[i][own] - now[i, own])
    gu, gv = gstar[0], gstar[1]
    input_gradient(count, b_first, lambda r: first[r * CH : (r + 4) * CH, :], gvel)
    interp_gradients(count, gu, gv, ext[0], ext[1], ginterp)
    columns = put_columns()

    def at(start, size):
        return pl.ds(pl.multiple_of(start, size), size) if size > 1 else pl.ds(start, size)

    def step(i, _):
        for k in range(2):
            spread_back(4 * i + 2 * k - RAW, at, columns, mix, raw, ginterp, spread)
        return 0

    lax.fori_loop(0, (count + 2 * RAW) // 4, step, 0)
    change = velocity_gradients(count, gu, gv, interp, spread, lines)
    for i in range(2):
        out[2 + i] = base[i] + change[i] + gvel[i]


def weights_kernel(count, fields, feats, grads, buffer, extra):
    for half in range(2):

        def put(q, value, half=half):
            buffer[place(half * HALF + q * 3 * CH, 3 * CH), :] = value

        weight_half(count, half, fields, feats, grads, put, extra)


def half_kernel(count, side, previous, fields, feats, grads, out, extra):
    half = (lax.axis_index("strip") & 1) ^ side

    def put(q, value):
        value = value + previous[place(half * HALF + q * 3 * CH, 3 * CH), :]
        out[q * 3 * CH : (q + 1) * 3 * CH, :] = value.astype(bf16)

    weight_half(count, half, fields, feats, grads, put, extra)
    if out.shape[0] > HALF:
        out[HALF:, :] = jnp.zeros((out.shape[0] - HALF, N), bf16)


def exchanged(flags, blocks):
    for bit in range(len(blocks).bit_length() - 1):
        flag = flags[STEPS + 1 + bit]
        blocks = [chosen(flag, blocks[i ^ (1 << bit)], x) for i, x in enumerate(blocks)]
    return blocks


def halves_kernel(flags, keep, received, *out):
    rows_each = out[0].shape[0]
    blocks = []
    for i in range(len(out)):
        at = slice(i * rows_each, (i + 1) * rows_each)
        blocks.append(keep[at, :].astype(f32) + received[at, :].astype(f32))
    for ref, x in zip(out, exchanged(flags, blocks)):
        ref[...] = x.astype(bf16)


def arrange_kernel(flags, *refs):
    *blocks, out = refs
    rows_each = blocks[0].shape[0]
    for i, x in enumerate(exchanged(flags, [x[...].astype(f32) for x in blocks])):
        out[i * rows_each : (i + 1) * rows_each, :] = x.astype(bf16)


def unpack_kernel(flags, mine, other, first, first_bias, middle, middle_bias, last, last_bias):
    for half in range(2):
        a, b = (mine, other) if half == 0 else (other, mine)
        blocks = []
        for q in range(5):
            at = slice(q * 3 * CH, (q + 1) * 3 * CH)
            blocks.append(chosen(flags[STEPS], a[at, :].astype(f32), b[at, :].astype(f32)))
        wide = jnp.concatenate(blocks, axis=1)
        turned = [blocks[4][two * CH : (two + 1) * CH].T[CH:] for two in range(2)]
        for i in range(3):
            m = 3 * half + i
            for a in range(3):
                part = wide[:, (3 * i + a) * CH : (3 * i + a + 1) * CH]
                for e in range(3):
                    value = part[e * CH : (e + 1) * CH]
                    if m < LAYERS - 1:
                        middle[m, 3 * a + e] = value
                    else:
                        last[3 * a + e] = value
            if m < LAYERS - 1:
                middle_bias[m : m + 1, :] = turned[0][32 + i : 33 + i]
            else:
                last_bias[...] = turned[0][32 + i]
    first_bias[...] = turned[0][35]
    for a in range(3):
        for e in range(3):
            for ch in range(2):
                low, high = 16 * ch + 4 * a + e, 16 * ch + 4 * (a + 1) + e
                first[3 * a + e, ch : ch + 1, :] = turned[0][low : low + 1] + turned[1][high : high + 1]


VMEM = pl.BlockSpec(memory_space=pltpu.VMEM)
SMEM = pl.BlockSpec(memory_space=pltpu.SMEM)
PARAMS = pltpu.CompilerParams(vmem_limit_bytes=VMEM_BYTES)


def array(dtype, *shape):
    return jax.ShapeDtypeStruct(shape, dtype)


def cost(flops, moved):
    return pl.CostEstimate(flops=flops, bytes_accessed=moved, transcendentals=0)


def field(count, *lead):
    return pltpu.VMEM(lead + (count, N), f32)


def feature_array(count):
    return array(bf16, LAYERS * (count + 24) * CH, N)


def gradient_array(count, slots):
    return array(bf16, slots * (count + 16) * CH, N)


def call(kernel, name, flops, inputs, out, scratch=()):
    return pl.pallas_call(
        kernel,
        in_specs=[VMEM] * len(inputs),
        out_specs=jax.tree.map(lambda _: VMEM, out),
        out_shape=out,
        scratch_shapes=list(scratch),
        compiler_params=PARAMS,
        cost_estimate=cost(flops, 10**6),
        name=name,
    )(*inputs)


def run_prepare(lengths, vel, cot, params, bits):
    out = [
        array(f32, 2, 2, vel.shape[2], N),
        array(bf16, 2 * CH, 32),
        array(bf16, LAYERS, 6 * CH, 4 * CH),
        array(f32, LAYERS + 1, CH, N),
        array(bf16, 48, 64),
        array(bf16, 16, N),
        array(f32, STEPS + 1 + bits, 8, N),
    ]
    inputs = [vel, cot, *params, jnp.asarray(constant_tables(N)), lengths]
    scratch = [pltpu.VMEM(x.shape, x.dtype) for x in inputs[:-1]] + [pltpu.SMEM(lengths.shape, lengths.dtype)]
    return call_from_hbm(prepare_kernel, "prepare", inputs, out, scratch)


def run_prepare_back(params, after):
    first, _, middle, _, last, _ = params
    out = [
        array(bf16, 16, 4 * CH),
        array(bf16, LAYERS, 6 * CH, 4 * CH),
        array(bf16, 3 * N, N),
        array(bf16, N, 3 * N),
        array(f32, N, N),
    ]
    inputs = [first, middle, last, jnp.asarray(constant_tables(N))]
    scratch = [pltpu.VMEM(x.shape, x.dtype) for x in inputs]
    b_first, b_hidden, *tables = call_from_hbm(prepare_back_kernel, "prepare_back", inputs, out, scratch, after)
    return b_first, b_hidden, tables


def call_from_hbm(kernel, name, inputs, out, scratch, *after):
    hbm = pl.BlockSpec(memory_space=pltpu.HBM)
    inputs = [pltpu.with_memory_space_constraint(x, pltpu.HBM) for x in inputs]
    return pl.pallas_call(
        kernel,
        in_specs=[hbm] * len(inputs) + [VMEM] * len(after),
        out_specs=[VMEM] * len(out),
        out_shape=out,
        scratch_shapes=scratch + [pltpu.SemaphoreType.DMA((len(inputs),))],
        compiler_params=PARAMS,
        cost_estimate=cost(10**9, 10**6),
        name=name,
    )(*inputs, *after)


def message_arrays(count):
    near = 4 * MARGIN + 2 * (count - MARGIN) + 8
    return [array(f32, near, N), array(f32, near, N), array(f32, 2 * count + 8, N)]


def run_assemble(count, flags, fields):
    out = [array(f32, 2, count + 2 * MARGIN, N), array(f32, 2, count, N)]
    return call(assemble_kernel, "assemble", 10**6, [flags, *fields], out)


def run_network(count, vel, extra, weights, last=False):
    local_rows, mid = count + 2 * MARGIN, count + 2 * MID
    out = [array(f32, 4, count, N), *([] if last else message_arrays(count)), array(f32, 4 * mid, N), array(f32, mid * CH, N), array(f32, mid * 32, N)]
    out += [array(f32, 2, 4 * local_rows, N)]
    out += [feature_array(count), gradient_array(count, LAYERS)]
    scratch = [field(4 * mid), field((count + 2 * LAYERS) * CH, 2)]
    return call(functools.partial(network_kernel, count), "network", 4 * 10**9, [vel, extra, *weights], out, scratch)


def run_project(count, steps, flags, gathered, tables, *vel):
    local_rows = count + 2 * MARGIN
    out = [array(f32, 2, local_rows, N), array(f32, 2, count, N)]
    if vel:
        out.append(array(f32, 2, local_rows, N))
    kernel = functools.partial(project_kernel, count, len(gathered), steps)
    return call(kernel, "project", 10**9, [flags, *gathered, *vel, *tables], out)


def run_back(count, ext, gstar, clear, b_first, b_hidden, slopes, *more):
    mid = count + 2 * MID
    inputs = [ext, gstar, clear, b_first, b_hidden, slopes, *more]
    out = [gradient_array(count, LAYERS + 1)]
    if more:
        out += [array(f32, 2, count, N), array(f32, 2, 4, 4 * mid, N)]
    else:
        out.append(array(bf16, (count + 2) * CH, N))
    return call(functools.partial(back_kernel, count), "back", 4 * 10**9, inputs, out, [field(mid, 4)])


def run_finish(count, *inputs):
    kernel = functools.partial(finish_kernel, count)
    out = [array(f32, 4, count, N), *message_arrays(count)]
    return call(kernel, "finish", 10**9, inputs, out, [field(4 * count, 2)])


def run_last(count, flags, gathered, *inputs):
    mid = count + 2 * MID
    scratch = [field(4 * count, 2), field(4 * mid, 2, 4), field(mid, 4), field(count, 2)]
    kernel = functools.partial(last_kernel, count, len(gathered))
    return call(kernel, "last", 10**9, [flags, *gathered, *inputs], array(f32, 4, count, N), scratch)


def run_weights(count, fields, feats, grads):
    kernel = functools.partial(weights_kernel, count)
    return call(kernel, "weights", 3 * 10**9, [fields, feats, grads], array(f32, 2 * HALF, N), [field(3 * CH)])


def run_half(count, side, rows, previous, fields, feats, grads, *after):
    inputs = [previous, fields, feats, grads, *after]
    kernel = functools.partial(half_kernel, count, side)
    if after:
        kernel = lambda *refs: half_kernel(count, side, *refs[:4], *refs[5:])
    return call(kernel, "half", 10**9, inputs, array(bf16, rows, N), [field(3 * CH)])


def run_halves(flags, keep, received, parts):
    out = [array(bf16, keep.shape[0] // parts, N)] * parts
    return call(halves_kernel, "halves", 10**6, [flags, keep, received], out)


def run_arrange(flags, blocks):
    out = array(bf16, len(blocks) * blocks[0].shape[0], N)
    return call(arrange_kernel, "arrange", 10**6, [flags, *blocks], out)


def run_unpack(flags, mine, other):
    out = [
        array(f32, 9, 2, CH),
        array(f32, CH),
        array(f32, LAYERS - 1, 9, CH, CH),
        array(f32, LAYERS - 1, CH),
        array(f32, 9, CH, CH),
        array(f32, CH),
    ]
    return call(unpack_kernel, "unpack", 10**7, [flags, mine, other], out)


def swap(x, axis, offset):
    count = lax.axis_size(axis)
    return lax.ppermute(x, axis, [(i, i ^ offset) for i in range(count)])


def from_group(x, ahead):
    count = lax.axis_size("strip")
    return lax.ppermute(x, "strip", [(i, (i - 2 * ahead) % count) for i in range(count)])


def gather_groups(block, top, bottom, far):
    groups = lax.axis_size("strip") // 2
    others = [from_group(far, k) for k in range(2, groups - 1)]
    return [block, from_group(top, 1), *others, from_group(bottom, -1)]


def margins(velocity, partner, core):
    count = lax.axis_size("strip")
    if velocity.shape[2] < MARGIN:
        upper = core[0] == 0
        pair = jnp.where(
            upper,
            jnp.concatenate([velocity[0], partner[0]], axis=1),
            jnp.concatenate([partner[1], velocity[1]], axis=1),
        )
        above, below = from_group(pair[:, -MARGIN:], -1), from_group(pair[:, :MARGIN], 1)
        return jnp.stack([above, below]), jnp.stack([below, above])
    cross = [(i, (i - 1) % count if i % 2 == 0 else (i + 1) % count) for i in range(count)]
    same = [(i, (i - 2) % count if i % 2 == 0 else (i + 2) % count) for i in range(count)]
    return lax.ppermute(velocity, "strip", cross), lax.ppermute(velocity, "strip", same)


def sum_everywhere(keep, received, flags):
    parts = lax.axis_size("traj")
    groups = lax.axis_size("strip") // 2
    blocks = run_halves(flags, keep, received, parts)
    total = blocks[0].astype(f32)
    for k in range(1, parts):
        total = total + swap(blocks[k], "traj", k).astype(f32)
    x = total.astype(bf16)
    total = x.astype(f32)
    for k in range(1, groups):
        total = total + swap(x, "strip", 2 * k).astype(f32)
    x = total.astype(bf16)
    x = run_arrange(flags, [x] + [swap(x, "traj", k) for k in range(1, parts)])
    return x, swap(x, "strip", 1)


def per_device(
    velocity, lengths, cotangent, first_kernel, first_bias, middle_kernels, middle_biases, last_kernel, last_bias
):
    rc = velocity.shape[2]
    count = 2 * rc
    index = lax.axis_index("strip") & 1
    core = index[None]
    pick = lambda y, i: lax.dynamic_index_in_dim(y, i, 0, False)

    partner = swap(velocity, "strip", 1)
    cross, same = margins(velocity, partner, core)
    cot_partner = swap(cotangent, "strip", 1)
    first_kernel = first_kernel.transpose(0, 2, 1)
    params = (first_kernel, first_bias, middle_kernels, middle_biases, last_kernel, last_bias)
    parts = lax.axis_size("traj")
    half_rows = -(-HALF // (parts * 16)) * parts * 16
    own, w_first, w_hidden, bias, mix, adder, flags = run_prepare(
        lengths, velocity, cotangent, params, parts.bit_length() - 1
    )
    weights = (w_first, w_hidden, bias, mix, adder)

    v0, cot = run_assemble(count, flags, (own, partner, cross, same, cot_partner))
    block, *sent, interp0, raw0, clear0, fields0, feats0, slopes0 = run_network(count, v0, cot, weights)
    gathered = gather_groups(block, *sent)
    b_first, b_hidden, tables = run_prepare_back(params, interp0)
    gstar1, base, v1 = run_project(count, (0, 1), flags, gathered, tables, v0)
    block, interp1, raw1, clear1, fields1, feats1, slopes1 = run_network(count, v1, cot, weights, last=True)
    grads1, gvel, spread = run_back(count, v1, gstar1, clear1, b_first, b_hidden, slopes1, mix, raw1)
    gathered = gather_groups(*run_finish(count, block, base, gstar1, interp1, gvel, spread))
    buffer = run_weights(count, fields1, feats1, grads1)
    gstar0, base = run_project(count, (None, 0), flags, gathered, tables)
    grads0, first = run_back(count, v0, gstar0, clear0, b_first, b_hidden, slopes0)
    send = run_half(count, 1, half_rows, buffer, fields0, feats0, grads0)
    received = swap(send, "strip", 1)
    keep = run_half(count, 0, half_rows, buffer, fields0, feats0, grads0, send)
    out = run_last(
        count, flags, gathered, v1, *tables, base, v0, gstar0, interp0, first, b_first, mix, raw0
    )

    strips = out.reshape(4, 2, rc, N).transpose(1, 0, 2, 3)
    mine, other = pick(strips, index)[None], swap(pick(strips, 1 - index), "strip", 1)[None]
    out = jnp.where(
        index == 0, jnp.concatenate([mine, other], axis=0), jnp.concatenate([other, mine], axis=0)
    )
    mine, other = sum_everywhere(keep, received, flags)
    grad_first, *rest = run_unpack(flags, mine, other)
    return (out[:, :2], out[:, 2:], grad_first.transpose(0, 2, 1), *rest)


def solution(mesh):
    band = P("traj", None, "strip", None)
    return jax.shard_map(
        per_device,
        mesh=mesh,
        in_specs=(band, P("traj"), band) + (P(),) * 6,
        out_specs=(band, band) + (P(),) * 6,
        check_vma=False,
    )
```
